32 devices in a mesh: row: 8 (over y, x, core), col: 4 (over z).
Axes of the slice: x: 2, y: 2, z: 4, core: 2. Of those that a mesh axis runs over, the one named last changes fastest.
Arguments:
- activations: bfloat16 [8192, 2048], P('col', 'row'), may hold values from -6 to 6
- document_ids: int32 [8192], P('col'), may hold values from 0 to 15, never falling along the last dimension, each value on 1 to 2048 neighbouring positions
- attention_gain: float32 [2048], P('row'), may hold values from 0.5 to 1.5
- attention_shift: float32 [2048], P('row'), may hold values from -1.75 to 1.75
- feedforward_gain: float32 [2048], P('row'), may hold values from 0.5 to 1.5
- feedforward_shift: float32 [2048], P('row'), may hold values from -1.75 to 1.75
- query_key_value: float32 [2048, 16, 384], P('col', 'row'), may hold values from -1 to 1
- query_key_value_bias: float32 [16, 384], P('row'), may hold values from -3 to 3
- output_weight: float32 [2048, 2048], P('row', 'col'), may hold values from -0.5 to 0.5
- output_bias: float32 [2048], P('row'), may hold values from -1.75 to 1.75
- up_weight: float32 [2048, 8192], P('col', 'row'), may hold values from -1 to 1
- up_bias: float32 [8192], P('row'), may hold values from -3 to 3
- down_weight: float32 [8192, 2048], P('row', 'col'), may hold values from -0.0625 to 0.0625
- down_bias: float32 [2048], P('row'), may hold values from -1.75 to 1.75
- out_grad: bfloat16 [8192, 2048], P('col', 'row'), may hold values from -6 to 6
Outputs:
- layer_out: float32 [8192, 2048], P('col', 'row')
- activations_grad: float32 [8192, 2048], P('col', 'row')
- attention_gain_grad: float32 [2048], P('row')
- attention_shift_grad: float32 [2048], P('row')
- feedforward_gain_grad: float32 [2048], P('row')
- feedforward_shift_grad: float32 [2048], P('row')
- query_key_value_grad: float32 [2048, 16, 384], P('col', 'row')
- query_key_value_bias_grad: float32 [16, 384], P('row')
- output_weight_grad: float32 [2048, 2048], P('row', 'col')
- output_bias_grad: float32 [2048], P('row')
- up_weight_grad: float32 [2048, 8192], P('col', 'row')
- up_bias_grad: float32 [8192], P('row')
- down_weight_grad: float32 [8192, 2048], P('row', 'col')
- down_bias_grad: float32 [2048], P('row')
The draws below stay inside these ranges and needn't reach their ends.
Inputs may be any that keep to these rules, and one draw needn't show every extreme that they name: `document_ids`: ids never fall from one token to the next; attention stays inside a packed row of 2048 tokens.
All inputs are finite; a program needn't handle non-finite values.
Results may differ from the reference program's by a relative error of at most 0.012.
The reference program's roundings to bfloat16 on the way count: a program that leaves them out, or rounds other values in their place, can miss the bound.
Values may be sent and summed in bfloat16 or wider, within the bound.
No kernel may reach another device: no remote copies, remote signals or barrier semaphores. Data moves between devices by JAX's collectives and lax.ppermute only.
A program may use at most 256 MiB of HBM per device.

```python
import math
import jax
import jax.numpy as jnp
import numpy as np
from jax import lax

D = 2048
HEADS = 16
HEAD_DIM = 128
ROTARY = 32
FF = 8192
LENGTH = 2048
TOKENS = 8192


def draw_query_key_value(key, part):
    key = jax.random.fold_in(key, 11)
    jitter_key, shared_key = jax.random.split(key)
    full_shape = (D, HEADS, 3 * HEAD_DIM)
    spread_scale = (D // 2) ** (-0.5)
    jitter_values = jax.random.truncated_normal(jitter_key, -6.0, 6.0, full_shape, jnp.float32)
    shared_row = 0.5 * jax.random.truncated_normal(shared_key, -6.0, 6.0, full_shape[1:], jnp.float32)
    return spread_scale * (jitter_values + shared_row[None])


def draw_up_weight(key, part):
    key = jax.random.fold_in(key, 12)
    jitter_key, shared_key = jax.random.split(key)
    full_shape = (D, FF)
    spread_scale = D ** (-0.5)
    jitter_values = jax.random.truncated_normal(jitter_key, -6.0, 6.0, full_shape, jnp.float32)
    shared_row = 0.5 * jax.random.truncated_normal(shared_key, -6.0, 6.0, (FF,), jnp.float32)
    return spread_scale * (jitter_values + shared_row[None])


def block_levels(stream_key, extent, shards, least, largest):
    loudness = 1.0
    for axis_at, parts in shards:
        heights = jax.random.uniform(jax.random.fold_in(jax.random.fold_in(stream_key, 6), axis_at), (parts,), jnp.float32, least / len(shards), largest / len(shards))
        loudness = loudness * jnp.repeat(jnp.exp(heights), extent[axis_at] // parts).reshape((-1,) + (1,) * (len(extent) - 1 - axis_at))
    return loudness


def length_profile(amount, total, reach, slope):
    loads = [(1 << 20) // math.isqrt(grade ** slope) + 1 for grade in range(2, amount + 1)]
    spare, holding = total - reach - (amount - 1), [1] * (amount - 1)
    while spare > 0:
        candidates = [i for i in range(amount - 1) if holding[i] < reach]
        mass, left = sum([loads[i] for i in candidates]), spare
        for i in candidates:
            addition = min(reach - holding[i], max(1, left * loads[i] // mass), spare)
            holding[i] = holding[i] + addition
            spare = spare - addition
    return np.array([reach] + holding)


def uneven_parts(rng, amount, total, reach, slope):
    if amount == 2:
        one = jax.random.randint(rng, (), max(1, total - reach), min(reach, total - 1) + 1)
        return jnp.stack([one, total - one])
    tallies = jnp.asarray(length_profile(amount, total, reach, slope), jnp.int32)
    twos = (amount - 1) // 2
    donor, taker = tallies[1:1 + 2 * twos:2], tallies[2:2 + 2 * twos:2]
    margin = jnp.minimum(donor - 1, reach - taker)
    moved = jax.random.randint(jax.random.fold_in(rng, 1), (twos,), 0, 1 << 20) % (margin + 1)
    tallies = tallies.at[1:1 + 2 * twos:2].set(donor - moved).at[2:2 + 2 * twos:2].set(taker + moved)
    return tallies[jax.random.permutation(jax.random.fold_in(rng, 2), amount)]


def gaussian(own_key, extent, deviation, most, cuts=(), kind=jnp.bfloat16):
    gain = block_levels(own_key, extent, cuts, -0.22, 0.18) if cuts else 1.0
    values = jax.random.normal(own_key, extent, jnp.float32) * deviation * gain
    return jnp.minimum(jnp.maximum(values, -most), most).astype(kind)


def setup_inputs(seed: int = 0) -> dict:
    seeds = jax.random.split(jax.random.key(seed), 16)
    return {
        "activations": gaussian(seeds[0], (TOKENS, D), 1.0, 6.0, ((0, 4), (1, 8))),
        "document_ids": jnp.searchsorted(jnp.cumsum(uneven_parts(seeds[1], 4 * TOKENS // LENGTH, TOKENS, LENGTH, 2)), jnp.arange(TOKENS), side="right").astype(jnp.int32),
        "attention_gain": jnp.clip(1.0 + 0.1 * jax.random.normal(seeds[2], (D,), jnp.float32), 0.5, 1.5),
        "attention_shift": gaussian(seeds[3], (D,), 0.3, 1.75, ((0, 8),), jnp.float32),
        "feedforward_gain": jnp.clip(1.0 + 0.1 * jax.random.normal(seeds[4], (D,), jnp.float32), 0.5, 1.5),
        "feedforward_shift": gaussian(seeds[5], (D,), 0.3, 1.75, ((0, 8),), jnp.float32),
        "query_key_value": draw_query_key_value(jax.random.fold_in(seeds[15], 71), 0),
        "query_key_value_bias": gaussian(seeds[7], (HEADS, 3 * HEAD_DIM), 0.5, 3.0, ((0, 8),), jnp.float32),
        "output_weight": gaussian(seeds[8], (D, D), (D // 16) ** -0.5, 0.5, ((0, 8), (1, 4)), jnp.float32),
        "output_bias": gaussian(seeds[9], (D,), 0.3, 1.75, ((0, 8),), jnp.float32),
        "up_weight": draw_up_weight(jax.random.fold_in(seeds[15], 71), 0),
        "up_bias": gaussian(seeds[11], (FF,), 0.5, 3.0, ((0, 8),), jnp.float32),
        "down_weight": gaussian(seeds[12], (FF, D), FF ** -0.5, 0.0625, ((0, 8), (1, 4)), jnp.float32),
        "down_bias": gaussian(seeds[13], (D,), 0.3, 1.75, ((0, 8),), jnp.float32),
        "out_grad": gaussian(seeds[14], (TOKENS, D), 1.0, 6.0, ((0, 4), (1, 8))),
    }


EPSILON = 1e-05
MASKED = -1e+30
ROPE_BASE = 10000.0
HIGHEST = lax.Precision.HIGHEST

@jax.custom_vjp
def low(v):
    return lax.optimization_barrier(v.astype(jnp.bfloat16)).astype(jnp.float32)

@jax.custom_vjp
def low_back(v):
    return v

def low_keep(v):
    return (low(v), None)

def low_pass(kept, grad):
    return (grad,)

def back_keep(v):
    return (v, None)

def back_low(kept, grad):
    return (low(grad),)
low.defvjp(low_keep, low_pass)
low_back.defvjp(back_keep, back_low)

def matmul(left, right):
    return jnp.dot(left, right, precision=HIGHEST)

def rotate(tensor, cosine_table, sine_table):
    halfway = ROTARY // 2
    leading = tensor[..., :ROTARY]
    turned = jnp.concatenate([-leading[..., halfway:], leading[..., :halfway]], axis=-1)
    return jnp.concatenate([leading * cosine_table + turned * sine_table, tensor[..., ROTARY:]], axis=-1)

def pack_attention(queries, keys_in, values_in, documents):
    places = jnp.arange(LENGTH, dtype=jnp.int32)
    scores = jnp.einsum('qhd,khd->hqk', queries, keys_in, precision=HIGHEST) * HEAD_DIM ** (-0.5)
    scores = low_back(scores)
    allowed = (documents[:, None] == documents[None, :]) & (places[None, :] <= places[:, None])
    scores = jnp.where(allowed[None], scores, MASKED)
    totals = jax.nn.logsumexp(scores, axis=-1, keepdims=True)
    probs_low = low(jnp.exp(scores - totals))
    return jnp.einsum('hqk,khd->qhd', probs_low, values_in, precision=HIGHEST)

def checked_pack(group):
    return jax.checkpoint(pack_attention)(group[0], group[1], group[2], group[3])

def layer(input_float, attention_gain, attention_shift, feedforward_gain, feedforward_shift, query_key_value, query_key_value_bias, output_weight, output_bias, up_weight, up_bias, down_weight, down_bias, document_ids):
    token_mean = lax.optimization_barrier(jnp.mean(input_float, axis=-1, keepdims=True))
    centered = input_float - token_mean
    normed = centered * lax.rsqrt(lax.optimization_barrier(jnp.mean(centered * centered, axis=-1, keepdims=True)) + EPSILON)
    first_norm = low(normed * attention_gain + attention_shift)
    second_norm = low(normed * feedforward_gain + feedforward_shift)
    project_lin = low_back(matmul(first_norm, low(query_key_value).reshape(D, 3 * D)) + query_key_value_bias.reshape(3 * D))
    project_lin = project_lin.reshape(TOKENS, HEADS, 3 * HEAD_DIM)
    positions = (jnp.arange(TOKENS, dtype=jnp.int32) % LENGTH).astype(input_float.dtype)
    frequency = ROPE_BASE ** (-jnp.arange(0, ROTARY, 2, dtype=jnp.int32).astype(input_float.dtype) / ROTARY)
    turning = positions[:, None] * frequency[None, :]
    turning = jnp.concatenate([turning, turning], axis=1)
    cosine_table = jnp.cos(turning)[:, None, :]
    sine_table = jnp.sin(turning)[:, None, :]
    queries = low(rotate(project_lin[..., :HEAD_DIM], cosine_table, sine_table))
    keys_in = low(rotate(project_lin[..., HEAD_DIM:2 * HEAD_DIM], cosine_table, sine_table))
    values_in = low(project_lin[..., 2 * HEAD_DIM:])
    pack_count = TOKENS // LENGTH
    shape_packs = (pack_count, LENGTH, HEADS, HEAD_DIM)
    attended = lax.map(checked_pack, (queries.reshape(shape_packs), keys_in.reshape(shape_packs), values_in.reshape(shape_packs), document_ids.reshape(pack_count, LENGTH)))
    attended = low(low_back(attended.reshape(TOKENS, D)))
    up_lin = low_back(matmul(second_norm, low(up_weight)) + up_bias)
    hidden = low(jax.nn.gelu(up_lin, approximate=False))
    mixed_sum = low_back(matmul(attended, low(output_weight)) + matmul(hidden, low(down_weight)))
    return input_float + mixed_sum + output_bias + down_bias

def reference(activations, document_ids, attention_gain, attention_shift, feedforward_gain, feedforward_shift, query_key_value, query_key_value_bias, output_weight, output_bias, up_weight, up_bias, down_weight, down_bias, out_grad):

    def forward(input_float, gain_one, shift_one, gain_two, shift_two, project_weight, project_bias, out_weight, out_bias, expand_weight, expand_bias, reduce_weight, reduce_bias):
        return layer(input_float, gain_one, shift_one, gain_two, shift_two, project_weight, project_bias, out_weight, out_bias, expand_weight, expand_bias, reduce_weight, reduce_bias, document_ids)
    primals = (activations.astype(jnp.float32), attention_gain, attention_shift, feedforward_gain, feedforward_shift, query_key_value, query_key_value_bias, output_weight, output_bias, up_weight, up_bias, down_weight, down_bias)
    layer_out, pullback = jax.vjp(forward, *primals)
    grads = pullback(out_grad.astype(jnp.float32))
    return (layer_out, grads[0], grads[1], grads[2], grads[3], grads[4], grads[5], grads[6], grads[7], grads[8], grads[9], grads[10], grads[11], grads[12])
```

```python
import functools

import jax
import jax.numpy as jnp
from jax import lax
from jax.experimental import pallas as pl
from jax.experimental.pallas import tpu as pltpu
from jax.sharding import PartitionSpec as P

D = 2048
HEAD_DIM = 128
ROTARY = 32
LENGTH = 2048

EPSILON = 1e-05
MASKED = -1e30
ROPE_BASE = 10000.0
BF = jnp.bfloat16
F32 = jnp.float32
LAST = (((1,), (1,)), ((), ()))
FIRST = (((0,), (0,)), ((), ()))
TILE = 256
QUERY_BLOCK = 256
KEY_BLOCK = 256
VMEM_LIMIT = 50 * 1024 * 1024
LOG2_E = 1.4426950408889634
SQRT_HALF = 0.7071067811865476
INV_SQRT_2PI = 0.3989422804014327


def after(value, *others):
    return lax.optimization_barrier((value,) + others)[0]


def line_gather(shard, count):
    upward, downward = shard, shard
    from_below, from_above = [], []
    for step in range(1, count):
        upward = lax.ppermute(upward, "col", [(k, k + 1) for k in range(step - 1, count - 1)])
        downward = lax.ppermute(downward, "col", [(k, k - 1) for k in range(1, count - step + 1)])
        from_below.append(upward)
        from_above.append(downward)
    return [shard] + from_below + from_above


def line_scatter(partial, count, place, dim):
    extent = partial.shape[dim] // count

    def part(index):
        return lax.dynamic_slice_in_dim(
            partial, jnp.clip(index, 0, count - 1) * extent, extent, dim
        ).astype(F32)

    upward = downward = None
    for step in range(1, count):
        ahead, behind = part(place + count - step), part(place - count + step)
        if upward is not None:
            ahead, behind = ahead + upward.astype(F32), behind + downward.astype(F32)
        upward = lax.ppermute(ahead.astype(BF), "col", [(k, k + 1) for k in range(step)])
        downward = lax.ppermute(
            behind.astype(BF), "col", [(k, k - 1) for k in range(count - step, count)]
        )
    return part(place) + (upward.astype(F32) + downward.astype(F32))


def ring_sum(value, axis, count):
    total = value
    for back in range(1, count):
        total = total + lax.ppermute(value, axis, [(k, (k + back) % count) for k in range(count)])
    return total


def ring_scatter(value, axis, count, place):
    total = lax.dynamic_index_in_dim(value, place, 0, keepdims=False)
    for back in range(1, count):
        piece = lax.dynamic_index_in_dim(value, lax.rem(place + back, count), 0, keepdims=False)
        total = total + lax.ppermute(piece, axis, [(k, (k + back) % count) for k in range(count)])
    return total


def load_shards(refs, whole, sems, dim):
    count = (len(refs) + 1) // 2
    extent = refs[0].shape[dim]
    place = lax.axis_index("col")

    def spot(j):
        at = pl.ds(j * extent, extent)
        return whole.at[at, :] if dim == 0 else whole.at[:, at]

    for i in range(count):

        @pl.when(place == i)
        def _():
            for j in range(count):
                if j == i:
                    source = refs[0]
                elif j < i:
                    source = refs[i - j]
                else:
                    source = refs[count - 1 + j - i]
                pltpu.make_async_copy(source, spot(j), sems.at[j]).start()

    for j in range(count):
        pltpu.make_async_copy(refs[0], spot(j), sems.at[j]).wait()


def normalize(tile):
    values = tile.astype(F32)
    centered = values - jnp.mean(values, axis=1, keepdims=True)
    inverse_scale = lax.rsqrt(jnp.mean(centered * centered, axis=1, keepdims=True) + EPSILON)
    return centered * inverse_scale, inverse_scale


def up_kernel(count, *refs):
    act, params, bias = refs[:3]
    shards = refs[3 : 3 + 2 * count - 1]
    first_out, second_out, hidden_out, slope_out, whole, sems = refs[3 + 2 * count - 1 :]

    @pl.when(pl.program_id(0) == 0)
    def _():
        load_shards(shards, whole, sems, 0)

    normed, _ = normalize(act[...])
    first_out[...] = (normed * params[0:1, :] + params[1:2, :]).astype(BF)
    second = (normed * params[2:3, :] + params[3:4, :]).astype(BF)
    second_out[...] = second
    lin = jnp.dot(second, whole[...], preferred_element_type=F32) + bias[...]
    cdf = 0.5 + 0.5 * lax.erf(lin * SQRT_HALF)
    hidden_out[...] = (lin * cdf).astype(BF)
    slope_out[...] = cdf + lin * (INV_SQRT_2PI * jnp.exp(-0.5 * lin * lin))


def turn(values, tables, sign):
    cosine, left, right = tables
    half = ROTARY // 2
    turned = left * pltpu.roll(values, HEAD_DIM - half, 1) + right * pltpu.roll(values, half, 1)
    return values * cosine + sign * turned


def project_kernel(count, heads, *refs):
    norm, bias, cosine, left, right = refs[:5]
    shards = refs[5 : 5 + 2 * count - 1]
    out, whole, sems = refs[5 + 2 * count - 1 :]

    @pl.when(pl.program_id(0) == 0)
    def _():
        load_shards(shards, whole, sems, 0)

    lin = jnp.dot(norm[...], whole[...], preferred_element_type=F32) + bias[...]
    tables = cosine[...], left[...], right[...]
    for head in range(heads):
        for part in range(3):
            at = slice((head * 3 + part) * HEAD_DIM, (head * 3 + part + 1) * HEAD_DIM)
            piece = lin[:, at]
            out[:, at] = (turn(piece, tables, 1.0) if part < 2 else piece).astype(BF)


def attention_kernel(
    low, start, cosine, left, right, query, key, value, grad, out, project, q_t, k_t, v_t, g_t, dk, dv
):
    length = query.shape[0]
    scale = HEAD_DIM**-0.5
    q_t[...] = query[...].T
    k_t[...] = key[...].T
    v_t[...] = value[...].T
    g_t[...] = grad[...].T
    dk[...] = jnp.zeros_like(dk)
    dv[...] = jnp.zeros_like(dv)

    def query_block(block, _):
        rows = pl.ds(pl.multiple_of(block * QUERY_BLOCK, QUERY_BLOCK), QUERY_BLOCK)
        queries_t, grads_t = q_t[:, rows], g_t[:, rows]
        first = start[:, rows]
        place = block * QUERY_BLOCK + lax.broadcasted_iota(jnp.int32, (1, QUERY_BLOCK), 1)

        def block_scores(at):
            keys = pl.ds(pl.multiple_of(at * KEY_BLOCK, KEY_BLOCK), KEY_BLOCK)
            scores = jnp.dot(key[keys, :], queries_t, preferred_element_type=F32) * (
                scale * LOG2_E
            )
            key_place = at * KEY_BLOCK + lax.broadcasted_iota(
                jnp.int32, (KEY_BLOCK, QUERY_BLOCK), 0
            )
            allowed = (key_place >= first) & (key_place <= place)
            prob_grad = jnp.dot(value[keys, :], grads_t, preferred_element_type=F32)
            return keys, jnp.where(allowed, scores, MASKED), prob_grad

        def forward(at, carry):
            largest, total, weighted, produced = carry
            keys, scores, prob_grad = block_scores(at)
            newest = jnp.maximum(largest, jnp.max(scores, axis=0, keepdims=True))
            shrink = jnp.exp2(largest - newest)
            parts = jnp.exp2(scores - newest)
            total = total * shrink + jnp.sum(parts, axis=0, keepdims=True)
            weighted = weighted * shrink + jnp.sum(parts * prob_grad, axis=0, keepdims=True)
            produced = produced * shrink + jnp.dot(
                v_t[:, keys], parts.astype(BF), preferred_element_type=F32
            )
            return newest, total, weighted, produced

        empty = jnp.zeros((1, QUERY_BLOCK), F32)
        low_block = low[block]
        last_block = (block + 1) * (QUERY_BLOCK // KEY_BLOCK)
        largest, total, weighted, produced = lax.fori_loop(
            low_block,
            last_block,
            forward,
            (empty + MASKED, empty, empty, jnp.zeros((HEAD_DIM, QUERY_BLOCK), F32)),
        )
        inverse = 1.0 / total
        out[rows, :] = (produced * inverse).T.astype(BF)
        log_total = largest + jnp.log2(total)
        delta = weighted * inverse

        def backward(at, query_grad):
            keys, scores, prob_grad = block_scores(at)
            probs = jnp.exp2(scores - log_total)
            score_grad = (probs * (prob_grad - delta)).astype(BF)
            dv[keys, :] += jnp.dot(probs.astype(BF), grad[rows, :], preferred_element_type=F32)
            dk[keys, :] += jnp.dot(score_grad, query[rows, :], preferred_element_type=F32)
            return query_grad + jnp.dot(k_t[:, keys], score_grad, preferred_element_type=F32)

        query_grad = lax.fori_loop(
            low_block, last_block, backward, jnp.zeros((HEAD_DIM, QUERY_BLOCK), F32)
        )
        tables = cosine[rows, :], left[rows, :], right[rows, :]
        project[rows, :HEAD_DIM] = turn((query_grad * scale).T, tables, -1.0).astype(BF)
        return 0

    lax.fori_loop(0, length // QUERY_BLOCK, query_block, 0)
    tables = cosine[...], left[...], right[...]
    project[:, HEAD_DIM : 2 * HEAD_DIM] = turn(dk[...] * scale, tables, -1.0).astype(BF)
    project[:, 2 * HEAD_DIM :] = dv[...].astype(BF)


def hidden_grad_kernel(count, *refs):
    grad, slope = refs[:2]
    shards = refs[2 : 2 + 2 * count - 1]
    out, whole, sems = refs[2 + 2 * count - 1 :]

    @pl.when(pl.program_id(0) == 0)
    def _():
        load_shards(shards, whole, sems, 1)

    hidden_grad = lax.dot_general(grad[...], whole[...], LAST, preferred_element_type=F32)
    out[...] = (hidden_grad * slope[...]).astype(BF)


def attended_grad_kernel(count, *refs):
    grad = refs[0]
    shards = refs[1 : 1 + 2 * count - 1]
    out, whole, sems = refs[1 + 2 * count - 1 :]

    @pl.when(pl.program_id(0) == 0)
    def _():
        load_shards(shards, whole, sems, 1)

    out[...] = lax.dot_general(
        grad[...], whole[...], LAST, preferred_element_type=F32
    ).astype(BF)


def mixed_kernel(count, *refs):
    attended, hidden = refs[:2]
    shards = 2 * count - 1
    output_shards, down_shards = refs[2 : 2 + shards], refs[2 + shards : 2 + 2 * shards]
    out, output_whole, down_whole, output_sems, down_sems = refs[2 + 2 * shards :]

    @pl.when(pl.program_id(0) == 0)
    def _():
        load_shards(output_shards, output_whole, output_sems, 1)
        load_shards(down_shards, down_whole, down_sems, 1)

    out[...] = (
        jnp.dot(attended[...], output_whole[...], preferred_element_type=F32)
        + jnp.dot(hidden[...], down_whole[...], preferred_element_type=F32)
    ).astype(BF)


def back_kernel(count, *refs):
    act, params, project, expand = refs[:4]
    shards = 2 * count - 1
    project_shards, up_shards = refs[4 : 4 + shards], refs[4 + shards : 4 + 2 * shards]
    out, gains, project_bias, up_bias, project_whole, up_whole, project_sems, up_sems = refs[
        4 + 2 * shards :
    ]

    @pl.when(pl.program_id(0) == 0)
    def _():
        load_shards(project_shards, project_whole, project_sems, 0)
        load_shards(up_shards, up_whole, up_sems, 0)
        gains[...] = jnp.zeros_like(gains)
        project_bias[...] = jnp.zeros_like(project_bias)
        up_bias[...] = jnp.zeros_like(up_bias)

    normed, inverse_scale = normalize(act[...])
    first = lax.dot_general(project[...], project_whole[...], LAST, preferred_element_type=F32)
    second = lax.dot_general(expand[...], up_whole[...], LAST, preferred_element_type=F32)
    gains[0:1, :] += jnp.sum(first * normed, axis=0, keepdims=True)
    gains[1:2, :] += jnp.sum(first, axis=0, keepdims=True)
    gains[2:3, :] += jnp.sum(second * normed, axis=0, keepdims=True)
    gains[3:4, :] += jnp.sum(second, axis=0, keepdims=True)
    project_bias[...] += jnp.sum(project[...].astype(F32), axis=0, keepdims=True)
    up_bias[...] += jnp.sum(expand[...].astype(F32), axis=0, keepdims=True)
    normed_grad = first * params[0:1, :] + second * params[2:3, :]
    mean_grad = jnp.mean(normed_grad, axis=1, keepdims=True)
    mean_product = jnp.mean(normed_grad * normed, axis=1, keepdims=True)
    out[...] = (inverse_scale * (normed_grad - mean_grad - normed * mean_product)).astype(BF)


def tile_spec(width):
    return pl.BlockSpec((TILE, width), lambda i: (i, 0))


def fixed_spec(shape):
    return pl.BlockSpec(shape, lambda i: (0, 0))


ANY = pl.BlockSpec(memory_space=pl.ANY)


def shape_of(shape, kind):
    return jax.ShapeDtypeStruct(shape, kind)


def call(kernel, name, tokens, ins, outs, wholes, args, flops=0):
    scratch = [pltpu.VMEM(shape, BF) for shape, _ in wholes] + [
        pltpu.SemaphoreType.DMA((count,)) for _, count in wholes
    ]
    return pl.pallas_call(
        kernel,
        name=name,
        grid=(tokens // TILE,),
        in_specs=ins,
        out_specs=[spec for spec, _ in outs],
        out_shape=[shape for _, shape in outs],
        scratch_shapes=scratch,
        compiler_params=pltpu.CompilerParams(
            dimension_semantics=("arbitrary",), vmem_limit_bytes=VMEM_LIMIT
        ),
        cost_estimate=pl.CostEstimate(flops=flops, bytes_accessed=0, transcendentals=0),
    )(*args)


def angle_tables(row_total):
    positions = (jnp.arange(row_total, dtype=jnp.int32) % LENGTH).astype(F32)
    frequency = ROPE_BASE ** (-jnp.arange(0, ROTARY, 2, dtype=jnp.int32).astype(F32) / ROTARY)
    turning = positions[:, None] * frequency[None, :]
    cosine, sine = jnp.cos(turning), jnp.sin(turning)
    rest = HEAD_DIM - ROTARY
    zeros = jnp.zeros_like(sine)
    return (
        jnp.concatenate([cosine, cosine, jnp.ones((row_total, rest), F32)], axis=1),
        jnp.concatenate([-sine, zeros, jnp.zeros((row_total, rest), F32)], axis=1),
        jnp.concatenate([zeros, sine, jnp.zeros((row_total, rest), F32)], axis=1),
    )


def on_device(
    rows,
    cols,
    activations,
    document_ids,
    attention_gain,
    attention_shift,
    feedforward_gain,
    feedforward_shift,
    query_key_value,
    query_key_value_bias,
    output_weight,
    output_bias,
    up_weight,
    up_bias,
    down_weight,
    down_bias,
    out_grad,
):
    row_place, col_place = lax.axis_index("row"), lax.axis_index("col")
    tokens, features = activations.shape
    heads = query_key_value.shape[1]
    project_width, out_width = heads * 3 * HEAD_DIM, heads * HEAD_DIM
    hidden_width = up_weight.shape[1]

    norm_params = jnp.stack([attention_gain, attention_shift, feedforward_gain, feedforward_shift])
    norm_params = lax.all_gather(norm_params, "row", axis=1, tiled=True)
    full_input = lax.all_gather(activations, "row", axis=1, tiled=True)
    full_grad = lax.all_gather(out_grad, "row", axis=1, tiled=True)

    up_shards = line_gather(up_weight.astype(BF), cols)
    output_shards = line_gather(after(output_weight.astype(BF), *up_shards), cols)
    project_shards = line_gather(
        after(query_key_value.astype(BF).reshape(-1, project_width), *output_shards), cols
    )
    down_shards = line_gather(after(down_weight.astype(BF), *project_shards), cols)

    cosine, left, right = angle_tables(tokens)
    starts = jnp.sum(
        (document_ids[:, None] < document_ids[None, :]).astype(jnp.int32), axis=0
    )
    low_blocks = starts[::QUERY_BLOCK] // KEY_BLOCK

    first_norm, second_norm, hidden, slope = call(
        functools.partial(up_kernel, cols),
        "up",
        tokens,
        [tile_spec(D), fixed_spec((4, D)), fixed_spec((1, hidden_width))] + [ANY] * len(up_shards),
        [
            (tile_spec(D), shape_of((tokens, D), BF)),
            (tile_spec(D), shape_of((tokens, D), BF)),
            (tile_spec(hidden_width), shape_of((tokens, hidden_width), BF)),
            (tile_spec(hidden_width), shape_of((tokens, hidden_width), F32)),
        ],
        [((D, hidden_width), cols)],
        [full_input, norm_params, up_bias[None], *up_shards],
    )

    down_weight_part = lax.dot_general(hidden, full_grad, FIRST, preferred_element_type=F32)
    down_weight_grad = line_scatter(down_weight_part.astype(BF), cols, col_place, 1)

    (attended_grad,) = call(
        functools.partial(attended_grad_kernel, cols),
        "attended_grad",
        tokens,
        [tile_spec(D)] + [ANY] * len(output_shards),
        [(tile_spec(out_width), shape_of((tokens, out_width), BF))],
        [((out_width, D), cols)],
        [full_grad, *output_shards],
    )

    (projected,) = call(
        functools.partial(project_kernel, cols, heads),
        "project",
        tokens,
        [tile_spec(D), fixed_spec((1, project_width))]
        + [tile_spec(HEAD_DIM)] * 3
        + [ANY] * len(project_shards),
        [(tile_spec(project_width), shape_of((tokens, project_width), BF))],
        [((D, project_width), cols)],
        [
            first_norm,
            query_key_value_bias.reshape(1, -1),
            cosine,
            left,
            right,
            *project_shards,
        ],
    )

    def head_spec(part, parts):
        return pl.BlockSpec((tokens, HEAD_DIM), lambda h: (0, h * parts + part))

    whole_spec = pl.BlockSpec((tokens, HEAD_DIM), lambda h: (0, 0))
    attended, project_grad = pl.pallas_call(
        attention_kernel,
        name="attention",
        grid=(heads,),
        in_specs=[
            pl.BlockSpec(memory_space=pltpu.SMEM),
            pl.BlockSpec((1, tokens), lambda h: (0, 0)),
            whole_spec,
            whole_spec,
            whole_spec,
            head_spec(0, 3),
            head_spec(1, 3),
            head_spec(2, 3),
            head_spec(0, 1),
        ],
        out_specs=[
            head_spec(0, 1),
            pl.BlockSpec((tokens, 3 * HEAD_DIM), lambda h: (0, h)),
        ],
        out_shape=[
            shape_of((tokens, out_width), BF),
            shape_of((tokens, project_width), BF),
        ],
        scratch_shapes=[pltpu.VMEM((HEAD_DIM, tokens), BF)] * 4
        + [pltpu.VMEM((tokens, HEAD_DIM), F32)] * 2,
        compiler_params=pltpu.CompilerParams(
            dimension_semantics=("arbitrary",), vmem_limit_bytes=VMEM_LIMIT
        ),
        cost_estimate=pl.CostEstimate(flops=0, bytes_accessed=0, transcendentals=0),
    )(
        low_blocks,
        starts[None],
        cosine,
        left,
        right,
        projected,
        projected,
        projected,
        attended_grad,
    )

    out_weight_part = lax.dot_general(attended, full_grad, FIRST, preferred_element_type=F32)
    output_weight_grad = line_scatter(out_weight_part.astype(BF), cols, col_place, 1)
    project_weight_part = lax.dot_general(
        first_norm, project_grad, FIRST, preferred_element_type=F32
    )
    project_weight_grad = line_scatter(project_weight_part.astype(BF), cols, col_place, 0)
    project_weight_grad = project_weight_grad.reshape(query_key_value.shape)

    (expand_grad,) = call(
        functools.partial(hidden_grad_kernel, cols),
        "hidden_grad",
        tokens,
        [tile_spec(D), tile_spec(hidden_width)] + [ANY] * len(down_shards),
        [(tile_spec(hidden_width), shape_of((tokens, hidden_width), BF))],
        [((hidden_width, D), cols)],
        [full_grad, slope, *down_shards],
    )
    up_weight_part = lax.dot_general(second_norm, expand_grad, FIRST, preferred_element_type=F32)
    up_weight_grad = line_scatter(up_weight_part.astype(BF), cols, col_place, 0)

    (mixed_part,) = call(
        functools.partial(mixed_kernel, cols),
        "mixed",
        tokens,
        [tile_spec(out_width), tile_spec(hidden_width)] + [ANY] * (2 * len(down_shards)),
        [(tile_spec(D), shape_of((tokens, D), BF))],
        [((out_width, D), cols), ((hidden_width, D), cols)],
        [attended, hidden, *output_shards, *down_shards],
    )
    mixed_sum = lax.psum_scatter(mixed_part, "row", scatter_dimension=1, tiled=True)
    layer_out = activations.astype(F32) + mixed_sum.astype(F32) + output_bias + down_bias

    back_part, gain_terms, project_bias_grad, up_bias_grad = call(
        functools.partial(back_kernel, cols),
        "back",
        tokens,
        [tile_spec(D), fixed_spec((4, D)), tile_spec(project_width), tile_spec(hidden_width)]
        + [ANY] * (2 * len(up_shards)),
        [
            (tile_spec(D), shape_of((tokens, D), BF)),
            (fixed_spec((4, D)), shape_of((4, D), F32)),
            (fixed_spec((1, project_width)), shape_of((1, project_width), F32)),
            (fixed_spec((1, hidden_width)), shape_of((1, hidden_width), F32)),
        ],
        [((D, project_width), cols), ((D, hidden_width), cols)],
        [full_input, norm_params, project_grad, expand_grad, *project_shards, *up_shards],
    )
    back_sum = lax.psum_scatter(back_part, "row", scatter_dimension=1, tiled=True)
    grad_float = out_grad.astype(F32)
    activations_grad = grad_float + back_sum.astype(F32)

    gain_terms = gain_terms.reshape(4, rows, features).transpose(1, 0, 2).reshape(rows, -1)
    gain_terms = ring_scatter(gain_terms, "row", rows, row_place)
    shift_out_grad = jnp.sum(grad_float, axis=0)
    small = jnp.concatenate([gain_terms, project_bias_grad[0], up_bias_grad[0], shift_out_grad])
    small = ring_sum(small, "col", cols)
    sizes = [features] * 4 + [project_width, hidden_width, features]
    pieces, begin = [], 0
    for size in sizes:
        pieces.append(small[begin : begin + size])
        begin += size
    return (
        layer_out,
        activations_grad,
        pieces[0],
        pieces[1],
        pieces[2],
        pieces[3],
        project_weight_grad,
        pieces[4].reshape(query_key_value_bias.shape),
        output_weight_grad,
        pieces[6],
        up_weight_grad,
        pieces[5],
        down_weight_grad,
        pieces[6],
    )


def solution(mesh):
    placed = (
        P("col", "row"),
        P("col"),
        P("row"),
        P("row"),
        P("row"),
        P("row"),
        P("col", "row", None),
        P("row", None),
        P("row", "col"),
        P("row"),
        P("col", "row"),
        P("row"),
        P("row", "col"),
        P("row"),
        P("col", "row"),
    )

    def body(*args):
        return on_device(mesh.shape["row"], mesh.shape["col"], *args)

    return jax.shard_map(
        body,
        mesh=mesh,
        in_specs=placed,
        out_specs=(
            P("col", "row"),
            P("col", "row"),
            P("row"),
            P("row"),
            P("row"),
            P("row"),
            P("col", "row", None),
            P("row", None),
            P("row", "col"),
            P("row"),
            P("col", "row"),
            P("row"),
            P("row", "col"),
            P("row"),
        ),
        check_vma=False,
    )
```

```python
import functools

import jax
import jax.numpy as jnp
from jax import lax
from jax.experimental import pallas as pl
from jax.experimental.pallas import tpu as pltpu
from jax.sharding import PartitionSpec as P

D = 2048
HEAD_DIM = 128
ROTARY = 32
LENGTH = 2048

EPSILON = 1e-05
MASKED = -1e30
ROPE_BASE = 10000.0
BF = jnp.bfloat16
F32 = jnp.float32
LAST = (((1,), (1,)), ((), ()))
FIRST = (((0,), (0,)), ((), ()))
TILE = 256
QUERY_BLOCK = 512
KEY_BLOCK = 512
VMEM_LIMIT = 56 * 1024 * 1024
LOG2_E = 1.4426950408889634
SQRT_HALF = 0.7071067811865476
INV_SQRT_2PI = 0.3989422804014327


def after(value, gate):
    return lax.optimization_barrier((value,) + tuple(gate))[0]


class LineGather:
    def __init__(self, shard, count):
        self.shard, self.count = shard, count
        self.upward, self.downward = shard, shard
        self.from_below, self.from_above = [], []

    def step(self, gate):
        count, step = self.count, len(self.from_below) + 1
        self.upward = lax.ppermute(
            after(self.upward, gate), "col", [(k, k + 1) for k in range(step - 1, count - 1)]
        )
        self.downward = lax.ppermute(
            after(self.downward, gate), "col", [(k, k - 1) for k in range(1, count - step + 1)]
        )
        self.from_below.append(self.upward)
        self.from_above.append(self.downward)
        return [self.upward, self.downward]

    def shards(self):
        return [self.shard] + self.from_below + self.from_above


class LineScatter:
    def __init__(self, chunks, count):
        self.chunks, self.count = chunks, count
        self.upward = self.downward = None
        self.done = 0

    def step(self, gate):
        self.done += 1
        count, step = self.count, self.done
        ahead, behind = self.chunks[count - step], self.chunks[step]
        if self.upward is not None:
            ahead = (ahead.astype(F32) + self.upward.astype(F32)).astype(BF)
            behind = (behind.astype(F32) + self.downward.astype(F32)).astype(BF)
        self.upward = lax.ppermute(after(ahead, gate), "col", [(k, k + 1) for k in range(step)])
        self.downward = lax.ppermute(
            after(behind, gate), "col", [(k, k - 1) for k in range(count - step, count)]
        )
        return [self.upward, self.downward]

    def result(self):
        return self.chunks[0] + (self.upward.astype(F32) + self.downward.astype(F32))


def ring_sum(value, axis, count):
    total = value
    for back in range(1, count):
        total = total + lax.ppermute(value, axis, [(k, (k + back) % count) for k in range(count)])
    return total


def ring_scatter(value, axis, count, place):
    total = lax.dynamic_index_in_dim(value, place, 0, keepdims=False)
    for back in range(1, count):
        piece = lax.dynamic_index_in_dim(value, lax.rem(place + back, count), 0, keepdims=False)
        total = total + lax.ppermute(piece, axis, [(k, (k + back) % count) for k in range(count)])
    return total


def load_shards(refs, whole, sems, dim, columns=None):
    if columns is not None:
        refs = [ref.at[:, columns] for ref in refs]
    count = (len(refs) + 1) // 2
    extent = refs[0].shape[dim]
    place = lax.axis_index("col")

    def spot(j):
        at = pl.ds(j * extent, extent)
        return whole.at[at, :] if dim == 0 else whole.at[:, at]

    for i in range(count):

        @pl.when(place == i)
        def _():
            for j in range(count):
                if j == i:
                    source = refs[0]
                elif j < i:
                    source = refs[i - j]
                else:
                    source = refs[count - 1 + j - i]
                pltpu.make_async_copy(source, spot(j), sems.at[j]).start()

    for j in range(count):
        pltpu.make_async_copy(refs[0], spot(j), sems.at[j]).wait()


def normalize(tile):
    values = tile.astype(F32)
    centered = values - jnp.mean(values, axis=1, keepdims=True)
    inverse_scale = lax.rsqrt(jnp.mean(centered * centered, axis=1, keepdims=True) + EPSILON)
    return centered * inverse_scale, inverse_scale


def norm_kernel(act, params, first_out, second_out):
    normed, _ = normalize(act[...])
    first_out[...] = (normed * params[0:1, :] + params[1:2, :]).astype(BF)
    second_out[...] = (normed * params[2:3, :] + params[3:4, :]).astype(BF)


def up_kernel(count, *refs):
    norm, bias = refs[:2]
    shards = refs[2 : 2 + 2 * count - 1]
    hidden_out, slope_out, whole, sems = refs[2 + 2 * count - 1 :]

    @pl.when(pl.program_id(0) == 0)
    def _():
        load_shards(shards, whole, sems, 0)

    lin = jnp.dot(norm[...], whole[...], preferred_element_type=F32) + bias[...]
    cdf = 0.5 + 0.5 * lax.erf(lin * SQRT_HALF)
    hidden_out[...] = (lin * cdf).astype(BF)
    slope_out[...] = cdf + lin * (INV_SQRT_2PI * jnp.exp(-0.5 * lin * lin))


def turn(values, tables, sign):
    cosine, left, right = tables
    half = ROTARY // 2
    turned = left * pltpu.roll(values, HEAD_DIM - half, 1) + right * pltpu.roll(values, half, 1)
    return values * cosine + sign * turned


def project_kernel(count, heads, *refs):
    norm, bias, cosine, left, right = refs[:5]
    shards = refs[5 : 5 + 2 * count - 1]
    out, whole, sems = refs[5 + 2 * count - 1 :]

    @pl.when(pl.program_id(0) == 0)
    def _():
        load_shards(shards, whole, sems, 0, pl.ds(0, whole.shape[1]))

    lin = jnp.dot(norm[...], whole[...], preferred_element_type=F32) + bias[...]
    tables = cosine[...], left[...], right[...]
    for head in range(heads):
        for part in range(3):
            at = slice((head * 3 + part) * HEAD_DIM, (head * 3 + part + 1) * HEAD_DIM)
            piece = lin[:, at]
            out[:, at] = (turn(piece, tables, 1.0) if part < 2 else piece).astype(BF)


def attended_grad_kernel(count, *refs):
    grad = refs[0]
    shards = refs[1 : 1 + 2 * count - 1]
    out, whole, sems = refs[1 + 2 * count - 1 :]

    @pl.when(pl.program_id(0) == 0)
    def _():
        columns = pl.ds(shards[0].shape[1] - whole.shape[1], whole.shape[1])
        load_shards(shards, whole, sems, 0, columns)

    out[...] = jnp.dot(grad[...], whole[...], preferred_element_type=F32).astype(BF)


def attention_kernel(
    heads,
    low,
    start,
    cosine,
    left,
    right,
    project,
    grad,
    *rest,
):
    out, project_grad, k_t, v_t, dk, dv, kept_scores, kept_grads = rest[-8:]
    length = project.shape[0]
    scale = HEAD_DIM**-0.5

    def column(head, part):
        return slice((3 * head + part) * HEAD_DIM, (3 * head + part + 1) * HEAD_DIM)

    def own(head):
        return slice(head * HEAD_DIM, (head + 1) * HEAD_DIM)

    for head in range(heads):
        k_t[head] = project[:, column(head, 1)].T
        v_t[head] = project[:, column(head, 2)].T
    dk[...] = jnp.zeros_like(dk)
    dv[...] = jnp.zeros_like(dv)

    def query_block(block, _):
        rows = pl.ds(pl.multiple_of(block * QUERY_BLOCK, QUERY_BLOCK), QUERY_BLOCK)
        first = start[:, rows]
        place = block * QUERY_BLOCK + lax.broadcasted_iota(jnp.int32, (1, QUERY_BLOCK), 1)

        def keys_of(at):
            return pl.ds(pl.multiple_of(at * KEY_BLOCK, KEY_BLOCK), KEY_BLOCK)

        def forward(at, carry):
            keys, made = keys_of(at), []
            key_place = at * KEY_BLOCK + lax.broadcasted_iota(
                jnp.int32, (KEY_BLOCK, QUERY_BLOCK), 0
            )
            allowed = (key_place >= first) & (key_place <= place)
            for head in range(heads):
                largest, total, weighted, produced = carry[head]
                scores = lax.dot_general(
                    project[keys, column(head, 1)],
                    project[rows, column(head, 0)],
                    LAST,
                    preferred_element_type=F32,
                ) * (scale * LOG2_E)
                scores = jnp.where(allowed, scores, MASKED)
                prob_grad = lax.dot_general(
                    project[keys, column(head, 2)],
                    grad[rows, own(head)],
                    LAST,
                    preferred_element_type=F32,
                )
                kept_scores[head, keys, :] = scores
                kept_grads[head, keys, :] = prob_grad
                newest = jnp.maximum(largest, jnp.max(scores, axis=0, keepdims=True))
                shrink = jnp.exp2(largest - newest)
                parts = jnp.exp2(scores - newest)
                total = total * shrink + jnp.sum(parts, axis=0, keepdims=True)
                weighted = weighted * shrink + jnp.sum(parts * prob_grad, axis=0, keepdims=True)
                produced = produced * shrink + jnp.dot(
                    v_t[head, :, keys], parts.astype(BF), preferred_element_type=F32
                )
                made.append((newest, total, weighted, produced))
            return tuple(made)

        empty = jnp.zeros((1, QUERY_BLOCK), F32)
        wide = jnp.zeros((HEAD_DIM, QUERY_BLOCK), F32)
        first_block, last_block = low[block], (block + 1) * (QUERY_BLOCK // KEY_BLOCK)
        carry = lax.fori_loop(
            first_block, last_block, forward, ((empty + MASKED, empty, empty, wide),) * heads
        )
        log_totals, deltas = [], []
        for head in range(heads):
            largest, total, weighted, produced = carry[head]
            inverse = 1.0 / total
            out[rows, own(head)] = (produced * inverse).T.astype(BF)
            log_totals.append(largest + jnp.log2(total))
            deltas.append(weighted * inverse)

        def backward(at, query_grads):
            keys, made = keys_of(at), []
            for head in range(heads):
                probs = jnp.exp2(kept_scores[head, keys, :] - log_totals[head])
                score_grad = (probs * (kept_grads[head, keys, :] - deltas[head])).astype(BF)
                dv[head, keys, :] += jnp.dot(
                    probs.astype(BF), grad[rows, own(head)], preferred_element_type=F32
                )
                dk[head, keys, :] += jnp.dot(
                    score_grad, project[rows, column(head, 0)], preferred_element_type=F32
                )
                made.append(
                    query_grads[head]
                    + jnp.dot(k_t[head, :, keys], score_grad, preferred_element_type=F32)
                )
            return tuple(made)

        query_grads = lax.fori_loop(first_block, last_block, backward, (wide,) * heads)
        tables = cosine[rows, :], left[rows, :], right[rows, :]
        for head in range(heads):
            project_grad[rows, column(head, 0)] = turn(
                (query_grads[head] * scale).T, tables, -1.0
            ).astype(BF)
        return 0

    lax.fori_loop(0, length // QUERY_BLOCK, query_block, 0)
    tables = cosine[...], left[...], right[...]
    for head in range(heads):
        project_grad[:, column(head, 1)] = turn(dk[head] * scale, tables, -1.0).astype(BF)
        project_grad[:, column(head, 2)] = dv[head].astype(BF)


def mixed_kernel(count, *refs):
    attended, hidden = refs[:2]
    shards = 2 * count - 1
    pack_shards, down_shards = refs[2 : 2 + shards], refs[2 + shards : 2 + 2 * shards]
    out, output_whole, down_whole, output_sems, down_sems = refs[2 + 2 * shards :]

    @pl.when(pl.program_id(0) == 0)
    def _():
        width = pack_shards[0].shape[1]
        columns = pl.ds(width - output_whole.shape[1], output_whole.shape[1])
        load_shards(pack_shards, output_whole, output_sems, 0, columns)
        load_shards(down_shards, down_whole, down_sems, 1)

    out[...] = (
        lax.dot_general(attended[...], output_whole[...], LAST, preferred_element_type=F32)
        + jnp.dot(hidden[...], down_whole[...], preferred_element_type=F32)
    ).astype(BF)


def hidden_grad_kernel(count, *refs):
    grad, slope = refs[:2]
    shards = refs[2 : 2 + 2 * count - 1]
    out, whole, sems = refs[2 + 2 * count - 1 :]

    @pl.when(pl.program_id(0) == 0)
    def _():
        load_shards(shards, whole, sems, 1)

    hidden_grad = lax.dot_general(grad[...], whole[...], LAST, preferred_element_type=F32)
    out[...] = (hidden_grad * slope[...]).astype(BF)


def weight_grad_kernel(count, pairs, *refs):
    lefts_rights, outs = refs[: 2 * pairs], refs[2 * pairs :]
    for step in range(count):

        @pl.when(pl.program_id(0) == step)
        def _():
            begin = 0
            for pair in range(pairs):
                left, right = lefts_rights[2 * pair], lefts_rights[2 * pair + 1]
                made = lax.dot_general(left[...], right[...], FIRST, preferred_element_type=F32)
                width = made.shape[1]
                outs[step][:, begin : begin + width] = made.astype(outs[step].dtype)
                begin += width


def back_kernel(count, *refs):
    act, params, project, expand = refs[:4]
    shards = 2 * count - 1
    project_shards, up_shards = refs[4 : 4 + shards], refs[4 + shards : 4 + 2 * shards]
    out, gains, project_bias, up_bias, project_whole, up_whole, project_sems, up_sems = refs[
        4 + 2 * shards :
    ]

    @pl.when(pl.program_id(0) == 0)
    def _():
        load_shards(project_shards, project_whole, project_sems, 0, pl.ds(0, project_whole.shape[1]))
        load_shards(up_shards, up_whole, up_sems, 0)
        gains[...] = jnp.zeros_like(gains)
        project_bias[...] = jnp.zeros_like(project_bias)
        up_bias[...] = jnp.zeros_like(up_bias)

    normed, inverse_scale = normalize(act[...])
    first = lax.dot_general(project[...], project_whole[...], LAST, preferred_element_type=F32)
    second = lax.dot_general(expand[...], up_whole[...], LAST, preferred_element_type=F32)
    gains[0:1, :] += jnp.sum(first * normed, axis=0, keepdims=True)
    gains[1:2, :] += jnp.sum(first, axis=0, keepdims=True)
    gains[2:3, :] += jnp.sum(second * normed, axis=0, keepdims=True)
    gains[3:4, :] += jnp.sum(second, axis=0, keepdims=True)
    project_bias[...] += jnp.sum(project[...].astype(F32), axis=0, keepdims=True)
    up_bias[...] += jnp.sum(expand[...].astype(F32), axis=0, keepdims=True)
    normed_grad = first * params[0:1, :] + second * params[2:3, :]
    mean_grad = jnp.mean(normed_grad, axis=1, keepdims=True)
    mean_product = jnp.mean(normed_grad * normed, axis=1, keepdims=True)
    out[...] = (inverse_scale * (normed_grad - mean_grad - normed * mean_product)).astype(BF)


def tile_spec(width):
    return pl.BlockSpec((TILE, width), lambda i: (i, 0))


def fixed_spec(shape):
    return pl.BlockSpec(shape, lambda i: (0, 0))


ANY = pl.BlockSpec(memory_space=pl.ANY)


def shape_of(shape, kind):
    return jax.ShapeDtypeStruct(shape, kind)


def cost(flops, moved=0):
    return pl.CostEstimate(flops=int(flops), bytes_accessed=int(moved), transcendentals=0)


def call(kernel, name, tokens, ins, outs, wholes, args, moved=0):
    scratch = [pltpu.VMEM(shape, BF) for shape, _ in wholes] + [
        pltpu.SemaphoreType.DMA((count,)) for _, count in wholes
    ]
    return pl.pallas_call(
        kernel,
        name=name,
        grid=(tokens // TILE,),
        in_specs=ins,
        out_specs=[spec for spec, _ in outs],
        out_shape=[shape for _, shape in outs],
        scratch_shapes=scratch,
        compiler_params=pltpu.CompilerParams(
            dimension_semantics=("arbitrary",), vmem_limit_bytes=VMEM_LIMIT
        ),
        cost_estimate=cost(sum(2 * tokens * shape[0] * shape[1] for shape, _ in wholes), moved),
    )(*args)


def weight_grad(count, place, pairs, chunked_right=False):
    specs, arrays, width = [], [], 0
    for left, right in pairs:
        chunked, fixed = (right, left) if chunked_right else (left, right)
        extent = chunked.shape[1] // count
        chunk_spec = pl.BlockSpec(
            (chunked.shape[0], extent), lambda i, spot: (0, lax.rem(spot[0] + i, count))
        )
        fixed_spec_ = pl.BlockSpec(fixed.shape, lambda i, spot: (0, 0))
        specs += [fixed_spec_, chunk_spec] if chunked_right else [chunk_spec, fixed_spec_]
        arrays += [left, right]
        rows, columns = (fixed.shape[1], extent) if chunked_right else (extent, fixed.shape[1])
        width += columns
    shape = (rows, width)
    return pl.pallas_call(
        functools.partial(drop_first, functools.partial(weight_grad_kernel, count, len(pairs))),
        name="weight_grad",
        grid_spec=pltpu.PrefetchScalarGridSpec(
            num_scalar_prefetch=1,
            grid=(count,),
            in_specs=specs,
            out_specs=[pl.BlockSpec(shape, lambda i, spot: (0, 0))] * count,
        ),
        out_shape=[shape_of(shape, F32 if r == 0 else BF) for r in range(count)],
        compiler_params=pltpu.CompilerParams(
            dimension_semantics=("arbitrary",), vmem_limit_bytes=VMEM_LIMIT
        ),
        cost_estimate=cost(2 * arrays[0].shape[0] * rows * width * count),
    )(place[None], *arrays)


def drop_first(kernel, spot, *refs):
    kernel(*refs)


def angle_tables(row_total):
    positions = (jnp.arange(row_total, dtype=jnp.int32) % LENGTH).astype(F32)
    frequency = ROPE_BASE ** (-jnp.arange(0, ROTARY, 2, dtype=jnp.int32).astype(F32) / ROTARY)
    turning = positions[:, None] * frequency[None, :]
    cosine, sine = jnp.cos(turning), jnp.sin(turning)
    rest = HEAD_DIM - ROTARY
    zeros = jnp.zeros_like(sine)
    return (
        jnp.concatenate([cosine, cosine, jnp.ones((row_total, rest), F32)], axis=1),
        jnp.concatenate([-sine, zeros, jnp.zeros((row_total, rest), F32)], axis=1),
        jnp.concatenate([zeros, sine, jnp.zeros((row_total, rest), F32)], axis=1),
    )


def on_device(
    rows,
    cols,
    activations,
    document_ids,
    attention_gain,
    attention_shift,
    feedforward_gain,
    feedforward_shift,
    query_key_value,
    query_key_value_bias,
    output_weight,
    output_bias,
    up_weight,
    up_bias,
    down_weight,
    down_bias,
    out_grad,
):
    row_place, col_place = lax.axis_index("row"), lax.axis_index("col")
    tokens, features = activations.shape
    heads = query_key_value.shape[1]
    project_width, out_width = heads * 3 * HEAD_DIM, heads * HEAD_DIM
    hidden_width = up_weight.shape[1]

    full_input = lax.all_gather(activations, "row", axis=1, tiled=True)
    full_grad = lax.all_gather(out_grad, "row", axis=1, tiled=True)

    pack = jnp.concatenate(
        [query_key_value.astype(BF).reshape(-1, project_width), output_weight.astype(BF).T], axis=1
    )
    pack_gather = LineGather(pack, cols)
    up_gather = LineGather(up_weight.astype(BF), cols)
    down_gather = LineGather(down_weight.astype(BF), cols)

    def slot(transfers, gate, *works):
        moved = []
        for transfer in transfers:
            moved += transfer.step(gate)
        made = [work(gate) for work in works]
        return moved + [array for arrays in made for array in arrays], made

    def more(transfers, gate):
        for _ in range(cols - 4):
            gate, _ = slot(transfers, gate)
        return gate

    def tables_work(gate):
        cosine, left, right = angle_tables(tokens)
        starts = jnp.sum(
            (document_ids[:, None] < document_ids[None, :]).astype(jnp.int32), axis=0
        )
        return cosine, left, right, starts

    def params_work(gate):
        stacked = jnp.stack(
            [attention_gain, attention_shift, feedforward_gain, feedforward_shift]
        )
        return [lax.all_gather(after(stacked, gate), "row", axis=1, tiled=True)]

    def norm_work(gate):
        return call(
            norm_kernel,
            "norm",
            tokens,
            [tile_spec(D), fixed_spec((4, D))],
            [
                (tile_spec(D), shape_of((tokens, D), BF)),
                (tile_spec(D), shape_of((tokens, D), BF)),
            ],
            [],
            [full_input, after(norm_params, gate)],
            6 * tokens * D,
        )

    gate, ((cosine, left, right, starts),) = slot([pack_gather], [], tables_work)
    low_blocks = starts[::QUERY_BLOCK] // KEY_BLOCK
    gate, ((norm_params,),) = slot([pack_gather], gate, params_work)
    gate = more([pack_gather], gate)
    gate, ((first_norm, second_norm),) = slot([pack_gather], gate, norm_work)
    pack_shards = pack_gather.shards()

    def project_work(gate):
        return call(
            functools.partial(project_kernel, cols, heads),
            "project",
            tokens,
            [tile_spec(D), fixed_spec((1, project_width))]
            + [tile_spec(HEAD_DIM)] * 3
            + [ANY] * len(pack_shards),
            [(tile_spec(project_width), shape_of((tokens, project_width), BF))],
            [((D, project_width), cols)],
            [
                after(first_norm, gate),
                query_key_value_bias.reshape(1, -1),
                cosine,
                left,
                right,
                *pack_shards,
            ],
        )

    def attended_grad_work(gate):
        return call(
            functools.partial(attended_grad_kernel, cols),
            "attended_grad",
            tokens,
            [tile_spec(D)] + [ANY] * len(pack_shards),
            [(tile_spec(out_width), shape_of((tokens, out_width), BF))],
            [((D, out_width), cols)],
            [after(full_grad, gate), *pack_shards],
        )

    def attention_work(head, attended_grad, before):
        def column_spec(width, at=0):
            return pl.BlockSpec((tokens, width), lambda i: (0, at))

        shapes = [shape_of((tokens, out_width), BF), shape_of((tokens, project_width), BF)]
        return pl.pallas_call(
            functools.partial(attention_kernel, 1),
            name="attention",
            grid=(1,),
            in_specs=[
                pl.BlockSpec(memory_space=pltpu.SMEM),
                pl.BlockSpec((1, tokens), lambda i: (0, 0)),
                column_spec(HEAD_DIM),
                column_spec(HEAD_DIM),
                column_spec(HEAD_DIM),
                column_spec(3 * HEAD_DIM, head),
                column_spec(HEAD_DIM, head),
            ]
            + [ANY] * len(before),
            out_specs=[column_spec(HEAD_DIM, head), column_spec(3 * HEAD_DIM, head)],
            out_shape=shapes,
            input_output_aliases={7 + i: i for i in range(len(before))},
            scratch_shapes=[pltpu.VMEM((1, HEAD_DIM, tokens), BF)] * 2
            + [pltpu.VMEM((1, tokens, HEAD_DIM), F32)] * 2
            + [pltpu.VMEM((1, tokens, QUERY_BLOCK), F32)] * 2,
            compiler_params=pltpu.CompilerParams(vmem_limit_bytes=VMEM_LIMIT),
            cost_estimate=cost(24 * tokens * tokens * HEAD_DIM),
        )(low_blocks, starts[None], cosine, left, right, projected, attended_grad, *before)

    gate, ((projected,),) = slot([up_gather], gate, project_work)

    def first_head_work(gate):
        (attended_grad,) = attended_grad_work(gate)
        return [attended_grad, *attention_work(0, attended_grad, [])]

    gate, ((attended_grad, attended, project_grad),) = slot([up_gather], gate, first_head_work)
    gate = more([up_gather], gate)

    def other_heads_work(gate):
        made = [attended, project_grad]
        grads = after(attended_grad, gate)
        for head in range(1, heads):
            made = attention_work(head, grads, made)
        return made

    gate, ((attended, project_grad),) = slot([up_gather], gate, other_heads_work)
    up_shards = up_gather.shards()

    def pack_weight_work(gate):
        return weight_grad(
            cols, col_place, [(first_norm, after(project_grad, gate)), (full_grad, attended)]
        )

    def up_work(gate):
        return call(
            functools.partial(up_kernel, cols),
            "up",
            tokens,
            [tile_spec(D), fixed_spec((1, hidden_width))] + [ANY] * len(up_shards),
            [
                (tile_spec(hidden_width), shape_of((tokens, hidden_width), BF)),
                (tile_spec(hidden_width), shape_of((tokens, hidden_width), F32)),
            ],
            [((D, hidden_width), cols)],
            [after(second_norm, gate), up_bias[None], *up_shards],
        )

    def down_weight_work(gate):
        return weight_grad(cols, col_place, [(after(hidden, gate), full_grad)], True)

    gate, (pack_chunks,) = slot([down_gather], gate, pack_weight_work)
    pack_scatter = LineScatter(pack_chunks, cols)
    gate, ((hidden, slope),) = slot([pack_scatter, down_gather], gate, up_work)
    gate = more([pack_scatter, down_gather], gate)
    gate, (down_chunks,) = slot([pack_scatter, down_gather], gate, down_weight_work)
    down_shards = down_gather.shards()
    down_scatter = LineScatter(down_chunks, cols)

    def mixed_work(gate):
        return call(
            functools.partial(mixed_kernel, cols),
            "mixed",
            tokens,
            [tile_spec(out_width), tile_spec(hidden_width)] + [ANY] * (2 * len(down_shards)),
            [(tile_spec(D), shape_of((tokens, D), BF))],
            [((D, out_width), cols), ((hidden_width, D), cols)],
            [after(attended, gate), hidden, *pack_shards, *down_shards],
        )

    def hidden_grad_work(gate):
        return call(
            functools.partial(hidden_grad_kernel, cols),
            "hidden_grad",
            tokens,
            [tile_spec(D), tile_spec(hidden_width)] + [ANY] * len(down_shards),
            [(tile_spec(hidden_width), shape_of((tokens, hidden_width), BF))],
            [((hidden_width, D), cols)],
            [after(full_grad, gate), slope, *down_shards],
        )

    def back_work(gate):
        return call(
            functools.partial(back_kernel, cols),
            "back",
            tokens,
            [tile_spec(D), fixed_spec((4, D)), tile_spec(project_width), tile_spec(hidden_width)]
            + [ANY] * (2 * len(up_shards)),
            [
                (tile_spec(D), shape_of((tokens, D), BF)),
                (fixed_spec((4, D)), shape_of((4, D), F32)),
                (fixed_spec((1, project_width)), shape_of((1, project_width), F32)),
                (fixed_spec((1, hidden_width)), shape_of((1, hidden_width), F32)),
            ],
            [((D, project_width), cols), ((D, hidden_width), cols)],
            [
                full_input,
                norm_params,
                project_grad,
                after(expand_grad, gate),
                *pack_shards,
                *up_shards,
            ],
        )

    def up_weight_work(gate):
        return weight_grad(cols, col_place, [(second_norm, after(expand_grad, gate))])

    def pack_result_work(gate):
        return [pack_scatter.result()]

    def down_result_work(gate):
        return [down_scatter.result()]

    def layer_out_work(gate):
        return [
            activations.astype(F32) + after(mixed_sum, gate).astype(F32) + output_bias + down_bias
        ]

    gate, ((mixed_part,),) = slot([pack_scatter], gate, mixed_work)
    mixed_sum = lax.psum_scatter(after(mixed_part, gate), "row", scatter_dimension=1, tiled=True)
    gate, ((expand_grad,), (pack_weight_grad,)) = slot(
        [down_scatter], gate, hidden_grad_work, pack_result_work
    )
    project_weight_grad = pack_weight_grad[:, :project_width].reshape(query_key_value.shape)
    output_weight_grad = pack_weight_grad[:, project_width:].T
    gate = more([down_scatter], gate)
    gate, ((back_part, gain_terms, project_bias_grad, up_bias_grad),) = slot(
        [down_scatter], gate, back_work
    )
    back_sum = lax.psum_scatter(after(back_part, gate), "row", scatter_dimension=1, tiled=True)
    gate, (up_chunks,) = slot([down_scatter], gate, up_weight_work)
    up_scatter = LineScatter(up_chunks, cols)
    gate, ((down_weight_grad,),) = slot([up_scatter], gate, down_result_work)
    gate = more([up_scatter], gate)
    gate, ((layer_out,),) = slot([up_scatter], gate, layer_out_work)
    gate, _ = slot([up_scatter], gate)
    up_weight_grad = up_scatter.result()
    grad_float = out_grad.astype(F32)
    activations_grad = grad_float + back_sum.astype(F32)

    gain_terms = gain_terms.reshape(4, rows, features).transpose(1, 0, 2).reshape(rows, -1)
    gain_terms = ring_scatter(gain_terms, "row", rows, row_place)
    shift_out_grad = jnp.sum(grad_float, axis=0)
    small = jnp.concatenate([gain_terms, project_bias_grad[0], up_bias_grad[0], shift_out_grad])
    small = ring_sum(small, "col", cols)
    sizes = [features] * 4 + [project_width, hidden_width, features]
    pieces, begin = [], 0
    for size in sizes:
        pieces.append(small[begin : begin + size])
        begin += size
    return (
        layer_out,
        activations_grad,
        pieces[0],
        pieces[1],
        pieces[2],
        pieces[3],
        project_weight_grad,
        pieces[4].reshape(query_key_value_bias.shape),
        output_weight_grad,
        pieces[6],
        up_weight_grad,
        pieces[5],
        down_weight_grad,
        pieces[6],
    )


def solution(mesh):
    placed = (
        P("col", "row"),
        P("col"),
        P("row"),
        P("row"),
        P("row"),
        P("row"),
        P("col", "row", None),
        P("row", None),
        P("row", "col"),
        P("row"),
        P("col", "row"),
        P("row"),
        P("row", "col"),
        P("row"),
        P("col", "row"),
    )

    def body(*args):
        return on_device(mesh.shape["row"], mesh.shape["col"], *args)

    return jax.shard_map(
        body,
        mesh=mesh,
        in_specs=placed,
        out_specs=(
            P("col", "row"),
            P("col", "row"),
            P("row"),
            P("row"),
            P("row"),
            P("row"),
            P("col", "row", None),
            P("row", None),
            P("row", "col"),
            P("row"),
            P("col", "row"),
            P("row"),
            P("row", "col"),
            P("row"),
        ),
        check_vma=False,
    )
```

```python
import functools

import jax
import jax.numpy as jnp
from jax import lax
from jax.experimental import pallas as pl
from jax.experimental.pallas import tpu as pltpu
from jax.sharding import PartitionSpec as P

D = 2048
HEAD_DIM = 128
ROTARY = 32
LENGTH = 2048

EPSILON = 1e-05
MASKED = -1e30
ROPE_BASE = 10000.0
BF = jnp.bfloat16
F32 = jnp.float32
LAST = (((1,), (1,)), ((), ()))
FIRST = (((0,), (0,)), ((), ()))
TILE = 256
QUERY_BLOCK = 512
KEY_BLOCK = 512
VMEM_LIMIT = 56 * 1024 * 1024
LOG2_E = 1.4426950408889634
SQRT_HALF = 0.7071067811865476
INV_SQRT_2PI = 0.3989422804014327


def after(value, gate):
    return lax.optimization_barrier((value,) + tuple(gate))[0]


class RingGather:
    def __init__(self, shard, count):
        self.count, self.arrays = count, [shard]

    def step(self, gate):
        count = self.count
        pairs = [(k, (k + 1) % count) for k in range(count)]
        self.arrays = self.arrays + [lax.ppermute(after(self.arrays[-1], gate), "col", pairs)]
        return self.arrays[-1:]

    def shards(self):
        count = self.count
        return self.arrays, [[(i - j) % count for j in range(count)] for i in range(count)]


class RingScatter:
    def __init__(self, chunks, count):
        self.chunks, self.count = chunks, count
        self.moving, self.done = None, 0

    def step(self, gate):
        self.done += 1
        count = self.count
        sent = self.chunks[count - self.done]
        if self.moving is not None:
            sent = (sent.astype(F32) + self.moving.astype(F32)).astype(BF)
        pairs = [(k, (k + 1) % count) for k in range(count)]
        self.moving = lax.ppermute(after(sent, gate), "col", pairs)
        return [self.moving]

    def result(self):
        return self.chunks[0] + self.moving.astype(F32)


class LineBoth:
    def __init__(self, shard, place):
        self.shard, self.place = shard, place
        self.upward, self.downward = [shard], [shard]

    def step(self, gate):
        place, done = self.place, len(self.upward)
        up, down = self.upward[-1], self.downward[-1]
        if done == 2:
            up = jnp.where(place == 0, self.chunks[3], up)
            down = jnp.where(place == 3, self.chunks[1], down)
        elif done == 3:
            up = jnp.where(place == 2, up, self.add(2, up))
            down = jnp.where(place == 1, down, self.add(2, down))
        elif done == 4:
            up, down = self.add(1, up), self.add(3, down)
        up, down = after(up, gate), after(down, gate)
        self.upward.append(lax.ppermute(up, "col", [(0, 1), (1, 2), (2, 3)]))
        self.downward.append(lax.ppermute(down, "col", [(3, 2), (2, 1), (1, 0)]))
        return [self.upward[-1], self.downward[-1]]

    def add(self, at, array):
        return (self.chunks[at].astype(F32) + array.astype(F32)).astype(BF)

    def shards(self):
        table = [[0 if j == i else i - j if j < i else 3 + j - i for j in range(4)] for i in range(4)]
        return self.upward[:4] + self.downward[1:4], table

    def result(self):
        return self.chunks[0] + (self.upward[4].astype(F32) + self.downward[4].astype(F32))


def pair_sum(value, axis, count):
    mask = 1
    while mask < count:
        value = value + lax.ppermute(value, axis, [(k, k ^ mask) for k in range(count)])
        mask *= 2
    return value


def pair_scatter(value, axis, count, place):
    mask = count // 2
    while mask:
        upper = lax.rem(place // mask, 2) == 1
        low, high = value[:mask], value[mask:]
        kept, sent = jnp.where(upper, high, low), jnp.where(upper, low, high)
        value = kept + lax.ppermute(sent, axis, [(k, k ^ mask) for k in range(count)])
        mask //= 2
    return value[0]


def load_shards(refs, table, whole, sems, dim, columns=None):
    if columns is not None:
        refs = [ref.at[:, columns] for ref in refs]
    count = len(table)
    extent = refs[0].shape[dim]
    place = lax.axis_index("col")

    def spot(j):
        at = pl.ds(j * extent, extent)
        return whole.at[at, :] if dim == 0 else whole.at[:, at]

    for i in range(count):

        @pl.when(place == i)
        def _():
            for j in range(count):
                pltpu.make_async_copy(refs[table[i][j]], spot(j), sems.at[j]).start()

    for j in range(count):
        pltpu.make_async_copy(refs[0], spot(j), sems.at[j]).wait()


def normalize(tile):
    values = tile.astype(F32)
    centered = values - jnp.mean(values, axis=1, keepdims=True)
    inverse_scale = lax.rsqrt(jnp.mean(centered * centered, axis=1, keepdims=True) + EPSILON)
    return centered * inverse_scale, inverse_scale


def norm_kernel(act, params, first_out, second_out):
    normed, _ = normalize(act[...])
    first_out[...] = (normed * params[0:1, :] + params[1:2, :]).astype(BF)
    second_out[...] = (normed * params[2:3, :] + params[3:4, :]).astype(BF)


def up_kernel(table, *refs):
    norm, bias, *shards = refs[:-4]
    hidden_out, slope_out, whole, sems = refs[-4:]

    @pl.when(pl.program_id(0) == 0)
    def _():
        load_shards(shards, table, whole, sems, 0)

    lin = jnp.dot(norm[...], whole[...], preferred_element_type=F32) + bias[...]
    cdf = 0.5 + 0.5 * lax.erf(lin * SQRT_HALF)
    hidden_out[...] = (lin * cdf).astype(BF)
    slope_out[...] = cdf + lin * (INV_SQRT_2PI * jnp.exp(-0.5 * lin * lin))


def turn(values, tables, sign):
    cosine, left, right = tables
    half = ROTARY // 2
    turned = left * pltpu.roll(values, HEAD_DIM - half, 1) + right * pltpu.roll(values, half, 1)
    return values * cosine + sign * turned


def project_kernel(table, heads, *refs):
    norm, bias, cosine, left, right, *shards = refs[:-3]
    out, whole, sems = refs[-3:]

    @pl.when(pl.program_id(0) == 0)
    def _():
        load_shards(shards, table, whole, sems, 0, pl.ds(0, whole.shape[1]))

    lin = jnp.dot(norm[...], whole[...], preferred_element_type=F32) + bias[...]
    tables = cosine[...], left[...], right[...]
    for head in range(heads):
        for part in range(3):
            at = slice((head * 3 + part) * HEAD_DIM, (head * 3 + part + 1) * HEAD_DIM)
            piece = lin[:, at]
            out[:, at] = (turn(piece, tables, 1.0) if part < 2 else piece).astype(BF)


def attended_grad_kernel(table, *refs):
    grad, *shards = refs[:-3]
    out, whole, sems = refs[-3:]

    @pl.when(pl.program_id(0) == 0)
    def _():
        columns = pl.ds(shards[0].shape[1] - whole.shape[1], whole.shape[1])
        load_shards(shards, table, whole, sems, 0, columns)

    out[...] = jnp.dot(grad[...], whole[...], preferred_element_type=F32).astype(BF)


def head_columns(head, part):
    return slice((3 * head + part) * HEAD_DIM, (3 * head + part + 1) * HEAD_DIM)


def own_columns(head):
    return slice(head * HEAD_DIM, (head + 1) * HEAD_DIM)


def rows_of(block, extent):
    return pl.ds(pl.multiple_of(block * extent, extent), extent)


def allowed_scores(project, start, block, at, head):
    rows, keys = rows_of(block, QUERY_BLOCK), rows_of(at, KEY_BLOCK)
    scores = lax.dot_general(
        project[keys, head_columns(head, 1)],
        project[rows, head_columns(head, 0)],
        LAST,
        preferred_element_type=F32,
    ) * (HEAD_DIM**-0.5 * LOG2_E)
    place = block * QUERY_BLOCK + lax.broadcasted_iota(jnp.int32, (1, QUERY_BLOCK), 1)
    key_place = at * KEY_BLOCK + lax.broadcasted_iota(jnp.int32, (KEY_BLOCK, QUERY_BLOCK), 0)
    allowed = (key_place >= start[:, rows]) & (key_place <= place)
    return jnp.where(allowed, scores, MASKED)


def attention_kernel(heads, low, start, project, out, produced_t, log_total, v_t):
    length = project.shape[0]
    for head in range(heads):
        v_t[head] = project[:, head_columns(head, 2)].T

    def query_block(block, _):
        rows = rows_of(block, QUERY_BLOCK)

        def forward(at, carry):
            keys, made = rows_of(at, KEY_BLOCK), []
            for head in range(heads):
                largest, total, produced = carry[head]
                scores = allowed_scores(project, start, block, at, head)
                newest = jnp.maximum(largest, jnp.max(scores, axis=0, keepdims=True))
                shrink = jnp.exp2(largest - newest)
                parts = jnp.exp2(scores - newest)
                total = total * shrink + jnp.sum(parts, axis=0, keepdims=True)
                produced = produced * shrink + jnp.dot(
                    v_t[head, :, keys], parts.astype(BF), preferred_element_type=F32
                )
                made.append((newest, total, produced))
            return tuple(made)

        empty = jnp.zeros((1, QUERY_BLOCK), F32)
        wide = jnp.zeros((HEAD_DIM, QUERY_BLOCK), F32)
        last_block = (block + 1) * (QUERY_BLOCK // KEY_BLOCK)
        carry = lax.fori_loop(
            low[block], last_block, forward, ((empty + MASKED, empty, wide),) * heads
        )
        for head in range(heads):
            largest, total, produced = carry[head]
            produced = produced * (1.0 / total)
            out[rows, own_columns(head)] = produced.T.astype(BF)
            produced_t[own_columns(head), rows] = produced
            log_total[head : head + 1, rows] = largest + jnp.log2(total)
        return 0

    lax.fori_loop(0, length // QUERY_BLOCK, query_block, 0)


def attention_back_kernel(
    heads,
    low,
    start,
    cosine,
    left,
    right,
    project,
    grad,
    produced_t,
    log_total,
    project_grad,
    k_t,
    dk,
    dv,
):
    length = project.shape[0]
    scale = HEAD_DIM**-0.5
    for head in range(heads):
        k_t[head] = project[:, head_columns(head, 1)].T
    dk[...] = jnp.zeros_like(dk)
    dv[...] = jnp.zeros_like(dv)

    def query_block(block, _):
        rows = rows_of(block, QUERY_BLOCK)
        deltas = [
            jnp.sum(
                produced_t[own_columns(head), rows] * grad[rows, own_columns(head)].astype(F32).T,
                axis=0,
                keepdims=True,
            )
            for head in range(heads)
        ]

        def backward(at, query_grads):
            keys, made = rows_of(at, KEY_BLOCK), []
            for head in range(heads):
                scores = allowed_scores(project, start, block, at, head)
                prob_grad = lax.dot_general(
                    project[keys, head_columns(head, 2)],
                    grad[rows, own_columns(head)],
                    LAST,
                    preferred_element_type=F32,
                )
                probs = jnp.exp2(scores - log_total[head : head + 1, rows])
                score_grad = (probs * (prob_grad - deltas[head])).astype(BF)
                dv[head, keys, :] += jnp.dot(
                    probs.astype(BF), grad[rows, own_columns(head)], preferred_element_type=F32
                )
                dk[head, keys, :] += jnp.dot(
                    score_grad, project[rows, head_columns(head, 0)], preferred_element_type=F32
                )
                made.append(
                    query_grads[head]
                    + jnp.dot(k_t[head, :, keys], score_grad, preferred_element_type=F32)
                )
            return tuple(made)

        wide = jnp.zeros((HEAD_DIM, QUERY_BLOCK), F32)
        last_block = (block + 1) * (QUERY_BLOCK // KEY_BLOCK)
        query_grads = lax.fori_loop(low[block], last_block, backward, (wide,) * heads)
        tables = cosine[rows, :], left[rows, :], right[rows, :]
        for head in range(heads):
            project_grad[rows, head_columns(head, 0)] = turn(
                (query_grads[head] * scale).T, tables, -1.0
            ).astype(BF)
        return 0

    lax.fori_loop(0, length // QUERY_BLOCK, query_block, 0)
    tables = cosine[...], left[...], right[...]
    for head in range(heads):
        project_grad[:, head_columns(head, 1)] = turn(dk[head] * scale, tables, -1.0).astype(BF)
        project_grad[:, head_columns(head, 2)] = dv[head].astype(BF)


def mixed_kernel(pack_count, pack_table, down_table, *refs):
    attended, hidden, *shards = refs[:-5]
    pack_shards, down_shards = shards[:pack_count], shards[pack_count:]
    out, output_whole, down_whole, output_sems, down_sems = refs[-5:]

    @pl.when(pl.program_id(0) == 0)
    def _():
        width = pack_shards[0].shape[1]
        columns = pl.ds(width - output_whole.shape[1], output_whole.shape[1])
        load_shards(pack_shards, pack_table, output_whole, output_sems, 0, columns)
        load_shards(down_shards, down_table, down_whole, down_sems, 0)

    out[...] = (
        lax.dot_general(attended[...], output_whole[...], LAST, preferred_element_type=F32)
        + lax.dot_general(hidden[...], down_whole[...], LAST, preferred_element_type=F32)
    ).astype(BF)


def hidden_grad_kernel(table, *refs):
    grad, slope, *shards = refs[:-3]
    out, whole, sems = refs[-3:]

    @pl.when(pl.program_id(0) == 0)
    def _():
        load_shards(shards, table, whole, sems, 0)

    hidden_grad = jnp.dot(grad[...], whole[...], preferred_element_type=F32)
    out[...] = (hidden_grad * slope[...]).astype(BF)


def weight_grad_kernel(count, pairs, *refs):
    lefts_rights, outs = refs[: 2 * pairs], refs[2 * pairs :]
    for step in range(count):

        @pl.when(pl.program_id(0) == step)
        def _():
            begin = 0
            for pair in range(pairs):
                left, right = lefts_rights[2 * pair], lefts_rights[2 * pair + 1]
                made = lax.dot_general(left[...], right[...], FIRST, preferred_element_type=F32)
                width = made.shape[1]
                outs[step][:, begin : begin + width] = made.astype(outs[step].dtype)
                begin += width


def back_kernel(pack_count, pack_table, up_table, *refs):
    act, params, project, expand, *shards = refs[:-8]
    project_shards, up_shards = shards[:pack_count], shards[pack_count:]
    out, gains, project_bias, up_bias, project_whole, up_whole, project_sems, up_sems = refs[-8:]

    @pl.when(pl.program_id(0) == 0)
    def _():
        columns = pl.ds(0, project_whole.shape[1])
        load_shards(project_shards, pack_table, project_whole, project_sems, 0, columns)
        load_shards(up_shards, up_table, up_whole, up_sems, 0)
        gains[...] = jnp.zeros_like(gains)
        project_bias[...] = jnp.zeros_like(project_bias)
        up_bias[...] = jnp.zeros_like(up_bias)

    normed, inverse_scale = normalize(act[...])
    first = lax.dot_general(project[...], project_whole[...], LAST, preferred_element_type=F32)
    second = lax.dot_general(expand[...], up_whole[...], LAST, preferred_element_type=F32)
    gains[0:1, :] += jnp.sum(first * normed, axis=0, keepdims=True)
    gains[1:2, :] += jnp.sum(first, axis=0, keepdims=True)
    gains[2:3, :] += jnp.sum(second * normed, axis=0, keepdims=True)
    gains[3:4, :] += jnp.sum(second, axis=0, keepdims=True)
    project_bias[...] += jnp.sum(project[...].astype(F32), axis=0, keepdims=True)
    up_bias[...] += jnp.sum(expand[...].astype(F32), axis=0, keepdims=True)
    normed_grad = first * params[0:1, :] + second * params[2:3, :]
    mean_grad = jnp.mean(normed_grad, axis=1, keepdims=True)
    mean_product = jnp.mean(normed_grad * normed, axis=1, keepdims=True)
    out[...] = (inverse_scale * (normed_grad - mean_grad - normed * mean_product)).astype(BF)


def tile_spec(width, tile=TILE):
    return pl.BlockSpec((tile, width), lambda i: (i, 0))


def fixed_spec(shape):
    return pl.BlockSpec(shape, lambda i: (0, 0))


ANY = pl.BlockSpec(memory_space=pl.ANY)


def shape_of(shape, kind):
    return jax.ShapeDtypeStruct(shape, kind)


def cost(flops, moved=0):
    return pl.CostEstimate(flops=int(flops), bytes_accessed=int(moved), transcendentals=0)


def call(kernel, name, tokens, ins, outs, wholes, args, moved=0, tile=TILE):
    scratch = [pltpu.VMEM(shape, BF) for shape, _ in wholes] + [
        pltpu.SemaphoreType.DMA((count,)) for _, count in wholes
    ]
    return pl.pallas_call(
        kernel,
        name=name,
        grid=(tokens // tile,),
        in_specs=ins,
        out_specs=[spec for spec, _ in outs],
        out_shape=[shape for _, shape in outs],
        scratch_shapes=scratch,
        compiler_params=pltpu.CompilerParams(
            dimension_semantics=("arbitrary",), vmem_limit_bytes=VMEM_LIMIT
        ),
        cost_estimate=cost(sum(2 * tokens * shape[0] * shape[1] for shape, _ in wholes), moved),
    )(*args)


def weight_grad(count, place, pairs, chunked_right=False):
    specs, arrays, width = [], [], 0
    for left, right in pairs:
        chunked, fixed = (right, left) if chunked_right else (left, right)
        extent = chunked.shape[1] // count
        chunk_spec = pl.BlockSpec(
            (chunked.shape[0], extent), lambda i, spot: (0, lax.rem(spot[0] + i, count))
        )
        fixed_spec_ = pl.BlockSpec(fixed.shape, lambda i, spot: (0, 0))
        specs += [fixed_spec_, chunk_spec] if chunked_right else [chunk_spec, fixed_spec_]
        arrays += [left, right]
        rows, columns = (fixed.shape[1], extent) if chunked_right else (extent, fixed.shape[1])
        width += columns
    shape = (rows, width)
    return pl.pallas_call(
        functools.partial(drop_first, functools.partial(weight_grad_kernel, count, len(pairs))),
        name="weight_grad",
        grid_spec=pltpu.PrefetchScalarGridSpec(
            num_scalar_prefetch=1,
            grid=(count,),
            in_specs=specs,
            out_specs=[pl.BlockSpec(shape, lambda i, spot: (0, 0))] * count,
        ),
        out_shape=[shape_of(shape, F32 if r == 0 else BF) for r in range(count)],
        compiler_params=pltpu.CompilerParams(
            dimension_semantics=("arbitrary",), vmem_limit_bytes=VMEM_LIMIT
        ),
        cost_estimate=cost(2 * arrays[0].shape[0] * rows * width * count),
    )(place[None], *arrays)


def drop_first(kernel, spot, *refs):
    kernel(*refs)


def angle_tables(row_total):
    positions = (jnp.arange(row_total, dtype=jnp.int32) % LENGTH).astype(F32)
    frequency = ROPE_BASE ** (-jnp.arange(0, ROTARY, 2, dtype=jnp.int32).astype(F32) / ROTARY)
    turning = positions[:, None] * frequency[None, :]
    cosine, sine = jnp.cos(turning), jnp.sin(turning)
    rest = HEAD_DIM - ROTARY
    zeros = jnp.zeros_like(sine)
    return (
        jnp.concatenate([cosine, cosine, jnp.ones((row_total, rest), F32)], axis=1),
        jnp.concatenate([-sine, zeros, jnp.zeros((row_total, rest), F32)], axis=1),
        jnp.concatenate([zeros, sine, jnp.zeros((row_total, rest), F32)], axis=1),
    )


def on_device(
    rows,
    cols,
    activations,
    document_ids,
    attention_gain,
    attention_shift,
    feedforward_gain,
    feedforward_shift,
    query_key_value,
    query_key_value_bias,
    output_weight,
    output_bias,
    up_weight,
    up_bias,
    down_weight,
    down_bias,
    out_grad,
):
    row_place, col_place = lax.axis_index("row"), lax.axis_index("col")
    tokens, features = activations.shape
    heads = query_key_value.shape[1]
    project_width, out_width = heads * 3 * HEAD_DIM, heads * HEAD_DIM
    hidden_width = up_weight.shape[1]

    full_input = lax.all_gather(activations, "row", axis=1, tiled=True)
    full_grad = lax.all_gather(out_grad, "row", axis=1, tiled=True)

    pack = jnp.concatenate(
        [query_key_value.astype(BF).reshape(-1, project_width), output_weight.astype(BF).T], axis=1
    )
    pack_gather = RingGather(pack, cols)
    up_gather = RingGather(up_weight.astype(BF), cols)
    down_shard = down_weight.astype(BF).T
    both = LineBoth(down_shard, col_place) if cols == 4 else None
    down_gather = both or RingGather(down_shard, cols)

    def slot(transfers, gate, *works):
        moved = []
        for transfer in transfers:
            moved += transfer.step(gate)
        made = [work(gate) for work in works]
        return moved + [array for arrays in made for array in arrays], made

    def more(transfers, gate):
        for _ in range(cols - 4):
            gate, _ = slot(transfers, gate)
        return gate

    def tables_work(gate):
        cosine, left, right = angle_tables(tokens)
        starts = jnp.sum(
            (document_ids[:, None] < document_ids[None, :]).astype(jnp.int32), axis=0
        )
        return cosine, left, right, starts, jnp.sum(out_grad.astype(F32), axis=0)

    def params_work(gate):
        stacked = jnp.stack(
            [attention_gain, attention_shift, feedforward_gain, feedforward_shift]
        )
        return [lax.all_gather(after(stacked, gate), "row", axis=1, tiled=True)]

    def norm_work(gate):
        return call(
            norm_kernel,
            "norm",
            tokens,
            [tile_spec(D), fixed_spec((4, D))],
            [
                (tile_spec(D), shape_of((tokens, D), BF)),
                (tile_spec(D), shape_of((tokens, D), BF)),
            ],
            [],
            [full_input, after(norm_params, gate)],
            6 * tokens * D,
        )

    gate, ((cosine, left, right, starts, shift_out_grad),) = slot([pack_gather], [], tables_work)
    low_blocks = starts[::QUERY_BLOCK] // KEY_BLOCK
    gate, ((norm_params,),) = slot([pack_gather], gate, params_work)
    gate = more([pack_gather], gate)
    gate, ((first_norm, second_norm),) = slot([pack_gather], gate, norm_work)
    pack_shards, pack_table = pack_gather.shards()

    def project_work(gate):
        return call(
            functools.partial(project_kernel, pack_table, heads),
            "project",
            tokens,
            [tile_spec(D), fixed_spec((1, project_width))]
            + [tile_spec(HEAD_DIM)] * 3
            + [ANY] * len(pack_shards),
            [(tile_spec(project_width), shape_of((tokens, project_width), BF))],
            [((D, project_width), cols)],
            [
                after(first_norm, gate),
                query_key_value_bias.reshape(1, -1),
                cosine,
                left,
                right,
                *pack_shards,
            ],
        )

    def attended_grad_work(gate):
        return call(
            functools.partial(attended_grad_kernel, pack_table),
            "attended_grad",
            tokens,
            [tile_spec(D, 4 * TILE)] + [ANY] * len(pack_shards),
            [(tile_spec(out_width, 4 * TILE), shape_of((tokens, out_width), BF))],
            [((D, out_width), cols)],
            [after(full_grad, gate), *pack_shards],
            tile=4 * TILE,
        )

    def whole_spec(*shape):
        return pl.BlockSpec(shape, lambda i: (0, 0))

    head_rows = whole_spec(heads, tokens), shape_of((heads, tokens), F32)
    head_entries = whole_spec(out_width, tokens), shape_of((out_width, tokens), F32)

    def attention_work(gate):
        return pl.pallas_call(
            functools.partial(attention_kernel, heads),
            name="attention",
            grid=(1,),
            in_specs=[
                pl.BlockSpec(memory_space=pltpu.SMEM),
                whole_spec(1, tokens),
                whole_spec(tokens, project_width),
            ],
            out_specs=[whole_spec(tokens, out_width), head_entries[0], head_rows[0]],
            out_shape=[shape_of((tokens, out_width), BF), head_entries[1], head_rows[1]],
            scratch_shapes=[pltpu.VMEM((heads, HEAD_DIM, tokens), BF)],
            compiler_params=pltpu.CompilerParams(vmem_limit_bytes=VMEM_LIMIT),
            cost_estimate=cost(8 * tokens * tokens * out_width),
        )(low_blocks, starts[None], after(projected, gate))

    def attention_back_work(gate):
        return pl.pallas_call(
            functools.partial(attention_back_kernel, heads),
            name="attention_back",
            grid=(1,),
            in_specs=[
                pl.BlockSpec(memory_space=pltpu.SMEM),
                whole_spec(1, tokens),
                *[whole_spec(tokens, HEAD_DIM)] * 3,
                whole_spec(tokens, project_width),
                whole_spec(tokens, out_width),
                head_entries[0],
                head_rows[0],
            ],
            out_specs=[whole_spec(tokens, project_width)],
            out_shape=[shape_of((tokens, project_width), BF)],
            scratch_shapes=[pltpu.VMEM((heads, HEAD_DIM, tokens), BF)]
            + [pltpu.VMEM((heads, tokens, HEAD_DIM), F32)] * 2,
            compiler_params=pltpu.CompilerParams(vmem_limit_bytes=VMEM_LIMIT),
            cost_estimate=cost(16 * tokens * tokens * out_width),
        )(
            low_blocks,
            starts[None],
            cosine,
            left,
            right,
            projected,
            after(attended_grad, gate),
            produced_t,
            log_total,
        )

    gate, ((projected,),) = slot([up_gather], gate, project_work)

    def attention_grad_work(gate):
        made = attention_work(gate)
        return *made, *attended_grad_work(gate + [made[2]])

    gate, ((attended, produced_t, log_total, attended_grad),) = slot(
        [up_gather], gate, attention_grad_work
    )
    gate = more([up_gather], gate)
    gate, ((project_grad,),) = slot([up_gather], gate, attention_back_work)
    up_shards, up_table = up_gather.shards()

    def pack_weight_work(gate):
        return weight_grad(
            cols, col_place, [(first_norm, after(project_grad, gate)), (full_grad, attended)]
        )

    def up_work(gate):
        return call(
            functools.partial(up_kernel, up_table),
            "up",
            tokens,
            [tile_spec(D), fixed_spec((1, hidden_width))] + [ANY] * len(up_shards),
            [
                (tile_spec(hidden_width), shape_of((tokens, hidden_width), BF)),
                (tile_spec(hidden_width), shape_of((tokens, hidden_width), F32)),
            ],
            [((D, hidden_width), cols)],
            [after(second_norm, gate), up_bias[None], *up_shards],
        )

    def down_weight_work(gate):
        return weight_grad(cols, col_place, [(after(hidden, gate), full_grad)], True)

    gate, (pack_chunks,) = slot([down_gather], gate, pack_weight_work)
    gate = more([down_gather], gate)
    if both is not None:
        both.chunks = pack_chunks
    gate, ((hidden, slope),) = slot([down_gather], gate, up_work)
    gate, (down_chunks,) = slot([down_gather], gate, down_weight_work)
    down_shards, down_table = down_gather.shards()
    pack_scatter = both or RingScatter(pack_chunks, cols)
    down_scatter = RingScatter(down_chunks, cols)
    if both is None:
        for _ in range(cols - 2):
            gate, _ = slot([pack_scatter], gate)

    def mixed_work(gate):
        return call(
            functools.partial(mixed_kernel, len(pack_shards), pack_table, down_table),
            "mixed",
            tokens,
            [tile_spec(out_width), tile_spec(hidden_width)] + [ANY] * (len(pack_shards) + len(down_shards)),
            [(tile_spec(D), shape_of((tokens, D), BF))],
            [((D, out_width), cols), ((D, hidden_width), cols)],
            [after(attended, gate), hidden, *pack_shards, *down_shards],
        )

    def hidden_grad_work(gate):
        return call(
            functools.partial(hidden_grad_kernel, down_table),
            "hidden_grad",
            tokens,
            [tile_spec(D), tile_spec(hidden_width)] + [ANY] * len(down_shards),
            [(tile_spec(hidden_width), shape_of((tokens, hidden_width), BF))],
            [((D, hidden_width), cols)],
            [after(full_grad, gate), slope, *down_shards],
        )

    def back_work(gate):
        return call(
            functools.partial(back_kernel, len(pack_shards), pack_table, up_table),
            "back",
            tokens,
            [tile_spec(D), fixed_spec((4, D)), tile_spec(project_width), tile_spec(hidden_width)]
            + [ANY] * (len(pack_shards) + len(up_shards)),
            [
                (tile_spec(D), shape_of((tokens, D), BF)),
                (fixed_spec((4, D)), shape_of((4, D), F32)),
                (fixed_spec((1, project_width)), shape_of((1, project_width), F32)),
                (fixed_spec((1, hidden_width)), shape_of((1, hidden_width), F32)),
            ],
            [((D, project_width), cols), ((D, hidden_width), cols)],
            [
                full_input,
                norm_params,
                project_grad,
                after(expand_grad, gate),
                *pack_shards,
                *up_shards,
            ],
        )

    def up_weight_work(gate):
        return weight_grad(cols, col_place, [(second_norm, after(expand_grad, gate))])

    def pack_result_work(gate):
        return [pack_scatter.result()]

    def down_result_work(gate):
        return [down_scatter.result()]

    def layer_out_work(gate):
        return [
            activations.astype(F32) + after(mixed_sum, gate).astype(F32) + output_bias + down_bias
        ]

    gate, ((mixed_part,),) = slot([pack_scatter], gate, mixed_work)
    mixed_sum = lax.psum_scatter(after(mixed_part, gate), "row", scatter_dimension=1, tiled=True)
    gate, ((expand_grad,), (pack_weight_grad,)) = slot(
        [down_scatter], gate, hidden_grad_work, pack_result_work
    )
    project_weight_grad = pack_weight_grad[:, :project_width].reshape(query_key_value.shape)
    output_weight_grad = pack_weight_grad[:, project_width:].T
    gate = more([down_scatter], gate)
    gate, ((back_part, gains, project_bias_grad, up_bias_grad),) = slot(
        [down_scatter], gate, back_work
    )
    back_sum = lax.psum_scatter(after(back_part, gate), "row", scatter_dimension=1, tiled=True)
    gate, (up_chunks,) = slot([down_scatter], gate, up_weight_work)
    up_scatter = RingScatter(up_chunks, cols)

    def gains_work(gate):
        terms = after(gains, gate).reshape(4, rows, features).transpose(1, 0, 2).reshape(rows, -1)
        return [pair_scatter(terms, "row", rows, row_place)]

    def small_work(gate):
        small = [after(gain_terms, gate), project_bias_grad[0], up_bias_grad[0], shift_out_grad]
        return [pair_sum(jnp.concatenate(small), "col", cols)]

    gate, ((gain_terms,), (down_weight_grad,)) = slot(
        [up_scatter], gate, gains_work, down_result_work
    )
    gate = more([up_scatter], gate)
    gate, _ = slot([up_scatter], gate)
    up_scatter.step(gate)
    (small,) = small_work(gate)
    (layer_out,) = layer_out_work(gate)
    up_weight_grad = up_scatter.result()
    grad_float = out_grad.astype(F32)
    activations_grad = grad_float + back_sum.astype(F32)

    sizes = [features] * 4 + [project_width, hidden_width, features]
    pieces, begin = [], 0
    for size in sizes:
        pieces.append(small[begin : begin + size])
        begin += size
    return (
        layer_out,
        activations_grad,
        pieces[0],
        pieces[1],
        pieces[2],
        pieces[3],
        project_weight_grad,
        pieces[4].reshape(query_key_value_bias.shape),
        output_weight_grad,
        pieces[6],
        up_weight_grad,
        pieces[5],
        down_weight_grad,
        pieces[6],
    )


def solution(mesh):
    placed = (
        P("col", "row"),
        P("col"),
        P("row"),
        P("row"),
        P("row"),
        P("row"),
        P("col", "row", None),
        P("row", None),
        P("row", "col"),
        P("row"),
        P("col", "row"),
        P("row"),
        P("row", "col"),
        P("row"),
        P("col", "row"),
    )

    def body(*args):
        return on_device(mesh.shape["row"], mesh.shape["col"], *args)

    return jax.shard_map(
        body,
        mesh=mesh,
        in_specs=placed,
        out_specs=(
            P("col", "row"),
            P("col", "row"),
            P("row"),
            P("row"),
            P("row"),
            P("row"),
            P("col", "row", None),
            P("row", None),
            P("row", "col"),
            P("row"),
            P("col", "row"),
            P("row"),
            P("row", "col"),
            P("row"),
        ),
        check_vma=False,
    )
```

```python
import functools

import jax
import jax.numpy as jnp
from jax import lax
from jax.experimental import pallas as pl
from jax.experimental.pallas import tpu as pltpu
from jax.sharding import PartitionSpec as P

D = 2048
HEAD_DIM = 128
ROTARY = 32
LENGTH = 2048

EPSILON = 1e-05
MASKED = -1e30
ROPE_BASE = 10000.0
BF = jnp.bfloat16
F32 = jnp.float32
LAST = (((1,), (1,)), ((), ()))
FIRST = (((0,), (0,)), ((), ()))
TILE = 256
QUERY_BLOCK = 512
KEY_BLOCK = 512
VMEM_LIMIT = 56 * 1024 * 1024
LOG2_E = 1.4426950408889634
SQRT_HALF = 0.7071067811865476
INV_SQRT_2PI = 0.3989422804014327


def after(value, gate):
    return lax.optimization_barrier((value,) + tuple(gate))[0] if gate else value


class RingGather:
    def __init__(self, shard, count):
        self.count, self.arrays = count, [shard]

    def step(self, gate):
        count = self.count
        pairs = [(k, (k + 1) % count) for k in range(count)]
        self.arrays = self.arrays + [lax.ppermute(after(self.arrays[-1], gate), "col", pairs)]
        return self.arrays[-1:]

    def shards(self):
        count = self.count
        return self.arrays, [[(i - j) % count for j in range(count)] for i in range(count)]


class RingScatter:
    def __init__(self, chunks, count):
        self.chunks, self.count = chunks, count
        self.moving, self.done = None, 0

    def step(self, gate):
        self.done += 1
        count = self.count
        sent = after(self.chunks[count - self.done], gate)
        if self.moving is not None:
            sent = (sent.astype(F32) + self.moving.astype(F32)).astype(BF)
        pairs = [(k, (k + 1) % count) for k in range(count)]
        self.sent = sent
        self.moving = lax.ppermute(self.sent, "col", pairs)
        return [self.moving]

    def result(self, gate):
        return after(self.chunks[0], gate) + self.moving.astype(F32)


class LineBoth:
    def __init__(self, shard, place):
        self.shard, self.place = shard, place
        self.upward, self.downward = [shard], [shard]

    def step(self, gate):
        place, done = self.place, len(self.upward)
        up, down = self.upward[-1], self.downward[-1]
        if done == 2:
            up = jnp.where(place == 0, self.chunks[3], up)
            down = jnp.where(place == 3, self.chunks[1], down)
        elif done == 3:
            up = jnp.where(place == 2, up, self.add(2, up))
            down = jnp.where(place == 1, down, self.add(2, down))
        elif done == 4:
            up, down = self.add(1, up), self.add(3, down)
        up, down = after(up, gate), after(down, gate)
        self.upward.append(lax.ppermute(up, "col", [(0, 1), (1, 2), (2, 3)]))
        self.downward.append(lax.ppermute(down, "col", [(3, 2), (2, 1), (1, 0)]))
        return [self.upward[-1], self.downward[-1]]

    def add(self, at, array):
        return (self.chunks[at].astype(F32) + array.astype(F32)).astype(BF)

    def shards(self):
        table = [[0 if j == i else i - j if j < i else 3 + j - i for j in range(4)] for i in range(4)]
        return self.upward[:4] + self.downward[1:4], table

    def result(self, gate):
        return after(self.chunks[0], gate) + (self.upward[4].astype(F32) + self.downward[4].astype(F32))


class RowScatter:
    KEPT, SENT = [0, 2, 4, 6], [1, 3, 5, 7]

    def __init__(self, kept, sent):
        self.kept, self.sent, self.done = kept, sent, 0
        self.width, self.parts = kept.shape[1] // 4, []

    def send(self, array, mask, gate):
        self.parts.append(after(array, gate))
        return lax.ppermute(self.parts[-1], "row", [(k, k ^ mask) for k in range(8)])

    def piece(self, at):
        columns = slice(at * self.width, (at + 1) * self.width)
        return self.kept[:, columns].astype(F32) + self.core[:, columns].astype(F32)

    def step(self, gate):
        self.done += 1
        half = self.kept.shape[0] // 2
        if self.done == 1:
            self.core = self.send(self.sent, 1, gate)
            return [self.core]
        if self.done == 2:
            far = self.piece(3).astype(BF)
            self.from_x = self.send(far[:half], 2, gate)
            self.from_y = self.send(far[half:], 4, gate)
        else:
            empty = jnp.zeros_like(self.from_x, F32)
            from_x, from_y = self.from_x.astype(F32), self.from_y.astype(F32)
            for_x = self.piece(1) + jnp.concatenate([empty, from_y])
            for_y = self.piece(2) + jnp.concatenate([from_x, empty])
            self.from_x = self.send(for_x.astype(BF), 2, gate)
            self.from_y = self.send(for_y.astype(BF), 4, gate)
        return [self.from_x, self.from_y]

    def result(self):
        return self.piece(0) + self.from_x.astype(F32) + self.from_y.astype(F32)


def pair_sum(value, axis, count, masks, gate):
    for mask in masks:
        value = value + pair_exchange(value, axis, count, mask, gate)
    return value


def pair_exchange(value, axis, count, mask, gate):
    return lax.ppermute(after(value, gate), axis, [(k, k ^ mask) for k in range(count)])


def pair_scatter(value, axis, count, place):
    mask = count // 2
    while mask:
        upper = lax.rem(place // mask, 2) == 1
        low, high = value[:mask], value[mask:]
        kept, sent = jnp.where(upper, high, low), jnp.where(upper, low, high)
        value = kept + lax.ppermute(sent, axis, [(k, k ^ mask) for k in range(count)])
        mask //= 2
    return value[0]


def load_shards(refs, table, whole, sems, dim, columns=None):
    if columns is not None:
        refs = [ref.at[:, columns] for ref in refs]
    count = len(table)
    extent = refs[0].shape[dim]
    place = lax.axis_index("col")

    def spot(j):
        at = pl.ds(j * extent, extent)
        return whole.at[at, :] if dim == 0 else whole.at[:, at]

    for i in range(count):

        @pl.when(place == i)
        def _():
            for j in range(count):
                pltpu.make_async_copy(refs[table[i][j]], spot(j), sems.at[j]).start()

    for j in range(count):
        pltpu.make_async_copy(refs[0], spot(j), sems.at[j]).wait()


def normalize(tile):
    values = tile.astype(F32)
    centered = values - jnp.mean(values, axis=1, keepdims=True)
    inverse_scale = lax.rsqrt(jnp.mean(centered * centered, axis=1, keepdims=True) + EPSILON)
    return centered * inverse_scale, inverse_scale


def norm_kernel(act, params, first_out, second_out):
    normed, _ = normalize(act[...])
    first_out[...] = (normed * params[0:1, :] + params[1:2, :]).astype(BF)
    second_out[...] = (normed * params[2:3, :] + params[3:4, :]).astype(BF)


def up_kernel(table, *refs):
    norm, bias, *shards = refs[:-4]
    hidden_out, slope_out, whole, sems = refs[-4:]

    @pl.when(pl.program_id(0) == 0)
    def _():
        load_shards(shards, table, whole, sems, 0)

    lin = jnp.dot(norm[...], whole[...], preferred_element_type=F32) + bias[...]
    cdf = 0.5 + 0.5 * lax.erf(lin * SQRT_HALF)
    hidden_out[...] = (lin * cdf).astype(BF)
    slope_out[...] = cdf + lin * (INV_SQRT_2PI * jnp.exp(-0.5 * lin * lin))


def turn(values, tables, sign):
    cosine, left, right = tables
    half = ROTARY // 2
    turned = left * pltpu.roll(values, HEAD_DIM - half, 1) + right * pltpu.roll(values, half, 1)
    return values * cosine + sign * turned


def project_kernel(table, heads, *refs):
    norm, bias, cosine, left, right, *shards = refs[:-3]
    out, whole, sems = refs[-3:]

    @pl.when(pl.program_id(0) == 0)
    def _():
        load_shards(shards, table, whole, sems, 0, pl.ds(0, whole.shape[1]))

    lin = jnp.dot(norm[...], whole[...], preferred_element_type=F32) + bias[...]
    tables = cosine[...], left[...], right[...]
    for head in range(heads):
        for part in range(3):
            at = slice((head * 3 + part) * HEAD_DIM, (head * 3 + part + 1) * HEAD_DIM)
            piece = lin[:, at]
            out[:, at] = (turn(piece, tables, 1.0) if part < 2 else piece).astype(BF)


def attended_grad_kernel(table, *refs):
    grad, *shards = refs[:-3]
    out, whole, sems = refs[-3:]

    @pl.when(pl.program_id(0) == 0)
    def _():
        columns = pl.ds(shards[0].shape[1] - whole.shape[1], whole.shape[1])
        load_shards(shards, table, whole, sems, 0, columns)

    out[...] = jnp.dot(grad[...], whole[...], preferred_element_type=F32).astype(BF)


def head_columns(head, part):
    return slice((3 * head + part) * HEAD_DIM, (3 * head + part + 1) * HEAD_DIM)


def own_columns(head):
    return slice(head * HEAD_DIM, (head + 1) * HEAD_DIM)


def rows_of(block, extent):
    return pl.ds(pl.multiple_of(block * extent, extent), extent)


def allowed_scores(project, start, block, at, head):
    rows, keys = rows_of(block, QUERY_BLOCK), rows_of(at, KEY_BLOCK)
    scores = lax.dot_general(
        project[keys, head_columns(head, 1)],
        project[rows, head_columns(head, 0)],
        LAST,
        preferred_element_type=F32,
    ) * (HEAD_DIM**-0.5 * LOG2_E)
    place = block * QUERY_BLOCK + lax.broadcasted_iota(jnp.int32, (1, QUERY_BLOCK), 1)
    key_place = at * KEY_BLOCK + lax.broadcasted_iota(jnp.int32, (KEY_BLOCK, QUERY_BLOCK), 0)
    allowed = (key_place >= start[:, rows]) & (key_place <= place)
    return jnp.where(allowed, scores, MASKED)


def attention_kernel(heads, low, start, project, out, produced_t, log_total, v_t):
    length = project.shape[0]
    for head in range(heads):
        v_t[head] = project[:, head_columns(head, 2)].T

    def query_block(block, _):
        rows = rows_of(block, QUERY_BLOCK)

        def forward(at, carry):
            keys, made = rows_of(at, KEY_BLOCK), []
            for head in range(heads):
                largest, total, produced = carry[head]
                scores = allowed_scores(project, start, block, at, head)
                newest = jnp.maximum(largest, jnp.max(scores, axis=0, keepdims=True))
                shrink = jnp.exp2(largest - newest)
                parts = jnp.exp2(scores - newest)
                total = total * shrink + jnp.sum(parts, axis=0, keepdims=True)
                produced = produced * shrink + jnp.dot(
                    v_t[head, :, keys], parts.astype(BF), preferred_element_type=F32
                )
                made.append((newest, total, produced))
            return tuple(made)

        empty = jnp.zeros((1, QUERY_BLOCK), F32)
        wide = jnp.zeros((HEAD_DIM, QUERY_BLOCK), F32)
        last_block = (block + 1) * (QUERY_BLOCK // KEY_BLOCK)
        carry = lax.fori_loop(
            low[block], last_block, forward, ((empty + MASKED, empty, wide),) * heads
        )
        for head in range(heads):
            largest, total, produced = carry[head]
            produced = produced * (1.0 / total)
            out[rows, own_columns(head)] = produced.T.astype(BF)
            produced_t[own_columns(head), rows] = produced
            log_total[head : head + 1, rows] = largest + jnp.log2(total)
        return 0

    lax.fori_loop(0, length // QUERY_BLOCK, query_block, 0)


def attention_back_kernel(
    heads,
    low,
    start,
    cosine,
    left,
    right,
    project,
    grad,
    produced_t,
    log_total,
    project_grad,
    k_t,
    dk,
    dv,
):
    length = project.shape[0]
    scale = HEAD_DIM**-0.5
    for head in range(heads):
        k_t[head] = project[:, head_columns(head, 1)].T
    dk[...] = jnp.zeros_like(dk)
    dv[...] = jnp.zeros_like(dv)

    def query_block(block, _):
        rows = rows_of(block, QUERY_BLOCK)
        deltas = [
            jnp.sum(
                produced_t[own_columns(head), rows] * grad[rows, own_columns(head)].astype(F32).T,
                axis=0,
                keepdims=True,
            )
            for head in range(heads)
        ]

        def backward(at, query_grads):
            keys, made = rows_of(at, KEY_BLOCK), []
            for head in range(heads):
                scores = allowed_scores(project, start, block, at, head)
                prob_grad = lax.dot_general(
                    project[keys, head_columns(head, 2)],
                    grad[rows, own_columns(head)],
                    LAST,
                    preferred_element_type=F32,
                )
                probs = jnp.exp2(scores - log_total[head : head + 1, rows])
                score_grad = (probs * (prob_grad - deltas[head])).astype(BF)
                dv[head, keys, :] += jnp.dot(
                    probs.astype(BF), grad[rows, own_columns(head)], preferred_element_type=F32
                )
                dk[head, keys, :] += jnp.dot(
                    score_grad, project[rows, head_columns(head, 0)], preferred_element_type=F32
                )
                made.append(
                    query_grads[head]
                    + jnp.dot(k_t[head, :, keys], score_grad, preferred_element_type=F32)
                )
            return tuple(made)

        wide = jnp.zeros((HEAD_DIM, QUERY_BLOCK), F32)
        last_block = (block + 1) * (QUERY_BLOCK // KEY_BLOCK)
        query_grads = lax.fori_loop(low[block], last_block, backward, (wide,) * heads)
        tables = cosine[rows, :], left[rows, :], right[rows, :]
        for head in range(heads):
            project_grad[rows, head_columns(head, 0)] = turn(
                (query_grads[head] * scale).T, tables, -1.0
            ).astype(BF)
        return 0

    lax.fori_loop(0, length // QUERY_BLOCK, query_block, 0)
    tables = cosine[...], left[...], right[...]
    for head in range(heads):
        project_grad[:, head_columns(head, 1)] = turn(dk[head] * scale, tables, -1.0).astype(BF)
        project_grad[:, head_columns(head, 2)] = dv[head].astype(BF)


def mixed_kernel(pack_count, pack_table, down_table, *refs):
    attended, hidden, *shards = refs[:-5]
    pack_shards, down_shards = shards[:pack_count], shards[pack_count:]
    out, output_whole, down_whole, output_sems, down_sems = refs[-5:]

    @pl.when(pl.program_id(0) == 0)
    def _():
        width = pack_shards[0].shape[1]
        columns = pl.ds(width - output_whole.shape[1], output_whole.shape[1])
        load_shards(pack_shards, pack_table, output_whole, output_sems, 0, columns)
        load_shards(down_shards, down_table, down_whole, down_sems, 0)

    out[...] = (
        lax.dot_general(attended[...], output_whole[...], LAST, preferred_element_type=F32)
        + lax.dot_general(hidden[...], down_whole[...], LAST, preferred_element_type=F32)
    ).astype(BF)


def hidden_grad_kernel(table, *refs):
    grad, slope, *shards = refs[:-3]
    out, whole, sems = refs[-3:]

    @pl.when(pl.program_id(0) == 0)
    def _():
        load_shards(shards, table, whole, sems, 0)

    hidden_grad = jnp.dot(grad[...], whole[...], preferred_element_type=F32)
    out[...] = (hidden_grad * slope[...]).astype(BF)


def weight_grad_kernel(count, pairs, *refs):
    lefts_rights, outs = refs[: 2 * pairs], refs[2 * pairs :]
    for step in range(count):

        @pl.when(pl.program_id(0) == step)
        def _():
            begin = 0
            for pair in range(pairs):
                left, right = lefts_rights[2 * pair], lefts_rights[2 * pair + 1]
                made = lax.dot_general(left[...], right[...], FIRST, preferred_element_type=F32)
                width = made.shape[1]
                outs[step][:, begin : begin + width] = made.astype(outs[step].dtype)
                begin += width


def back_kernel(pack_count, pack_table, up_table, pieces, *refs):
    act, params, project, expand, *shards = refs[: -8 - len(pieces)]
    project_shards, up_shards = shards[:pack_count], shards[pack_count:]
    outs = refs[-8 - len(pieces) : -8]
    gains, project_bias, up_bias, project_whole, up_whole, project_sems, up_sems, tile = refs[-8:]

    @pl.when(pl.program_id(0) == 0)
    def _():
        columns = pl.ds(0, project_whole.shape[1])
        load_shards(project_shards, pack_table, project_whole, project_sems, 0, columns)
        load_shards(up_shards, up_table, up_whole, up_sems, 0)
        gains[...] = jnp.zeros_like(gains)
        project_bias[...] = jnp.zeros_like(project_bias)
        up_bias[...] = jnp.zeros_like(up_bias)

    normed, inverse_scale = normalize(act[...])
    first = lax.dot_general(project[...], project_whole[...], LAST, preferred_element_type=F32)
    second = lax.dot_general(expand[...], up_whole[...], LAST, preferred_element_type=F32)
    gains[0:1, :] += jnp.sum(first * normed, axis=0, keepdims=True)
    gains[1:2, :] += jnp.sum(first, axis=0, keepdims=True)
    gains[2:3, :] += jnp.sum(second * normed, axis=0, keepdims=True)
    gains[3:4, :] += jnp.sum(second, axis=0, keepdims=True)
    project_bias[...] += jnp.sum(project[...].astype(F32), axis=0, keepdims=True)
    up_bias[...] += jnp.sum(expand[...].astype(F32), axis=0, keepdims=True)
    normed_grad = first * params[0:1, :] + second * params[2:3, :]
    mean_grad = jnp.mean(normed_grad, axis=1, keepdims=True)
    mean_product = jnp.mean(normed_grad * normed, axis=1, keepdims=True)
    result = (inverse_scale * (normed_grad - mean_grad - normed * mean_product)).astype(BF)
    if pieces == [None]:
        outs[0][...] = result
        return
    tile[...] = result
    place, width = lax.axis_index("row"), tile.shape[1] // 8
    for out, masks in zip(outs, pieces):
        for at, mask in enumerate(masks):
            source = pl.ds(pl.multiple_of((place ^ mask) * width, width), width)
            out[:, at * width : (at + 1) * width] = tile[:, source]


def tile_spec(width, tile=TILE):
    return pl.BlockSpec((tile, width), lambda i: (i, 0))


def fixed_spec(shape):
    return pl.BlockSpec(shape, lambda i: (0, 0))


ANY = pl.BlockSpec(memory_space=pl.ANY)


def shape_of(shape, kind):
    return jax.ShapeDtypeStruct(shape, kind)


def cost(flops, moved=0):
    return pl.CostEstimate(flops=int(flops), bytes_accessed=int(moved), transcendentals=0)


def call(kernel, name, tokens, ins, outs, wholes, args, moved=0, tile=TILE):
    scratch = [pltpu.VMEM(shape, BF) for shape, _ in wholes] + [
        pltpu.SemaphoreType.DMA((count,)) for _, count in wholes
    ]
    return pl.pallas_call(
        kernel,
        name=name,
        grid=(tokens // tile,),
        in_specs=ins,
        out_specs=[spec for spec, _ in outs],
        out_shape=[shape for _, shape in outs],
        scratch_shapes=scratch,
        compiler_params=pltpu.CompilerParams(
            dimension_semantics=("arbitrary",), vmem_limit_bytes=VMEM_LIMIT
        ),
        cost_estimate=cost(sum(2 * tokens * shape[0] * shape[1] for shape, _ in wholes), moved),
    )(*args)


def weight_grad(count, place, pairs, chunked_right=False):
    specs, arrays, width = [], [], 0
    for left, right in pairs:
        chunked, fixed = (right, left) if chunked_right else (left, right)
        extent = chunked.shape[1] // count
        chunk_spec = pl.BlockSpec(
            (chunked.shape[0], extent), lambda i, spot: (0, lax.rem(spot[0] + i, count))
        )
        fixed_spec_ = pl.BlockSpec(fixed.shape, lambda i, spot: (0, 0))
        specs += [fixed_spec_, chunk_spec] if chunked_right else [chunk_spec, fixed_spec_]
        arrays += [left, right]
        rows, columns = (fixed.shape[1], extent) if chunked_right else (extent, fixed.shape[1])
        width += columns
    shape = (rows, width)
    return pl.pallas_call(
        functools.partial(drop_first, functools.partial(weight_grad_kernel, count, len(pairs))),
        name="weight_grad",
        grid_spec=pltpu.PrefetchScalarGridSpec(
            num_scalar_prefetch=1,
            grid=(count,),
            in_specs=specs,
            out_specs=[pl.BlockSpec(shape, lambda i, spot: (0, 0))] * count,
        ),
        out_shape=[shape_of(shape, F32 if r == 0 else BF) for r in range(count)],
        compiler_params=pltpu.CompilerParams(
            dimension_semantics=("arbitrary",), vmem_limit_bytes=VMEM_LIMIT
        ),
        cost_estimate=cost(2 * arrays[0].shape[0] * rows * width * count),
    )(place[None], *arrays)


def drop_first(kernel, spot, *refs):
    kernel(*refs)


def angle_tables(row_total):
    positions = (jnp.arange(row_total, dtype=jnp.int32) % LENGTH).astype(F32)
    frequency = ROPE_BASE ** (-jnp.arange(0, ROTARY, 2, dtype=jnp.int32).astype(F32) / ROTARY)
    turning = positions[:, None] * frequency[None, :]
    cosine, sine = jnp.cos(turning), jnp.sin(turning)
    rest = HEAD_DIM - ROTARY
    zeros = jnp.zeros_like(sine)
    return (
        jnp.concatenate([cosine, cosine, jnp.ones((row_total, rest), F32)], axis=1),
        jnp.concatenate([-sine, zeros, jnp.zeros((row_total, rest), F32)], axis=1),
        jnp.concatenate([zeros, sine, jnp.zeros((row_total, rest), F32)], axis=1),
    )


def on_device(
    rows,
    cols,
    activations,
    document_ids,
    attention_gain,
    attention_shift,
    feedforward_gain,
    feedforward_shift,
    query_key_value,
    query_key_value_bias,
    output_weight,
    output_bias,
    up_weight,
    up_bias,
    down_weight,
    down_bias,
    out_grad,
):
    row_place, col_place = lax.axis_index("row"), lax.axis_index("col")
    tokens, features = activations.shape
    heads = query_key_value.shape[1]
    project_width, out_width = heads * 3 * HEAD_DIM, heads * HEAD_DIM
    hidden_width = up_weight.shape[1]

    full_input = lax.all_gather(activations, "row", axis=1, tiled=True)
    full_grad = lax.all_gather(out_grad, "row", axis=1, tiled=True)

    pack = jnp.concatenate(
        [query_key_value.astype(BF).reshape(-1, project_width), output_weight.astype(BF).T], axis=1
    )
    pack_gather = RingGather(pack, cols)
    down_shard = down_weight.astype(BF).T
    up_shard = up_weight.astype(BF)
    up_gather = RingGather(up_shard, cols)
    both = LineBoth(down_shard, col_place) if cols == 4 else None
    down_gather = both or RingGather(down_shard, cols)

    def slot(transfers, gate, *works):
        moved = []
        for transfer in transfers:
            moved += transfer.step(gate)
        made = [work(gate) for work in works]
        return moved + [array for arrays in made for array in arrays], made

    def more(transfers, gate):
        for _ in range(cols - 4):
            gate, _ = slot(transfers, gate)
        return gate

    def tables_work(gate):
        cosine, left, right = angle_tables(tokens)
        starts = jnp.sum(
            (document_ids[:, None] < document_ids[None, :]).astype(jnp.int32), axis=0
        )
        sums = jnp.sum(out_grad.astype(F32), axis=0)
        return cosine, left, right, starts, sums, down_shard, up_shard

    def params_work(gate):
        stacked = jnp.stack(
            [attention_gain, attention_shift, feedforward_gain, feedforward_shift]
        )
        return [lax.all_gather(after(stacked, gate), "row", axis=1, tiled=True)]

    def norm_work(gate):
        return call(
            norm_kernel,
            "norm",
            tokens,
            [tile_spec(D), fixed_spec((4, D))],
            [
                (tile_spec(D), shape_of((tokens, D), BF)),
                (tile_spec(D), shape_of((tokens, D), BF)),
            ],
            [],
            [full_input, after(norm_params, gate)],
            6 * tokens * D,
        )

    gate, ((cosine, left, right, starts, shift_out_grad, *_),) = slot([pack_gather], [], tables_work)
    low_blocks = starts[::QUERY_BLOCK] // KEY_BLOCK
    gate, ((norm_params,),) = slot([pack_gather], gate, params_work)
    gate = more([pack_gather], gate)
    gate, ((first_norm, second_norm),) = slot([pack_gather], gate, norm_work)
    pack_shards, pack_table = pack_gather.shards()

    def project_work(gate):
        return call(
            functools.partial(project_kernel, pack_table, heads),
            "project",
            tokens,
            [tile_spec(D), fixed_spec((1, project_width))]
            + [tile_spec(HEAD_DIM)] * 3
            + [ANY] * len(pack_shards),
            [(tile_spec(project_width), shape_of((tokens, project_width), BF))],
            [((D, project_width), cols)],
            [
                after(first_norm, gate),
                query_key_value_bias.reshape(1, -1),
                cosine,
                left,
                right,
                *pack_shards,
            ],
        )

    def attended_grad_work(gate):
        return call(
            functools.partial(attended_grad_kernel, pack_table),
            "attended_grad",
            tokens,
            [tile_spec(D, 4 * TILE)] + [ANY] * len(pack_shards),
            [(tile_spec(out_width, 4 * TILE), shape_of((tokens, out_width), BF))],
            [((D, out_width), cols)],
            [after(full_grad, gate), *pack_shards],
            tile=4 * TILE,
        )

    def whole_spec(*shape):
        return pl.BlockSpec(shape, lambda i: (0, 0))

    head_rows = whole_spec(heads, tokens), shape_of((heads, tokens), F32)
    head_entries = whole_spec(out_width, tokens), shape_of((out_width, tokens), F32)

    def attention_work(gate):
        return pl.pallas_call(
            functools.partial(attention_kernel, heads),
            name="attention",
            grid=(1,),
            in_specs=[
                pl.BlockSpec(memory_space=pltpu.SMEM),
                whole_spec(1, tokens),
                whole_spec(tokens, project_width),
            ],
            out_specs=[whole_spec(tokens, out_width), head_entries[0], head_rows[0]],
            out_shape=[shape_of((tokens, out_width), BF), head_entries[1], head_rows[1]],
            scratch_shapes=[pltpu.VMEM((heads, HEAD_DIM, tokens), BF)],
            compiler_params=pltpu.CompilerParams(vmem_limit_bytes=VMEM_LIMIT),
            cost_estimate=cost(8 * tokens * tokens * out_width),
        )(low_blocks, starts[None], after(projected, gate))

    def attention_back_work(gate):
        return pl.pallas_call(
            functools.partial(attention_back_kernel, heads),
            name="attention_back",
            grid=(1,),
            in_specs=[
                pl.BlockSpec(memory_space=pltpu.SMEM),
                whole_spec(1, tokens),
                *[whole_spec(tokens, HEAD_DIM)] * 3,
                whole_spec(tokens, project_width),
                whole_spec(tokens, out_width),
                head_entries[0],
                head_rows[0],
            ],
            out_specs=[whole_spec(tokens, project_width)],
            out_shape=[shape_of((tokens, project_width), BF)],
            scratch_shapes=[pltpu.VMEM((heads, HEAD_DIM, tokens), BF)]
            + [pltpu.VMEM((heads, tokens, HEAD_DIM), F32)] * 2,
            compiler_params=pltpu.CompilerParams(vmem_limit_bytes=VMEM_LIMIT),
            cost_estimate=cost(16 * tokens * tokens * out_width),
        )(
            low_blocks,
            starts[None],
            cosine,
            left,
            right,
            projected,
            after(attended_grad, gate),
            produced_t,
            log_total,
        )

    gate, ((projected,),) = slot([up_gather], gate, project_work)

    def attention_grad_work(gate):
        made = attention_work(gate)
        return *made, *attended_grad_work(gate + [made[2]])

    gate, ((attended, produced_t, log_total, attended_grad),) = slot(
        [up_gather], gate, attention_grad_work
    )
    gate = more([up_gather], gate)
    gate, ((project_grad,),) = slot([up_gather], gate, attention_back_work)
    up_shards, up_table = up_gather.shards()

    def pack_weight_work(gate):
        return weight_grad(
            cols, col_place, [(first_norm, after(project_grad, gate)), (full_grad, attended)]
        )

    def up_work(gate):
        return call(
            functools.partial(up_kernel, up_table),
            "up",
            tokens,
            [tile_spec(D), fixed_spec((1, hidden_width))] + [ANY] * len(up_shards),
            [
                (tile_spec(hidden_width), shape_of((tokens, hidden_width), BF)),
                (tile_spec(hidden_width), shape_of((tokens, hidden_width), F32)),
            ],
            [((D, hidden_width), cols)],
            [after(second_norm, gate), up_bias[None], *up_shards],
        )

    def down_weight_work(gate):
        return weight_grad(cols, col_place, [(after(hidden, gate), full_grad)], True)

    gate, (pack_chunks,) = slot([down_gather], gate, pack_weight_work)
    gate = more([down_gather], gate)
    if both is not None:
        both.chunks = pack_chunks
    gate, ((hidden, slope),) = slot([down_gather], gate, up_work)
    gate, (down_chunks,) = slot([down_gather], gate, down_weight_work)
    down_shards, down_table = down_gather.shards()
    pack_scatter = both or RingScatter(pack_chunks, cols)
    down_scatter = RingScatter(down_chunks, cols)
    if both is None:
        for _ in range(cols - 2):
            gate, _ = slot([pack_scatter], gate)

    def mixed_work(gate):
        return call(
            functools.partial(mixed_kernel, len(pack_shards), pack_table, down_table),
            "mixed",
            tokens,
            [tile_spec(out_width), tile_spec(hidden_width)] + [ANY] * (len(pack_shards) + len(down_shards)),
            [(tile_spec(D), shape_of((tokens, D), BF))],
            [((D, out_width), cols), ((D, hidden_width), cols)],
            [after(attended, gate), hidden, *pack_shards, *down_shards],
        )

    def hidden_grad_work(gate):
        return call(
            functools.partial(hidden_grad_kernel, down_table),
            "hidden_grad",
            tokens,
            [tile_spec(D), tile_spec(hidden_width)] + [ANY] * len(down_shards),
            [(tile_spec(hidden_width), shape_of((tokens, hidden_width), BF))],
            [((D, hidden_width), cols)],
            [after(full_grad, gate), slope, *down_shards],
        )

    pieces = [RowScatter.KEPT, RowScatter.SENT] if rows == 8 else [None]

    def back_work(gate):
        widths = project_width, hidden_width
        share = D // len(pieces)
        return pl.pallas_call(
            functools.partial(back_kernel, len(pack_shards), pack_table, up_table, pieces),
            name="back",
            grid=(tokens // TILE,),
            in_specs=[tile_spec(D), fixed_spec((4, D)), *map(tile_spec, widths)]
            + [ANY] * (len(pack_shards) + len(up_shards)),
            out_specs=[tile_spec(share)] * len(pieces)
            + [fixed_spec((4, D)), *[fixed_spec((1, width)) for width in widths]],
            out_shape=[shape_of((tokens, share), BF)] * len(pieces)
            + [shape_of((4, D), F32), *[shape_of((1, width), F32) for width in widths]],
            scratch_shapes=[pltpu.VMEM((D, width), BF) for width in widths]
            + [pltpu.SemaphoreType.DMA((cols,))] * 2
            + [pltpu.VMEM((TILE, D), BF)],
            compiler_params=pltpu.CompilerParams(
                dimension_semantics=("arbitrary",), vmem_limit_bytes=VMEM_LIMIT
            ),
            cost_estimate=cost(2 * tokens * D * sum(widths)),
        )(
            full_input,
            norm_params,
            project_grad,
            after(expand_grad, gate),
            *pack_shards,
            *up_shards,
        )

    def up_weight_work(gate):
        return weight_grad(cols, col_place, [(second_norm, after(expand_grad, gate))])

    def down_result_work(gate):
        return [down_scatter.result(gate)]

    def layer_out_work(gate):
        return [
            activations.astype(F32) + after(mixed_sum, gate).astype(F32) + output_bias + down_bias
        ]

    gate, ((mixed_part,),) = slot([pack_scatter], gate, mixed_work)
    mixed_sum = lax.psum_scatter(after(mixed_part, gate), "row", scatter_dimension=1, tiled=True)
    gate, ((expand_grad,),) = slot([down_scatter], gate, hidden_grad_work)
    gate = more([down_scatter], gate)
    gate, (up_chunks,) = slot([down_scatter], gate, up_weight_work)
    up_scatter = RingScatter(up_chunks, cols)
    gate, ((*back_parts, gains, project_bias_grad, up_bias_grad),) = slot(
        [down_scatter, up_scatter], gate, back_work
    )

    def split_work(gate):
        parts = pack_scatter.result(gate)
        shape = query_key_value.shape
        return parts[:, :project_width].reshape(shape), parts[:, project_width:].T

    def gains_work(gate):
        terms = after(gains, gate)
        terms = terms.reshape(4, rows, features).transpose(1, 0, 2).reshape(rows, -1)
        return [pair_scatter(terms, "row", rows, row_place)]

    row_scatter = RowScatter(*back_parts) if rows == 8 else None
    row_steps = [row_scatter] if rows == 8 else []

    for step in row_steps + [up_scatter]:
        step.step(gate)
    (gain_terms,) = gains_work(gate + [up_scatter.sent])
    (down_weight_grad,) = down_result_work(gate)
    project_weight_grad, output_weight_grad = split_work(gate)
    for step in row_steps:
        step.step([])
    small = [gain_terms, project_bias_grad[0], up_bias_grad[0], shift_out_grad]
    masks = [1 << bit for bit in range(cols.bit_length() - 1)]
    gate = row_scatter.parts if row_scatter is not None else []
    small = pair_sum(jnp.concatenate(small), "col", cols, masks[:-1], gate)
    gate = gate + [down_weight_grad, project_weight_grad, output_weight_grad, small]
    for _ in range(cols - 3):
        up_scatter.step(gate)
    (layer_out,) = layer_out_work([up_scatter.sent])
    arrived = pair_exchange(small, "col", cols, masks[-1], [up_scatter.sent])
    for step in row_steps:
        step.step([up_scatter.sent])
    up_weight_grad = up_scatter.result([layer_out])
    if row_scatter is not None:
        back_sum = row_scatter.result()
    else:
        back_sum = lax.psum_scatter(back_parts[0], "row", scatter_dimension=1, tiled=True)
    activations_grad = after(out_grad, [up_weight_grad]).astype(F32) + back_sum.astype(F32)
    small = after(small, [activations_grad]) + arrived
    sizes = [features] * 4 + [project_width, hidden_width, features]
    pieces, begin = [], 0
    for size in sizes:
        pieces.append(small[begin : begin + size])
        begin += size
    return (
        layer_out,
        activations_grad,
        pieces[0],
        pieces[1],
        pieces[2],
        pieces[3],
        project_weight_grad,
        pieces[4].reshape(query_key_value_bias.shape),
        output_weight_grad,
        pieces[6],
        up_weight_grad,
        pieces[5],
        down_weight_grad,
        pieces[6],
    )


def solution(mesh):
    placed = (
        P("col", "row"),
        P("col"),
        P("row"),
        P("row"),
        P("row"),
        P("row"),
        P("col", "row", None),
        P("row", None),
        P("row", "col"),
        P("row"),
        P("col", "row"),
        P("row"),
        P("row", "col"),
        P("row"),
        P("col", "row"),
    )

    def body(*args):
        return on_device(mesh.shape["row"], mesh.shape["col"], *args)

    return jax.shard_map(
        body,
        mesh=mesh,
        in_specs=placed,
        out_specs=(
            P("col", "row"),
            P("col", "row"),
            P("row"),
            P("row"),
            P("row"),
            P("row"),
            P("col", "row", None),
            P("row", None),
            P("row", "col"),
            P("row"),
            P("col", "row"),
            P("row"),
            P("row", "col"),
            P("row"),
        ),
        check_vma=False,
    )
```

```python
import functools

import jax
import jax.numpy as jnp
from jax import lax
from jax.experimental import pallas as pl
from jax.experimental.pallas import tpu as pltpu
from jax.sharding import PartitionSpec as P

D = 2048
HEAD_DIM = 128
ROTARY = 32
LENGTH = 2048

EPSILON = 1e-05
MASKED = -1e30
ROPE_BASE = 10000.0
BF = jnp.bfloat16
F32 = jnp.float32
LAST = (((1,), (1,)), ((), ()))
FIRST = (((0,), (0,)), ((), ()))
TILE = 256
QUERY_BLOCK = KEY_BLOCK = 512
VMEM_LIMIT = 56 * 1024 * 1024
LOG2_E = 1.4426950408889634
SQRT_HALF = 0.7071067811865476
INV_SQRT_2PI = 0.3989422804014327


def after(value, gate):
    return lax.optimization_barrier((value,) + tuple(gate))[0] if gate else value


class RingGather:
    def __init__(self, shard, count):
        self.count, self.arrays = count, [shard]

    def step(self, gate):
        count = self.count
        pairs = [(k, (k + 1) % count) for k in range(count)]
        self.arrays = self.arrays + [lax.ppermute(after(self.arrays[-1], gate), "col", pairs)]
        return self.arrays[-1:]

    def shards(self):
        count = self.count
        return self.arrays, [[(i - j) % count for j in range(count)] for i in range(count)]


class RingScatter:
    def __init__(self, chunks, count):
        self.chunks, self.count = chunks, count
        self.moving, self.done = None, 0

    def step(self, gate):
        self.done += 1
        count = self.count
        sent = after(self.chunks[count - self.done], gate)
        if self.moving is not None:
            sent = (sent.astype(F32) + self.moving.astype(F32)).astype(BF)
        pairs = [(k, (k + 1) % count) for k in range(count)]
        self.sent = sent
        self.moving = lax.ppermute(self.sent, "col", pairs)
        return [self.moving]

    def result(self, gate):
        return after(self.chunks[0], gate) + self.moving.astype(F32)


class LineBoth:
    def __init__(self, shard, place):
        self.shard, self.place = shard, place
        self.upward, self.downward = [shard], [shard]

    def step(self, gate):
        place, done = self.place, len(self.upward)
        up, down = self.upward[-1], self.downward[-1]
        if done == 2:
            up = jnp.where(place == 0, self.chunks[3], up)
            down = jnp.where(place == 3, self.chunks[1], down)
        elif done == 3:
            up = jnp.where(place == 2, up, self.add(2, up))
            down = jnp.where(place == 1, down, self.add(2, down))
        elif done == 4:
            up, down = self.add(1, up), self.add(3, down)
        up, down = after(up, gate), after(down, gate)
        self.upward.append(lax.ppermute(up, "col", [(0, 1), (1, 2), (2, 3)]))
        self.downward.append(lax.ppermute(down, "col", [(3, 2), (2, 1), (1, 0)]))
        return [self.upward[-1], self.downward[-1]]

    def add(self, at, array):
        return (self.chunks[at].astype(F32) + array.astype(F32)).astype(BF)

    def shards(self):
        table = [[0 if j == i else i - j if j < i else 3 + j - i for j in range(4)] for i in range(4)]
        return self.upward[:4] + self.downward[1:4], table

    def result(self, gate):
        return after(self.chunks[0], gate) + (self.upward[4].astype(F32) + self.downward[4].astype(F32))


class RowScatter:
    KEPT, SENT = [0, 2, 4, 6], [1, 3, 5, 7]

    def __init__(self, kept, sent):
        self.kept, self.sent, self.done = kept, sent, 0
        self.width, self.parts = kept.shape[1] // 4, []

    def send(self, array, mask, gate):
        self.parts.append(after(array, gate))
        return lax.ppermute(self.parts[-1], "row", [(k, k ^ mask) for k in range(8)])

    def piece(self, at):
        columns = slice(at * self.width, (at + 1) * self.width)
        return self.kept[:, columns].astype(F32) + self.core[:, columns].astype(F32)

    def step(self, gate):
        self.done += 1
        half = self.kept.shape[0] // 2
        if self.done == 1:
            self.core = self.send(self.sent, 1, gate)
            return [self.core]
        if self.done == 2:
            far = self.piece(3).astype(BF)
            self.from_x = self.send(far[:half], 2, gate)
            self.from_y = self.send(far[half:], 4, gate)
        else:
            empty = jnp.zeros_like(self.from_x, F32)
            from_x, from_y = self.from_x.astype(F32), self.from_y.astype(F32)
            for_x = self.piece(1) + jnp.concatenate([empty, from_y])
            for_y = self.piece(2) + jnp.concatenate([from_x, empty])
            self.from_x = self.send(for_x.astype(BF), 2, gate)
            self.from_y = self.send(for_y.astype(BF), 4, gate)
        return [self.from_x, self.from_y]

    def result(self):
        return self.piece(0) + self.from_x.astype(F32) + self.from_y.astype(F32)


def pair_sum(value, axis, count, masks, gate):
    for mask in masks:
        value = value + pair_exchange(value, axis, count, mask, gate)
    return value


def pair_exchange(value, axis, count, mask, gate):
    return lax.ppermute(after(value, gate), axis, [(k, k ^ mask) for k in range(count)])


def pair_scatter(value, axis, count, place):
    mask = count // 2
    while mask:
        upper = lax.rem(place // mask, 2) == 1
        low, high = value[:mask], value[mask:]
        kept, sent = jnp.where(upper, high, low), jnp.where(upper, low, high)
        value = kept + lax.ppermute(sent, axis, [(k, k ^ mask) for k in range(count)])
        mask //= 2
    return value[0]


def load_shards(refs, table, whole, sems, dim, columns=None):
    if columns is not None:
        refs = [ref.at[:, columns] for ref in refs]
    count = len(table)
    extent = refs[0].shape[dim]
    place = lax.axis_index("col")

    def spot(j):
        at = pl.ds(j * extent, extent)
        return whole.at[at, :] if dim == 0 else whole.at[:, at]

    for i in range(count):

        @pl.when(place == i)
        def _():
            for j in range(count):
                pltpu.make_async_copy(refs[table[i][j]], spot(j), sems.at[j]).start()

    for j in range(count):
        pltpu.make_async_copy(refs[0], spot(j), sems.at[j]).wait()


def normalize(tile):
    values = tile.astype(F32)
    centered = values - jnp.mean(values, axis=1, keepdims=True)
    inverse_scale = lax.rsqrt(jnp.mean(centered * centered, axis=1, keepdims=True) + EPSILON)
    return centered * inverse_scale, inverse_scale


def norm_kernel(act, params, first_out, second_out):
    normed, _ = normalize(act[...])
    first_out[...] = (normed * params[0:1, :] + params[1:2, :]).astype(BF)
    second_out[...] = (normed * params[2:3, :] + params[3:4, :]).astype(BF)


def up_kernel(table, *refs):
    norm, bias, *shards = refs[:-4]
    hidden_out, slope_out, whole, sems = refs[-4:]

    @pl.when(pl.program_id(0) == 0)
    def _():
        load_shards(shards, table, whole, sems, 0)

    lin = jnp.dot(norm[...], whole[...], preferred_element_type=F32) + bias[...]
    cdf = 0.5 + 0.5 * lax.erf(lin * SQRT_HALF)
    hidden_out[...] = (lin * cdf).astype(BF)
    slope_out[...] = cdf + lin * (INV_SQRT_2PI * jnp.exp(-0.5 * lin * lin))


def turn(values, tables, sign):
    cosine, left, right = tables
    half = ROTARY // 2
    turned = left * pltpu.roll(values, HEAD_DIM - half, 1) + right * pltpu.roll(values, half, 1)
    return values * cosine + sign * turned


def project_kernel(table, heads, *refs):
    norm, bias, cosine, left, right, *shards = refs[:-3]
    out, whole, sems = refs[-3:]

    @pl.when(pl.program_id(0) == 0)
    def _():
        load_shards(shards, table, whole, sems, 0, pl.ds(0, whole.shape[1]))

    lin = jnp.dot(norm[...], whole[...], preferred_element_type=F32) + bias[...]
    tables = cosine[...], left[...], right[...]
    for head in range(heads):
        for part in range(3):
            at = slice((head * 3 + part) * HEAD_DIM, (head * 3 + part + 1) * HEAD_DIM)
            piece = lin[:, at]
            out[:, at] = (turn(piece, tables, 1.0) if part < 2 else piece).astype(BF)


def attended_grad_kernel(table, *refs):
    grad, *shards = refs[:-3]
    out, whole, sems = refs[-3:]

    @pl.when(pl.program_id(0) == 0)
    def _():
        columns = pl.ds(shards[0].shape[1] - whole.shape[1], whole.shape[1])
        load_shards(shards, table, whole, sems, 0, columns)

    out[...] = jnp.dot(grad[...], whole[...], preferred_element_type=F32).astype(BF)


def head_columns(head, part):
    return slice((3 * head + part) * HEAD_DIM, (3 * head + part + 1) * HEAD_DIM)


def own_columns(head):
    return slice(head * HEAD_DIM, (head + 1) * HEAD_DIM)


def rows_of(block, extent):
    return pl.ds(pl.multiple_of(block * extent, extent), extent)


def allowed_scores(project, start, block, at, head, masked):
    rows, keys = rows_of(block, QUERY_BLOCK), rows_of(at, KEY_BLOCK)
    scores = lax.dot_general(
        project[keys, head_columns(head, 1)],
        project[rows, head_columns(head, 0)],
        LAST,
        preferred_element_type=F32,
    ) * (HEAD_DIM**-0.5 * LOG2_E)
    if not masked:
        return scores
    place = block * QUERY_BLOCK + lax.broadcasted_iota(jnp.int32, (1, QUERY_BLOCK), 1)
    key_place = at * KEY_BLOCK + lax.broadcasted_iota(jnp.int32, (KEY_BLOCK, QUERY_BLOCK), 0)
    allowed = (key_place >= start[:, rows]) & (key_place <= place)
    return jnp.where(allowed, scores, MASKED)


def over_keys(low, high, block, step, carry):
    between = jnp.minimum(high[block], block)
    carry = lax.fori_loop(low[block], between, functools.partial(step, True), carry)
    carry = lax.fori_loop(between, block, functools.partial(step, False), carry)
    return step(True, block, carry)


def attention_kernel(low, high, start, project, *refs):
    out, produced_t, log_total, v_t = refs[-4:]
    v_t[...] = project[:, head_columns(0, 2)].T

    def query_block(block, _):
        rows = rows_of(block, QUERY_BLOCK)

        def forward(masked, at, carry):
            largest, total, produced = carry
            scores = allowed_scores(project, start, block, at, 0, masked)
            newest = jnp.maximum(largest, jnp.max(scores, axis=0, keepdims=True))
            shrink = jnp.exp2(largest - newest)
            parts = jnp.exp2(scores - newest)
            total = total * shrink + jnp.sum(parts, axis=0, keepdims=True)
            produced = produced * shrink + jnp.dot(
                v_t[:, rows_of(at, KEY_BLOCK)], parts.astype(BF), preferred_element_type=F32
            )
            return newest, total, produced

        empty = jnp.zeros((1, QUERY_BLOCK), F32)
        wide = jnp.zeros((HEAD_DIM, QUERY_BLOCK), F32)
        largest, total, produced = over_keys(
            low, high, block, forward, (empty + MASKED, empty, wide)
        )
        produced = produced * (1.0 / total)
        out[rows, :] = produced.T.astype(BF)
        produced_t[:, rows] = produced
        log_total[:, rows] = largest + jnp.log2(total)
        return 0

    lax.fori_loop(0, project.shape[0] // QUERY_BLOCK, query_block, 0)


def attention_back_kernel(
    heads,
    low,
    high,
    start,
    cosine,
    left,
    right,
    project,
    grad,
    *refs,
):
    produced_t, log_total = refs[:heads], refs[heads : 2 * heads]
    project_grad, k_t, dk, dv = refs[2 * heads :]
    length = project.shape[0]
    scale = HEAD_DIM**-0.5
    for head in range(heads):
        k_t[head] = project[:, head_columns(head, 1)].T
    dk[...] = jnp.zeros_like(dk)
    dv[...] = jnp.zeros_like(dv)

    def query_block(block, _):
        rows = rows_of(block, QUERY_BLOCK)
        deltas = [
            jnp.sum(
                produced_t[head][:, rows] * grad[rows, own_columns(head)].astype(F32).T,
                axis=0,
                keepdims=True,
            )
            for head in range(heads)
        ]

        def backward(masked, at, query_grads):
            keys, made = rows_of(at, KEY_BLOCK), []
            for head in range(heads):
                scores = allowed_scores(project, start, block, at, head, masked)
                prob_grad = lax.dot_general(
                    project[keys, head_columns(head, 2)],
                    grad[rows, own_columns(head)],
                    LAST,
                    preferred_element_type=F32,
                )
                probs = jnp.exp2(scores - log_total[head][:, rows])
                score_grad = (probs * (prob_grad - deltas[head])).astype(BF)
                dv[head, keys, :] += jnp.dot(
                    probs.astype(BF), grad[rows, own_columns(head)], preferred_element_type=F32
                )
                dk[head, keys, :] += jnp.dot(
                    score_grad, project[rows, head_columns(head, 0)], preferred_element_type=F32
                )
                made.append(
                    query_grads[head]
                    + jnp.dot(k_t[head, :, keys], score_grad, preferred_element_type=F32)
                )
            return tuple(made)

        wide = jnp.zeros((HEAD_DIM, QUERY_BLOCK), F32)
        query_grads = over_keys(low, high, block, backward, (wide,) * heads)
        tables = cosine[rows, :], left[rows, :], right[rows, :]
        for head in range(heads):
            project_grad[rows, head_columns(head, 0)] = turn(
                (query_grads[head] * scale).T, tables, -1.0
            ).astype(BF)
        return 0

    lax.fori_loop(0, length // QUERY_BLOCK, query_block, 0)
    tables = cosine[...], left[...], right[...]
    for head in range(heads):
        project_grad[:, head_columns(head, 1)] = turn(dk[head] * scale, tables, -1.0).astype(BF)
        project_grad[:, head_columns(head, 2)] = dv[head].astype(BF)


def mixed_kernel(pack_count, pack_table, down_table, *refs):
    attended, hidden, *shards = refs[:-5]
    pack_shards, down_shards = shards[:pack_count], shards[pack_count:]
    out, output_whole, down_whole, output_sems, down_sems = refs[-5:]

    @pl.when(pl.program_id(0) == 0)
    def _():
        width = pack_shards[0].shape[1]
        columns = pl.ds(width - output_whole.shape[1], output_whole.shape[1])
        load_shards(pack_shards, pack_table, output_whole, output_sems, 0, columns)
        load_shards(down_shards, down_table, down_whole, down_sems, 0)

    out[...] = (
        lax.dot_general(attended[...], output_whole[...], LAST, preferred_element_type=F32)
        + lax.dot_general(hidden[...], down_whole[...], LAST, preferred_element_type=F32)
    ).astype(BF)


def hidden_grad_kernel(table, *refs):
    grad, slope, *shards = refs[:-3]
    out, whole, sems = refs[-3:]

    @pl.when(pl.program_id(0) == 0)
    def _():
        load_shards(shards, table, whole, sems, 0)

    hidden_grad = jnp.dot(grad[...], whole[...], preferred_element_type=F32)
    out[...] = (hidden_grad * slope[...]).astype(BF)


def weight_grad_kernel(count, pairs, *refs):
    lefts_rights, outs = refs[: 2 * pairs], refs[2 * pairs :]
    for step in range(count):

        @pl.when(pl.program_id(0) == step)
        def _():
            begin = 0
            for pair in range(pairs):
                left, right = lefts_rights[2 * pair], lefts_rights[2 * pair + 1]
                made = lax.dot_general(left[...], right[...], FIRST, preferred_element_type=F32)
                width = made.shape[1]
                outs[step][:, begin : begin + width] = made.astype(outs[step].dtype)
                begin += width


def back_kernel(pack_count, pack_table, up_table, pieces, *refs):
    act, params, project, expand, *shards = refs[: -8 - len(pieces)]
    project_shards, up_shards = shards[:pack_count], shards[pack_count:]
    outs = refs[-8 - len(pieces) : -8]
    gains, project_bias, up_bias, project_whole, up_whole, project_sems, up_sems, tile = refs[-8:]

    @pl.when(pl.program_id(0) == 0)
    def _():
        columns = pl.ds(0, project_whole.shape[1])
        load_shards(project_shards, pack_table, project_whole, project_sems, 0, columns)
        load_shards(up_shards, up_table, up_whole, up_sems, 0)
        gains[...] = jnp.zeros_like(gains)
        project_bias[...] = jnp.zeros_like(project_bias)
        up_bias[...] = jnp.zeros_like(up_bias)

    normed, inverse_scale = normalize(act[...])
    first = lax.dot_general(project[...], project_whole[...], LAST, preferred_element_type=F32)
    second = lax.dot_general(expand[...], up_whole[...], LAST, preferred_element_type=F32)
    gains[0:1, :] += jnp.sum(first * normed, axis=0, keepdims=True)
    gains[1:2, :] += jnp.sum(first, axis=0, keepdims=True)
    gains[2:3, :] += jnp.sum(second * normed, axis=0, keepdims=True)
    gains[3:4, :] += jnp.sum(second, axis=0, keepdims=True)
    project_bias[...] += jnp.sum(project[...].astype(F32), axis=0, keepdims=True)
    up_bias[...] += jnp.sum(expand[...].astype(F32), axis=0, keepdims=True)
    normed_grad = first * params[0:1, :] + second * params[2:3, :]
    mean_grad = jnp.mean(normed_grad, axis=1, keepdims=True)
    mean_product = jnp.mean(normed_grad * normed, axis=1, keepdims=True)
    result = (inverse_scale * (normed_grad - mean_grad - normed * mean_product)).astype(BF)
    if pieces == [None]:
        outs[0][...] = result
        return
    tile[...] = result
    place, width = lax.axis_index("row"), tile.shape[1] // 8
    for out, masks in zip(outs, pieces):
        for at, mask in enumerate(masks):
            source = pl.ds(pl.multiple_of((place ^ mask) * width, width), width)
            out[:, at * width : (at + 1) * width] = tile[:, source]


def tile_spec(width, tile=TILE):
    return pl.BlockSpec((tile, width), lambda i: (i, 0))


def fixed_spec(shape):
    return pl.BlockSpec(shape, lambda i: (0, 0))


ANY = pl.BlockSpec(memory_space=pl.ANY)


def shape_of(shape, kind):
    return jax.ShapeDtypeStruct(shape, kind)


def cost(flops, moved=0):
    return pl.CostEstimate(flops=int(flops), bytes_accessed=int(moved), transcendentals=0)


def call(kernel, name, tokens, ins, outs, wholes, args, moved=0, tile=TILE):
    scratch = [pltpu.VMEM(shape, BF) for shape, _ in wholes] + [
        pltpu.SemaphoreType.DMA((count,)) for _, count in wholes
    ]
    return pl.pallas_call(
        kernel,
        name=name,
        grid=(tokens // tile,),
        in_specs=ins,
        out_specs=[spec for spec, _ in outs],
        out_shape=[shape for _, shape in outs],
        scratch_shapes=scratch,
        compiler_params=pltpu.CompilerParams(
            dimension_semantics=("arbitrary",), vmem_limit_bytes=VMEM_LIMIT
        ),
        cost_estimate=cost(sum(2 * tokens * shape[0] * shape[1] for shape, _ in wholes), moved),
    )(*args)


def weight_grad(count, place, pairs, chunked_right=False):
    specs, arrays, width = [], [], 0
    for left, right in pairs:
        chunked, fixed = (right, left) if chunked_right else (left, right)
        extent = chunked.shape[1] // count
        chunk_spec = pl.BlockSpec(
            (chunked.shape[0], extent), lambda i, spot: (0, lax.rem(spot[0] + i, count))
        )
        fixed_spec_ = pl.BlockSpec(fixed.shape, lambda i, spot: (0, 0))
        specs += [fixed_spec_, chunk_spec] if chunked_right else [chunk_spec, fixed_spec_]
        arrays += [left, right]
        rows, columns = (fixed.shape[1], extent) if chunked_right else (extent, fixed.shape[1])
        width += columns
    shape = (rows, width)
    return pl.pallas_call(
        functools.partial(drop_first, functools.partial(weight_grad_kernel, count, len(pairs))),
        name="weight_grad",
        grid_spec=pltpu.PrefetchScalarGridSpec(
            num_scalar_prefetch=1,
            grid=(count,),
            in_specs=specs,
            out_specs=[pl.BlockSpec(shape, lambda i, spot: (0, 0))] * count,
        ),
        out_shape=[shape_of(shape, F32 if r == 0 else BF) for r in range(count)],
        compiler_params=pltpu.CompilerParams(
            dimension_semantics=("arbitrary",), vmem_limit_bytes=VMEM_LIMIT
        ),
        cost_estimate=cost(2 * arrays[0].shape[0] * rows * width * count),
    )(place[None], *arrays)


def drop_first(kernel, spot, *refs):
    kernel(*refs)


def angle_tables(row_total):
    positions = (jnp.arange(row_total, dtype=jnp.int32) % LENGTH).astype(F32)
    frequency = ROPE_BASE ** (-jnp.arange(0, ROTARY, 2, dtype=jnp.int32).astype(F32) / ROTARY)
    turning = positions[:, None] * frequency[None, :]
    cosine, sine = jnp.cos(turning), jnp.sin(turning)
    rest = HEAD_DIM - ROTARY
    zeros = jnp.zeros_like(sine)
    return (
        jnp.concatenate([cosine, cosine, jnp.ones((row_total, rest), F32)], axis=1),
        jnp.concatenate([-sine, zeros, jnp.zeros((row_total, rest), F32)], axis=1),
        jnp.concatenate([zeros, sine, jnp.zeros((row_total, rest), F32)], axis=1),
    )


def on_device(
    rows,
    cols,
    activations,
    document_ids,
    attention_gain,
    attention_shift,
    feedforward_gain,
    feedforward_shift,
    query_key_value,
    query_key_value_bias,
    output_weight,
    output_bias,
    up_weight,
    up_bias,
    down_weight,
    down_bias,
    out_grad,
):
    row_place, col_place = lax.axis_index("row"), lax.axis_index("col")
    tokens, features = activations.shape
    heads = query_key_value.shape[1]
    project_width, out_width = heads * 3 * HEAD_DIM, heads * HEAD_DIM
    hidden_width = up_weight.shape[1]

    full_input = lax.all_gather(activations, "row", axis=1, tiled=True)
    full_grad = lax.all_gather(out_grad, "row", axis=1, tiled=True)

    pack = jnp.concatenate(
        [query_key_value.astype(BF).reshape(-1, project_width), output_weight.astype(BF).T], axis=1
    )
    pack_gather = RingGather(pack, cols)
    down_shard = down_weight.astype(BF).T
    up_shard = up_weight.astype(BF)
    up_gather = RingGather(up_shard, cols)
    both = LineBoth(down_shard, col_place) if cols == 4 else None
    down_gather = both or RingGather(down_shard, cols)

    def slot(transfers, gate, *works):
        moved = []
        for transfer in transfers:
            moved += transfer.step(gate)
        made = [work(gate) for work in works]
        return moved + [array for arrays in made for array in arrays], made

    def more(transfers, gate):
        for _ in range(cols - 4):
            gate, _ = slot(transfers, gate)
        return gate

    def tables_work(gate):
        cosine, left, right = angle_tables(tokens)
        starts = jnp.sum(
            (document_ids[:, None] < document_ids[None, :]).astype(jnp.int32), axis=0
        )
        sums = jnp.sum(out_grad.astype(F32), axis=0)
        return cosine, left, right, starts, sums, down_shard, up_shard

    def params_work(gate):
        stacked = jnp.stack(
            [attention_gain, attention_shift, feedforward_gain, feedforward_shift]
        )
        return [lax.all_gather(after(stacked, gate), "row", axis=1, tiled=True)]

    def norm_work(gate):
        return call(
            norm_kernel,
            "norm",
            tokens,
            [tile_spec(D), fixed_spec((4, D))],
            [
                (tile_spec(D), shape_of((tokens, D), BF)),
                (tile_spec(D), shape_of((tokens, D), BF)),
            ],
            [],
            [full_input, after(norm_params, gate)],
            6 * tokens * D,
        )

    gate, ((cosine, left, right, starts, shift_out_grad, *_),) = slot([pack_gather], [], tables_work)
    low_blocks = starts[::QUERY_BLOCK] // KEY_BLOCK
    high_blocks = (starts[QUERY_BLOCK - 1 :: QUERY_BLOCK] + KEY_BLOCK - 1) // KEY_BLOCK
    gate, ((norm_params,),) = slot([pack_gather], gate, params_work)
    gate = more([pack_gather], gate)
    gate, ((first_norm, second_norm),) = slot([pack_gather], gate, norm_work)
    pack_shards, pack_table = pack_gather.shards()

    def project_work(gate):
        return call(
            functools.partial(project_kernel, pack_table, heads),
            "project",
            tokens,
            [tile_spec(D), fixed_spec((1, project_width))]
            + [tile_spec(HEAD_DIM)] * 3
            + [ANY] * len(pack_shards),
            [(tile_spec(project_width), shape_of((tokens, project_width), BF))],
            [((D, project_width), cols)],
            [
                after(first_norm, gate),
                query_key_value_bias.reshape(1, -1),
                cosine,
                left,
                right,
                *pack_shards,
            ],
        )

    def attended_grad_work(gate):
        return call(
            functools.partial(attended_grad_kernel, pack_table),
            "attended_grad",
            tokens,
            [tile_spec(D, 4 * TILE)] + [ANY] * len(pack_shards),
            [(tile_spec(out_width, 4 * TILE), shape_of((tokens, out_width), BF))],
            [((D, out_width), cols)],
            [after(full_grad, gate), *pack_shards],
            tile=4 * TILE,
        )

    def whole_spec(*shape):
        return pl.BlockSpec(shape, lambda i: (0, 0))

    def attention_work(projected, head, before):
        def column_spec(width):
            return pl.BlockSpec((tokens, width), lambda i: (0, head))

        return pl.pallas_call(
            attention_kernel,
            name="attention",
            grid=(1,),
            in_specs=[pl.BlockSpec(memory_space=pltpu.SMEM)] * 2
            + [whole_spec(1, tokens), column_spec(3 * HEAD_DIM)]
            + [ANY] * len(before),
            out_specs=[column_spec(HEAD_DIM), whole_spec(HEAD_DIM, tokens), whole_spec(1, tokens)],
            out_shape=[
                shape_of((tokens, out_width), BF),
                shape_of((HEAD_DIM, tokens), F32),
                shape_of((1, tokens), F32),
            ],
            input_output_aliases={4: 0} if before else {},
            scratch_shapes=[pltpu.VMEM((HEAD_DIM, tokens), BF)],
            compiler_params=pltpu.CompilerParams(vmem_limit_bytes=VMEM_LIMIT),
            cost_estimate=cost(8 * tokens * tokens * HEAD_DIM),
        )(low_blocks, high_blocks, starts[None], projected, *before)

    def attention_back_work(gate):
        return pl.pallas_call(
            functools.partial(attention_back_kernel, heads),
            name="attention_back",
            grid=(1,),
            in_specs=[pl.BlockSpec(memory_space=pltpu.SMEM)] * 2
            + [whole_spec(1, tokens)]
            + [whole_spec(tokens, HEAD_DIM)] * 3
            + [whole_spec(tokens, project_width), whole_spec(tokens, out_width)]
            + [whole_spec(HEAD_DIM, tokens)] * heads
            + [whole_spec(1, tokens)] * heads,
            out_specs=[whole_spec(tokens, project_width)],
            out_shape=[shape_of((tokens, project_width), BF)],
            scratch_shapes=[pltpu.VMEM((heads, HEAD_DIM, tokens), BF)]
            + [pltpu.VMEM((heads, tokens, HEAD_DIM), F32)] * 2,
            compiler_params=pltpu.CompilerParams(vmem_limit_bytes=VMEM_LIMIT),
            cost_estimate=cost(16 * tokens * tokens * out_width),
        )(
            low_blocks,
            high_blocks,
            starts[None],
            cosine,
            left,
            right,
            projected,
            after(attended_grad, gate),
            *[made[1] for made in by_head],
            *[made[2] for made in by_head],
        )

    by_head = []

    def first_head_work(gate):
        (projected,) = project_work(gate)
        by_head.append(attention_work(projected, 0, []))
        return projected, by_head[0][2]

    gate, ((projected, _),) = slot([up_gather], gate, first_head_work)

    def other_heads_work(gate):
        values = after(projected, gate)
        for head in range(1, heads):
            by_head.append(attention_work(values, head, [by_head[-1][0]]))
        return attended_grad_work(gate + [by_head[-1][2]])

    gate, ((attended_grad,),) = slot([up_gather], gate, other_heads_work)
    attended = by_head[-1][0]
    gate = more([up_gather], gate)
    gate, ((project_grad,),) = slot([up_gather], gate, attention_back_work)
    up_shards, up_table = up_gather.shards()

    def pack_weight_work(gate):
        return weight_grad(
            cols, col_place, [(first_norm, after(project_grad, gate)), (full_grad, attended)]
        )

    def up_work(gate):
        return call(
            functools.partial(up_kernel, up_table),
            "up",
            tokens,
            [tile_spec(D, 2 * TILE), fixed_spec((1, hidden_width))] + [ANY] * len(up_shards),
            [
                (tile_spec(hidden_width, 2 * TILE), shape_of((tokens, hidden_width), BF)),
                (tile_spec(hidden_width, 2 * TILE), shape_of((tokens, hidden_width), F32)),
            ],
            [((D, hidden_width), cols)],
            [after(second_norm, gate), up_bias[None], *up_shards],
            tile=2 * TILE,
        )

    def down_weight_work(gate):
        return weight_grad(cols, col_place, [(after(hidden, gate), full_grad)], True)

    gate, (pack_chunks,) = slot([down_gather], gate, pack_weight_work)
    gate = more([down_gather], gate)
    if both is not None:
        both.chunks = pack_chunks
    gate, ((hidden, slope),) = slot([down_gather], gate, up_work)
    gate, (down_chunks,) = slot([down_gather], gate, down_weight_work)
    down_shards, down_table = down_gather.shards()
    pack_scatter = both or RingScatter(pack_chunks, cols)
    down_scatter = RingScatter(down_chunks, cols)
    if both is None:
        for _ in range(cols - 2):
            gate, _ = slot([pack_scatter], gate)

    def mixed_work(gate):
        return call(
            functools.partial(mixed_kernel, len(pack_shards), pack_table, down_table),
            "mixed",
            tokens,
            [tile_spec(out_width, 2 * TILE), tile_spec(hidden_width, 2 * TILE)] + [ANY] * (len(pack_shards) + len(down_shards)),
            [(tile_spec(D, 2 * TILE), shape_of((tokens, D), BF))],
            [((D, out_width), cols), ((D, hidden_width), cols)],
            [after(attended, gate), hidden, *pack_shards, *down_shards],
            tile=2 * TILE,
        )

    def hidden_grad_work(gate):
        return call(
            functools.partial(hidden_grad_kernel, down_table),
            "hidden_grad",
            tokens,
            [tile_spec(D, 2 * TILE), tile_spec(hidden_width, 2 * TILE)] + [ANY] * len(down_shards),
            [(tile_spec(hidden_width, 2 * TILE), shape_of((tokens, hidden_width), BF))],
            [((D, hidden_width), cols)],
            [after(full_grad, gate), slope, *down_shards],
            tile=2 * TILE,
        )

    pieces = [RowScatter.KEPT, RowScatter.SENT] if rows == 8 else [None]

    def back_work(gate):
        widths = project_width, hidden_width
        share = D // len(pieces)
        return pl.pallas_call(
            functools.partial(back_kernel, len(pack_shards), pack_table, up_table, pieces),
            name="back",
            grid=(tokens // TILE,),
            in_specs=[tile_spec(D), fixed_spec((4, D)), *map(tile_spec, widths)]
            + [ANY] * (len(pack_shards) + len(up_shards)),
            out_specs=[tile_spec(share)] * len(pieces)
            + [fixed_spec((4, D)), *[fixed_spec((1, width)) for width in widths]],
            out_shape=[shape_of((tokens, share), BF)] * len(pieces)
            + [shape_of((4, D), F32), *[shape_of((1, width), F32) for width in widths]],
            scratch_shapes=[pltpu.VMEM((D, width), BF) for width in widths]
            + [pltpu.SemaphoreType.DMA((cols,))] * 2
            + [pltpu.VMEM((TILE, D), BF)],
            compiler_params=pltpu.CompilerParams(
                dimension_semantics=("arbitrary",), vmem_limit_bytes=VMEM_LIMIT
            ),
            cost_estimate=cost(2 * tokens * D * sum(widths)),
        )(
            full_input,
            norm_params,
            project_grad,
            after(expand_grad, gate),
            *pack_shards,
            *up_shards,
        )

    def up_weight_work(gate):
        return weight_grad(cols, col_place, [(second_norm, after(expand_grad, gate))])

    def down_result_work(gate):
        return [down_scatter.result(gate)]

    def layer_out_work(gate):
        return [
            activations.astype(F32) + after(mixed_sum, gate).astype(F32) + output_bias + down_bias
        ]

    gate, ((mixed_part,),) = slot([pack_scatter], gate, mixed_work)
    mixed_sum = lax.psum_scatter(after(mixed_part, gate), "row", scatter_dimension=1, tiled=True)
    gate, ((expand_grad,),) = slot([down_scatter], gate, hidden_grad_work)
    gate = more([down_scatter], gate)
    gate, (up_chunks,) = slot([down_scatter], gate, up_weight_work)
    up_scatter = RingScatter(up_chunks, cols)
    gate, ((*back_parts, gains, project_bias_grad, up_bias_grad),) = slot(
        [down_scatter, up_scatter], gate, back_work
    )

    def split_work(gate):
        parts = pack_scatter.result(gate)
        shape = query_key_value.shape
        return parts[:, :project_width].reshape(shape), parts[:, project_width:].T

    def gains_work(gate):
        terms = after(gains, gate)
        terms = terms.reshape(4, rows, features).transpose(1, 0, 2).reshape(rows, -1)
        return [pair_scatter(terms, "row", rows, row_place)]

    row_scatter = RowScatter(*back_parts) if rows == 8 else None
    row_steps = [row_scatter] if rows == 8 else []

    for step in row_steps + [up_scatter]:
        step.step(gate)
    (gain_terms,) = gains_work(gate + [up_scatter.sent])
    (down_weight_grad,) = down_result_work(gate)
    project_weight_grad, output_weight_grad = split_work(gate)
    for step in row_steps:
        step.step([])
    small = [gain_terms, project_bias_grad[0], up_bias_grad[0], shift_out_grad]
    masks = [1 << bit for bit in range(cols.bit_length() - 1)]
    gate = row_scatter.parts if row_scatter is not None else []
    small = pair_sum(jnp.concatenate(small), "col", cols, masks[:-1], gate)
    gate = gate + [down_weight_grad, project_weight_grad, output_weight_grad, small]
    for _ in range(cols - 3):
        up_scatter.step(gate)
    (layer_out,) = layer_out_work([up_scatter.sent])
    arrived = pair_exchange(small, "col", cols, masks[-1], [up_scatter.sent])
    for step in row_steps:
        step.step([up_scatter.sent])
    up_weight_grad = up_scatter.result([layer_out])
    if row_scatter is not None:
        back_sum = row_scatter.result()
    else:
        back_sum = lax.psum_scatter(back_parts[0], "row", scatter_dimension=1, tiled=True)
    activations_grad = after(out_grad, [up_weight_grad]).astype(F32) + back_sum.astype(F32)
    small = after(small, [activations_grad]) + arrived
    sizes = [features] * 4 + [project_width, hidden_width, features]
    pieces, begin = [], 0
    for size in sizes:
        pieces.append(small[begin : begin + size])
        begin += size
    return (
        layer_out,
        activations_grad,
        pieces[0],
        pieces[1],
        pieces[2],
        pieces[3],
        project_weight_grad,
        pieces[4].reshape(query_key_value_bias.shape),
        output_weight_grad,
        pieces[6],
        up_weight_grad,
        pieces[5],
        down_weight_grad,
        pieces[6],
    )


def solution(mesh):
    placed = (
        P("col", "row"),
        P("col"),
        P("row"),
        P("row"),
        P("row"),
        P("row"),
        P("col", "row", None),
        P("row", None),
        P("row", "col"),
        P("row"),
        P("col", "row"),
        P("row"),
        P("row", "col"),
        P("row"),
        P("col", "row"),
    )

    def body(*args):
        return on_device(mesh.shape["row"], mesh.shape["col"], *args)

    return jax.shard_map(
        body,
        mesh=mesh,
        in_specs=placed,
        out_specs=(
            P("col", "row"),
            P("col", "row"),
            P("row"),
            P("row"),
            P("row"),
            P("row"),
            P("col", "row", None),
            P("row", None),
            P("row", "col"),
            P("row"),
            P("col", "row"),
            P("row"),
            P("row", "col"),
            P("row"),
        ),
        check_vma=False,
    )
```

```python
import functools

import jax
import jax.numpy as jnp
from jax import lax
from jax.experimental import pallas as pl
from jax.experimental.pallas import tpu as pltpu
from jax.sharding import PartitionSpec as P

D = 2048
HEAD_DIM = 128
ROTARY = 32
LENGTH = 2048

EPSILON = 1e-05
MASKED = -1e30
ROPE_BASE = 10000.0
BF = jnp.bfloat16
F32 = jnp.float32
LAST = (((1,), (1,)), ((), ()))
FIRST = (((0,), (0,)), ((), ()))
TILE = 256
QUERY_BLOCK = KEY_BLOCK = 512
VMEM_LIMIT = 56 * 1024 * 1024
LOG2_E = 1.4426950408889634
SQRT_HALF = 0.7071067811865476
INV_SQRT_2PI = 0.3989422804014327


def after(value, gate):
    return lax.optimization_barrier((value,) + tuple(gate))[0] if gate else value


class RingGather:
    def __init__(self, shard, count):
        self.count, self.arrays = count, [shard]

    def step(self, gate):
        count = self.count
        pairs = [(k, (k + 1) % count) for k in range(count)]
        self.arrays = self.arrays + [lax.ppermute(after(self.arrays[-1], gate), "col", pairs)]
        return self.arrays[-1:]

    def shards(self):
        count = self.count
        return self.arrays, [[(i - j) % count for j in range(count)] for i in range(count)]


class RingScatter:
    def __init__(self, chunks, count):
        self.chunks, self.count = chunks, count
        self.moving, self.done = None, 0

    def step(self, gate):
        self.done += 1
        count = self.count
        sent = after(self.chunks[count - self.done], gate)
        if self.moving is not None:
            sent = (sent.astype(F32) + self.moving.astype(F32)).astype(BF)
        pairs = [(k, (k + 1) % count) for k in range(count)]
        self.sent = sent
        self.moving = lax.ppermute(self.sent, "col", pairs)
        return [self.moving]

    def result(self, gate):
        return after(self.chunks[0], gate) + self.moving.astype(F32)


class LineBoth:
    def __init__(self, shard, place):
        self.shard, self.place = shard, place
        self.upward, self.downward = [shard], [shard]

    def step(self, gate):
        place, done = self.place, len(self.upward)
        up, down = self.upward[-1], self.downward[-1]
        if done == 2:
            up = jnp.where(place == 0, self.chunks[3], up)
            down = jnp.where(place == 3, self.chunks[1], down)
        elif done == 3:
            up = jnp.where(place == 2, up, self.add(2, up))
            down = jnp.where(place == 1, down, self.add(2, down))
        elif done == 4:
            up, down = self.add(1, up), self.add(3, down)
        up, down = after(up, gate), after(down, gate)
        self.upward.append(lax.ppermute(up, "col", [(0, 1), (1, 2), (2, 3)]))
        self.downward.append(lax.ppermute(down, "col", [(3, 2), (2, 1), (1, 0)]))
        return [self.upward[-1], self.downward[-1]]

    def add(self, at, array):
        return (self.chunks[at].astype(F32) + array.astype(F32)).astype(BF)

    def shards(self):
        table = [[0 if j == i else i - j if j < i else 3 + j - i for j in range(4)] for i in range(4)]
        return self.upward[:4] + self.downward[1:4], table

    def result(self, gate):
        return after(self.chunks[0], gate) + (self.upward[4].astype(F32) + self.downward[4].astype(F32))


def pair_sum(value, axis, count, masks, gate):
    for mask in masks:
        value = value + pair_exchange(value, axis, count, mask, gate)
    return value


def pair_exchange(value, axis, count, mask, gate):
    return lax.ppermute(after(value, gate), axis, [(k, k ^ mask) for k in range(count)])


def pair_scatter(value, axis, count, place):
    mask = count // 2
    while mask:
        upper = lax.rem(place // mask, 2) == 1
        low, high = value[:mask], value[mask:]
        kept, sent = jnp.where(upper, high, low), jnp.where(upper, low, high)
        value = kept + lax.ppermute(sent, axis, [(k, k ^ mask) for k in range(count)])
        mask //= 2
    return value[0]


def load_shards(refs, table, whole, sems, dim, columns=None):
    if columns is not None:
        refs = [ref.at[:, columns] for ref in refs]
    count = len(table)
    extent = refs[0].shape[dim]
    place = lax.axis_index("col")

    def spot(j):
        at = pl.ds(j * extent, extent)
        return whole.at[at, :] if dim == 0 else whole.at[:, at]

    for i in range(count):

        @pl.when(place == i)
        def _():
            for j in range(count):
                pltpu.make_async_copy(refs[table[i][j]], spot(j), sems.at[j]).start()

    for j in range(count):
        pltpu.make_async_copy(refs[0], spot(j), sems.at[j]).wait()


def normalize(tile):
    values = tile.astype(F32)
    centered = values - jnp.mean(values, axis=1, keepdims=True)
    inverse_scale = lax.rsqrt(jnp.mean(centered * centered, axis=1, keepdims=True) + EPSILON)
    return centered * inverse_scale, inverse_scale


def norm_kernel(act, params, first_out, second_out):
    normed, _ = normalize(act[...])
    first_out[...] = (normed * params[0:1, :] + params[1:2, :]).astype(BF)
    second_out[...] = (normed * params[2:3, :] + params[3:4, :]).astype(BF)


def up_kernel(table, *refs):
    norm, bias, *shards = refs[:-4]
    hidden_out, slope_out, whole, sems = refs[-4:]

    @pl.when(pl.program_id(0) == 0)
    def _():
        load_shards(shards, table, whole, sems, 0)

    lin = jnp.dot(norm[...], whole[...], preferred_element_type=F32) + bias[...]
    cdf = 0.5 + 0.5 * lax.erf(lin * SQRT_HALF)
    hidden_out[...] = (lin * cdf).astype(BF)
    slope_out[...] = cdf + lin * (INV_SQRT_2PI * jnp.exp(-0.5 * lin * lin))


def turn(values, tables, sign):
    cosine, left, right = tables
    half = ROTARY // 2
    turned = left * pltpu.roll(values, HEAD_DIM - half, 1) + right * pltpu.roll(values, half, 1)
    return values * cosine + sign * turned


def project_kernel(table, heads, *refs):
    norm, bias, cosine, left, right, *shards = refs[:-3]
    out, whole, sems = refs[-3:]

    @pl.when(pl.program_id(0) == 0)
    def _():
        load_shards(shards, table, whole, sems, 0, pl.ds(0, whole.shape[1]))

    lin = jnp.dot(norm[...], whole[...], preferred_element_type=F32) + bias[...]
    tables = cosine[...], left[...], right[...]
    for head in range(heads):
        for part in range(3):
            at = slice((head * 3 + part) * HEAD_DIM, (head * 3 + part + 1) * HEAD_DIM)
            piece = lin[:, at]
            out[:, at] = (turn(piece, tables, 1.0) if part < 2 else piece).astype(BF)


def attended_grad_kernel(table, *refs):
    grad, *shards = refs[:-3]
    out, whole, sems = refs[-3:]

    @pl.when(pl.program_id(0) == 0)
    def _():
        columns = pl.ds(shards[0].shape[1] - whole.shape[1], whole.shape[1])
        load_shards(shards, table, whole, sems, 0, columns)

    out[...] = jnp.dot(grad[...], whole[...], preferred_element_type=F32).astype(BF)


def head_columns(head, part):
    return slice((3 * head + part) * HEAD_DIM, (3 * head + part + 1) * HEAD_DIM)


def own_columns(head):
    return slice(head * HEAD_DIM, (head + 1) * HEAD_DIM)


def rows_of(block, extent):
    return pl.ds(pl.multiple_of(block * extent, extent), extent)


def allowed_scores(project, start, block, at, head, masked):
    rows, keys = rows_of(block, QUERY_BLOCK), rows_of(at, KEY_BLOCK)
    scores = lax.dot_general(
        project[keys, head_columns(head, 1)],
        project[rows, head_columns(head, 0)],
        LAST,
        preferred_element_type=F32,
    ) * (HEAD_DIM**-0.5 * LOG2_E)
    if not masked:
        return scores
    place = block * QUERY_BLOCK + lax.broadcasted_iota(jnp.int32, (1, QUERY_BLOCK), 1)
    key_place = at * KEY_BLOCK + lax.broadcasted_iota(jnp.int32, (KEY_BLOCK, QUERY_BLOCK), 0)
    allowed = (key_place >= start[:, rows]) & (key_place <= place)
    return jnp.where(allowed, scores, MASKED)


def over_keys(low, high, block, step, carry):
    between = jnp.minimum(high[block], block)
    carry = lax.fori_loop(low[block], between, functools.partial(step, True), carry)
    carry = lax.fori_loop(between, block, functools.partial(step, False), carry)
    return step(True, block, carry)


def attention_kernel(low, high, start, project, *refs):
    out, produced_t, log_total, v_t = refs[-4:]
    v_t[...] = project[:, head_columns(0, 2)].T

    def query_block(block, _):
        rows = rows_of(block, QUERY_BLOCK)

        def forward(masked, at, carry):
            largest, total, produced = carry
            scores = allowed_scores(project, start, block, at, 0, masked)
            newest = jnp.maximum(largest, jnp.max(scores, axis=0, keepdims=True))
            shrink = jnp.exp2(largest - newest)
            parts = jnp.exp2(scores - newest)
            total = total * shrink + jnp.sum(parts, axis=0, keepdims=True)
            produced = produced * shrink + jnp.dot(
                v_t[:, rows_of(at, KEY_BLOCK)], parts.astype(BF), preferred_element_type=F32
            )
            return newest, total, produced

        empty = jnp.zeros((1, QUERY_BLOCK), F32)
        wide = jnp.zeros((HEAD_DIM, QUERY_BLOCK), F32)
        largest, total, produced = over_keys(
            low, high, block, forward, (empty + MASKED, empty, wide)
        )
        produced = produced * (1.0 / total)
        out[rows, :] = produced.T.astype(BF)
        produced_t[:, rows] = produced
        log_total[:, rows] = largest + jnp.log2(total)
        return 0

    lax.fori_loop(0, project.shape[0] // QUERY_BLOCK, query_block, 0)


def attention_back_kernel(
    heads,
    low,
    high,
    start,
    cosine,
    left,
    right,
    project,
    grad,
    *refs,
):
    produced_t, log_total = refs[:heads], refs[heads : 2 * heads]
    project_grad, k_t, dk, dv = refs[2 * heads :]
    length = project.shape[0]
    scale = HEAD_DIM**-0.5
    for head in range(heads):
        k_t[head] = project[:, head_columns(head, 1)].T
    dk[...] = jnp.zeros_like(dk)
    dv[...] = jnp.zeros_like(dv)

    def query_block(block, _):
        rows = rows_of(block, QUERY_BLOCK)
        deltas = [
            jnp.sum(
                produced_t[head][:, rows] * grad[rows, own_columns(head)].astype(F32).T,
                axis=0,
                keepdims=True,
            )
            for head in range(heads)
        ]

        def backward(masked, at, query_grads):
            keys, made = rows_of(at, KEY_BLOCK), []
            for head in range(heads):
                scores = allowed_scores(project, start, block, at, head, masked)
                prob_grad = lax.dot_general(
                    project[keys, head_columns(head, 2)],
                    grad[rows, own_columns(head)],
                    LAST,
                    preferred_element_type=F32,
                )
                probs = jnp.exp2(scores - log_total[head][:, rows])
                score_grad = (probs * (prob_grad - deltas[head])).astype(BF)
                dv[head, keys, :] += jnp.dot(
                    probs.astype(BF), grad[rows, own_columns(head)], preferred_element_type=F32
                )
                dk[head, keys, :] += jnp.dot(
                    score_grad, project[rows, head_columns(head, 0)], preferred_element_type=F32
                )
                made.append(
                    query_grads[head]
                    + jnp.dot(k_t[head, :, keys], score_grad, preferred_element_type=F32)
                )
            return tuple(made)

        wide = jnp.zeros((HEAD_DIM, QUERY_BLOCK), F32)
        query_grads = over_keys(low, high, block, backward, (wide,) * heads)
        tables = cosine[rows, :], left[rows, :], right[rows, :]
        for head in range(heads):
            project_grad[rows, head_columns(head, 0)] = turn(
                (query_grads[head] * scale).T, tables, -1.0
            ).astype(BF)
        return 0

    lax.fori_loop(0, length // QUERY_BLOCK, query_block, 0)
    tables = cosine[...], left[...], right[...]
    for head in range(heads):
        project_grad[:, head_columns(head, 1)] = turn(dk[head] * scale, tables, -1.0).astype(BF)
        project_grad[:, head_columns(head, 2)] = dv[head].astype(BF)


def mixed_kernel(pack_count, pack_table, down_table, *refs):
    attended, hidden, *shards = refs[:-5]
    pack_shards, down_shards = shards[:pack_count], shards[pack_count:]
    out, output_whole, down_whole, output_sems, down_sems = refs[-5:]

    @pl.when(pl.program_id(0) == 0)
    def _():
        width = pack_shards[0].shape[1]
        columns = pl.ds(width - output_whole.shape[1], output_whole.shape[1])
        load_shards(pack_shards, pack_table, output_whole, output_sems, 0, columns)
        load_shards(down_shards, down_table, down_whole, down_sems, 0)

    out[...] = (
        lax.dot_general(attended[...], output_whole[...], LAST, preferred_element_type=F32)
        + lax.dot_general(hidden[...], down_whole[...], LAST, preferred_element_type=F32)
    ).astype(BF)


def hidden_grad_kernel(table, *refs):
    grad, slope, *shards = refs[:-3]
    out, whole, sems = refs[-3:]

    @pl.when(pl.program_id(0) == 0)
    def _():
        load_shards(shards, table, whole, sems, 0)

    hidden_grad = jnp.dot(grad[...], whole[...], preferred_element_type=F32)
    out[...] = (hidden_grad * slope[...]).astype(BF)


def weight_grad_kernel(count, pairs, *refs):
    lefts_rights, outs = refs[: 2 * pairs], refs[2 * pairs :]
    for step in range(count):

        @pl.when(pl.program_id(0) == step)
        def _():
            begin = 0
            for pair in range(pairs):
                left, right = lefts_rights[2 * pair], lefts_rights[2 * pair + 1]
                made = lax.dot_general(left[...], right[...], FIRST, preferred_element_type=F32)
                width = made.shape[1]
                outs[step][:, begin : begin + width] = made.astype(outs[step].dtype)
                begin += width


def back_kernel(pack_count, pack_table, up_table, *refs):
    act, params, project, expand, *shards = refs[:-8]
    project_shards, up_shards = shards[:pack_count], shards[pack_count:]
    out, gains, project_bias, up_bias, project_whole, up_whole, project_sems, up_sems = refs[-8:]

    @pl.when(pl.program_id(0) == 0)
    def _():
        columns = pl.ds(0, project_whole.shape[1])
        load_shards(project_shards, pack_table, project_whole, project_sems, 0, columns)
        load_shards(up_shards, up_table, up_whole, up_sems, 0)
        gains[...] = jnp.zeros_like(gains)
        project_bias[...] = jnp.zeros_like(project_bias)
        up_bias[...] = jnp.zeros_like(up_bias)

    normed, inverse_scale = normalize(act[...])
    first = lax.dot_general(project[...], project_whole[...], LAST, preferred_element_type=F32)
    second = lax.dot_general(expand[...], up_whole[...], LAST, preferred_element_type=F32)
    gains[0:1, :] += jnp.sum(first * normed, axis=0, keepdims=True)
    gains[1:2, :] += jnp.sum(first, axis=0, keepdims=True)
    gains[2:3, :] += jnp.sum(second * normed, axis=0, keepdims=True)
    gains[3:4, :] += jnp.sum(second, axis=0, keepdims=True)
    project_bias[...] += jnp.sum(project[...].astype(F32), axis=0, keepdims=True)
    up_bias[...] += jnp.sum(expand[...].astype(F32), axis=0, keepdims=True)
    normed_grad = first * params[0:1, :] + second * params[2:3, :]
    mean_grad = jnp.mean(normed_grad, axis=1, keepdims=True)
    mean_product = jnp.mean(normed_grad * normed, axis=1, keepdims=True)
    out[...] = (inverse_scale * (normed_grad - mean_grad - normed * mean_product)).astype(BF)


def tile_spec(width, tile=TILE):
    return pl.BlockSpec((tile, width), lambda i: (i, 0))


def fixed_spec(shape):
    return pl.BlockSpec(shape, lambda i: (0, 0))


ANY = pl.BlockSpec(memory_space=pl.ANY)


def shape_of(shape, kind):
    return jax.ShapeDtypeStruct(shape, kind)


def cost(flops, moved=0):
    return pl.CostEstimate(flops=int(flops), bytes_accessed=int(moved), transcendentals=0)


def call(kernel, name, tokens, ins, outs, wholes, args, moved=0, tile=TILE):
    scratch = [pltpu.VMEM(shape, BF) for shape, _ in wholes] + [
        pltpu.SemaphoreType.DMA((count,)) for _, count in wholes
    ]
    return pl.pallas_call(
        kernel,
        name=name,
        grid=(tokens // tile,),
        in_specs=ins,
        out_specs=[spec for spec, _ in outs],
        out_shape=[shape for _, shape in outs],
        scratch_shapes=scratch,
        compiler_params=pltpu.CompilerParams(
            dimension_semantics=("arbitrary",), vmem_limit_bytes=VMEM_LIMIT
        ),
        cost_estimate=cost(sum(2 * tokens * shape[0] * shape[1] for shape, _ in wholes), moved),
    )(*args)


def weight_grad(count, place, pairs, chunked_right=False):
    specs, arrays, width = [], [], 0
    for left, right in pairs:
        chunked, fixed = (right, left) if chunked_right else (left, right)
        extent = chunked.shape[1] // count
        chunk_spec = pl.BlockSpec(
            (chunked.shape[0], extent), lambda i, spot: (0, lax.rem(spot[0] + i, count))
        )
        fixed_spec_ = pl.BlockSpec(fixed.shape, lambda i, spot: (0, 0))
        specs += [fixed_spec_, chunk_spec] if chunked_right else [chunk_spec, fixed_spec_]
        arrays += [left, right]
        rows, columns = (fixed.shape[1], extent) if chunked_right else (extent, fixed.shape[1])
        width += columns
    shape = (rows, width)
    return pl.pallas_call(
        functools.partial(drop_first, functools.partial(weight_grad_kernel, count, len(pairs))),
        name="weight_grad",
        grid_spec=pltpu.PrefetchScalarGridSpec(
            num_scalar_prefetch=1,
            grid=(count,),
            in_specs=specs,
            out_specs=[pl.BlockSpec(shape, lambda i, spot: (0, 0))] * count,
        ),
        out_shape=[shape_of(shape, F32 if r == 0 else BF) for r in range(count)],
        compiler_params=pltpu.CompilerParams(
            dimension_semantics=("arbitrary",), vmem_limit_bytes=VMEM_LIMIT
        ),
        cost_estimate=cost(2 * arrays[0].shape[0] * rows * width * count),
    )(place[None], *arrays)


def drop_first(kernel, spot, *refs):
    kernel(*refs)


def angle_tables(row_total):
    positions = (jnp.arange(row_total, dtype=jnp.int32) % LENGTH).astype(F32)
    frequency = ROPE_BASE ** (-jnp.arange(0, ROTARY, 2, dtype=jnp.int32).astype(F32) / ROTARY)
    turning = positions[:, None] * frequency[None, :]
    cosine, sine = jnp.cos(turning), jnp.sin(turning)
    rest = HEAD_DIM - ROTARY
    zeros = jnp.zeros_like(sine)
    return (
        jnp.concatenate([cosine, cosine, jnp.ones((row_total, rest), F32)], axis=1),
        jnp.concatenate([-sine, zeros, jnp.zeros((row_total, rest), F32)], axis=1),
        jnp.concatenate([zeros, sine, jnp.zeros((row_total, rest), F32)], axis=1),
    )


def on_device(
    rows,
    cols,
    activations,
    document_ids,
    attention_gain,
    attention_shift,
    feedforward_gain,
    feedforward_shift,
    query_key_value,
    query_key_value_bias,
    output_weight,
    output_bias,
    up_weight,
    up_bias,
    down_weight,
    down_bias,
    out_grad,
):
    row_place, col_place = lax.axis_index("row"), lax.axis_index("col")
    tokens, features = activations.shape
    heads = query_key_value.shape[1]
    project_width, out_width = heads * 3 * HEAD_DIM, heads * HEAD_DIM
    hidden_width = up_weight.shape[1]

    full_input = lax.all_gather(activations, "row", axis=1, tiled=True)
    full_grad = lax.all_gather(out_grad, "row", axis=1, tiled=True)

    pack = jnp.concatenate(
        [query_key_value.astype(BF).reshape(-1, project_width), output_weight.astype(BF).T], axis=1
    )
    pack_gather = RingGather(pack, cols)
    down_shard = down_weight.astype(BF).T
    up_shard = up_weight.astype(BF)
    up_gather = RingGather(up_shard, cols)
    both = LineBoth(down_shard, col_place) if cols == 4 else None
    down_gather = both or RingGather(down_shard, cols)

    def slot(transfers, gate, *works):
        moved = []
        for transfer in transfers:
            moved += transfer.step(gate)
        made = [work(gate) for work in works]
        return moved + [array for arrays in made for array in arrays], made

    def more(transfers, gate):
        for _ in range(cols - 4):
            gate, _ = slot(transfers, gate)
        return gate

    def tables_work(gate):
        cosine, left, right = angle_tables(tokens)
        starts = jnp.sum(
            (document_ids[:, None] < document_ids[None, :]).astype(jnp.int32), axis=0
        )
        sums = jnp.sum(out_grad.astype(F32), axis=0)
        return cosine, left, right, starts, sums, down_shard, up_shard

    def params_work(gate):
        stacked = jnp.stack(
            [attention_gain, attention_shift, feedforward_gain, feedforward_shift]
        )
        return [lax.all_gather(after(stacked, gate), "row", axis=1, tiled=True)]

    def norm_work(gate):
        return call(
            norm_kernel,
            "norm",
            tokens,
            [tile_spec(D), fixed_spec((4, D))],
            [
                (tile_spec(D), shape_of((tokens, D), BF)),
                (tile_spec(D), shape_of((tokens, D), BF)),
            ],
            [],
            [full_input, after(norm_params, gate)],
            6 * tokens * D,
        )

    gate, ((cosine, left, right, starts, shift_out_grad, *_),) = slot([pack_gather], [], tables_work)
    low_blocks = starts[::QUERY_BLOCK] // KEY_BLOCK
    high_blocks = (starts[QUERY_BLOCK - 1 :: QUERY_BLOCK] + KEY_BLOCK - 1) // KEY_BLOCK
    gate, ((norm_params,),) = slot([pack_gather], gate, params_work)
    gate = more([pack_gather], gate)
    gate, ((first_norm, second_norm),) = slot([pack_gather], gate, norm_work)
    pack_shards, pack_table = pack_gather.shards()

    def project_work(gate):
        return call(
            functools.partial(project_kernel, pack_table, heads),
            "project",
            tokens,
            [tile_spec(D), fixed_spec((1, project_width))]
            + [tile_spec(HEAD_DIM)] * 3
            + [ANY] * len(pack_shards),
            [(tile_spec(project_width), shape_of((tokens, project_width), BF))],
            [((D, project_width), cols)],
            [
                after(first_norm, gate),
                query_key_value_bias.reshape(1, -1),
                cosine,
                left,
                right,
                *pack_shards,
            ],
        )

    def attended_grad_work(gate):
        return call(
            functools.partial(attended_grad_kernel, pack_table),
            "attended_grad",
            tokens,
            [tile_spec(D, 4 * TILE)] + [ANY] * len(pack_shards),
            [(tile_spec(out_width, 4 * TILE), shape_of((tokens, out_width), BF))],
            [((D, out_width), cols)],
            [after(full_grad, gate), *pack_shards],
            tile=4 * TILE,
        )

    def whole_spec(*shape):
        return pl.BlockSpec(shape, lambda i: (0, 0))

    def attention_work(projected, head, before):
        def column_spec(width):
            return pl.BlockSpec((tokens, width), lambda i: (0, head))

        return pl.pallas_call(
            attention_kernel,
            name="attention",
            grid=(1,),
            in_specs=[pl.BlockSpec(memory_space=pltpu.SMEM)] * 2
            + [whole_spec(1, tokens), column_spec(3 * HEAD_DIM)]
            + [ANY] * len(before),
            out_specs=[column_spec(HEAD_DIM), whole_spec(HEAD_DIM, tokens), whole_spec(1, tokens)],
            out_shape=[
                shape_of((tokens, out_width), BF),
                shape_of((HEAD_DIM, tokens), F32),
                shape_of((1, tokens), F32),
            ],
            input_output_aliases={4: 0} if before else {},
            scratch_shapes=[pltpu.VMEM((HEAD_DIM, tokens), BF)],
            compiler_params=pltpu.CompilerParams(vmem_limit_bytes=VMEM_LIMIT),
            cost_estimate=cost(8 * tokens * tokens * HEAD_DIM),
        )(low_blocks, high_blocks, starts[None], projected, *before)

    def attention_back_work(gate):
        return pl.pallas_call(
            functools.partial(attention_back_kernel, heads),
            name="attention_back",
            grid=(1,),
            in_specs=[pl.BlockSpec(memory_space=pltpu.SMEM)] * 2
            + [whole_spec(1, tokens)]
            + [whole_spec(tokens, HEAD_DIM)] * 3
            + [whole_spec(tokens, project_width), whole_spec(tokens, out_width)]
            + [whole_spec(HEAD_DIM, tokens)] * heads
            + [whole_spec(1, tokens)] * heads,
            out_specs=[whole_spec(tokens, project_width)],
            out_shape=[shape_of((tokens, project_width), BF)],
            scratch_shapes=[pltpu.VMEM((heads, HEAD_DIM, tokens), BF)]
            + [pltpu.VMEM((heads, tokens, HEAD_DIM), F32)] * 2,
            compiler_params=pltpu.CompilerParams(vmem_limit_bytes=VMEM_LIMIT),
            cost_estimate=cost(16 * tokens * tokens * out_width),
        )(
            low_blocks,
            high_blocks,
            starts[None],
            cosine,
            left,
            right,
            projected,
            after(attended_grad, gate),
            *[made[1] for made in by_head],
            *[made[2] for made in by_head],
        )

    by_head = []

    def first_head_work(gate):
        (projected,) = project_work(gate)
        by_head.append(attention_work(projected, 0, []))
        return projected, by_head[0][2]

    gate, ((projected, _),) = slot([up_gather], gate, first_head_work)

    def other_heads_work(gate):
        values = after(projected, gate)
        for head in range(1, heads):
            by_head.append(attention_work(values, head, [by_head[-1][0]]))
        return attended_grad_work(gate + [by_head[-1][2]])

    gate, ((attended_grad,),) = slot([up_gather], gate, other_heads_work)
    attended = by_head[-1][0]
    gate = more([up_gather], gate)
    gate, ((project_grad,),) = slot([up_gather], gate, attention_back_work)
    up_shards, up_table = up_gather.shards()

    def pack_weight_work(gate):
        return weight_grad(
            cols, col_place, [(first_norm, after(project_grad, gate)), (full_grad, attended)]
        )

    def up_work(gate):
        return call(
            functools.partial(up_kernel, up_table),
            "up",
            tokens,
            [tile_spec(D, 2 * TILE), fixed_spec((1, hidden_width))] + [ANY] * len(up_shards),
            [
                (tile_spec(hidden_width, 2 * TILE), shape_of((tokens, hidden_width), BF)),
                (tile_spec(hidden_width, 2 * TILE), shape_of((tokens, hidden_width), F32)),
            ],
            [((D, hidden_width), cols)],
            [after(second_norm, gate), up_bias[None], *up_shards],
            tile=2 * TILE,
        )

    def down_weight_work(gate):
        return weight_grad(cols, col_place, [(after(hidden, gate), full_grad)], True)

    gate, (pack_chunks,) = slot([down_gather], gate, pack_weight_work)
    gate = more([down_gather], gate)
    if both is not None:
        both.chunks = pack_chunks
    gate, ((hidden, slope),) = slot([down_gather], gate, up_work)
    gate, (down_chunks,) = slot([down_gather], gate, down_weight_work)
    down_shards, down_table = down_gather.shards()
    pack_scatter = both or RingScatter(pack_chunks, cols)
    down_scatter = RingScatter(down_chunks, cols)
    if both is None:
        for _ in range(cols - 2):
            gate, _ = slot([pack_scatter], gate)

    def mixed_work(gate):
        return call(
            functools.partial(mixed_kernel, len(pack_shards), pack_table, down_table),
            "mixed",
            tokens,
            [tile_spec(out_width, 2 * TILE), tile_spec(hidden_width, 2 * TILE)] + [ANY] * (len(pack_shards) + len(down_shards)),
            [(tile_spec(D, 2 * TILE), shape_of((tokens, D), BF))],
            [((D, out_width), cols), ((D, hidden_width), cols)],
            [after(attended, gate), hidden, *pack_shards, *down_shards],
            tile=2 * TILE,
        )

    def hidden_grad_work(gate):
        return call(
            functools.partial(hidden_grad_kernel, down_table),
            "hidden_grad",
            tokens,
            [tile_spec(D, 2 * TILE), tile_spec(hidden_width, 2 * TILE)] + [ANY] * len(down_shards),
            [(tile_spec(hidden_width, 2 * TILE), shape_of((tokens, hidden_width), BF))],
            [((D, hidden_width), cols)],
            [after(full_grad, gate), slope, *down_shards],
            tile=2 * TILE,
        )

    def back_work(gate):
        return call(
            functools.partial(back_kernel, len(pack_shards), pack_table, up_table),
            "back",
            tokens,
            [tile_spec(D), fixed_spec((4, D)), tile_spec(project_width), tile_spec(hidden_width)]
            + [ANY] * (len(pack_shards) + len(up_shards)),
            [
                (tile_spec(D), shape_of((tokens, D), BF)),
                (fixed_spec((4, D)), shape_of((4, D), F32)),
                (fixed_spec((1, project_width)), shape_of((1, project_width), F32)),
                (fixed_spec((1, hidden_width)), shape_of((1, hidden_width), F32)),
            ],
            [((D, project_width), cols), ((D, hidden_width), cols)],
            [
                full_input,
                norm_params,
                project_grad,
                after(expand_grad, gate),
                *pack_shards,
                *up_shards,
            ],
        )

    def up_weight_work(gate):
        return weight_grad(cols, col_place, [(second_norm, after(expand_grad, gate))])

    def down_result_work(gate):
        return [down_scatter.result(gate)]

    def layer_out_work(gate):
        return [
            activations.astype(F32) + after(mixed_sum, gate).astype(F32) + output_bias + down_bias
        ]

    gate, ((mixed_part,),) = slot([pack_scatter], gate, mixed_work)
    mixed_sum = lax.psum_scatter(after(mixed_part, gate), "row", scatter_dimension=1, tiled=True)
    gate, ((expand_grad,),) = slot([down_scatter], gate, hidden_grad_work)
    gate = more([down_scatter], gate)
    gate, ((back_part, gains, project_bias_grad, up_bias_grad),) = slot(
        [down_scatter], gate, back_work
    )
    back_sum = lax.psum_scatter(after(back_part, gate), "row", scatter_dimension=1, tiled=True)
    gate, (up_chunks,) = slot([down_scatter], gate, up_weight_work)
    up_scatter = RingScatter(up_chunks, cols)

    def split_work(gate):
        parts = pack_scatter.result(gate)
        shape = query_key_value.shape
        return parts[:, :project_width].reshape(shape), parts[:, project_width:].T

    def gains_work(gate):
        terms = after(gains, gate)
        terms = terms.reshape(4, rows, features).transpose(1, 0, 2).reshape(rows, -1)
        return [pair_scatter(terms, "row", rows, row_place)]

    up_scatter.step(gate)
    (gain_terms,) = gains_work(gate + [up_scatter.sent])
    (down_weight_grad,) = down_result_work(gate)
    project_weight_grad, output_weight_grad = split_work(gate)
    up_scatter.step([down_weight_grad, project_weight_grad, output_weight_grad, gain_terms])
    small = [gain_terms, project_bias_grad[0], up_bias_grad[0], shift_out_grad]
    masks = [1 << bit for bit in range(cols.bit_length() - 1)]
    small = pair_sum(jnp.concatenate(small), "col", cols, masks[:-1], [up_scatter.sent])
    for _ in range(cols - 3):
        up_scatter.step([small])
    (layer_out,) = layer_out_work([up_scatter.sent])
    arrived = pair_exchange(small, "col", cols, masks[-1], [up_scatter.sent])
    activations_grad = after(out_grad, [layer_out]).astype(F32) + back_sum.astype(F32)
    up_weight_grad = up_scatter.result([activations_grad])
    small = after(small, [activations_grad]) + arrived
    sizes = [features] * 4 + [project_width, hidden_width, features]
    pieces, begin = [], 0
    for size in sizes:
        pieces.append(small[begin : begin + size])
        begin += size
    return (
        layer_out,
        activations_grad,
        pieces[0],
        pieces[1],
        pieces[2],
        pieces[3],
        project_weight_grad,
        pieces[4].reshape(query_key_value_bias.shape),
        output_weight_grad,
        pieces[6],
        up_weight_grad,
        pieces[5],
        down_weight_grad,
        pieces[6],
    )


def solution(mesh):
    placed = (
        P("col", "row"),
        P("col"),
        P("row"),
        P("row"),
        P("row"),
        P("row"),
        P("col", "row", None),
        P("row", None),
        P("row", "col"),
        P("row"),
        P("col", "row"),
        P("row"),
        P("row", "col"),
        P("row"),
        P("col", "row"),
    )

    def body(*args):
        return on_device(mesh.shape["row"], mesh.shape["col"], *args)

    return jax.shard_map(
        body,
        mesh=mesh,
        in_specs=placed,
        out_specs=(
            P("col", "row"),
            P("col", "row"),
            P("row"),
            P("row"),
            P("row"),
            P("row"),
            P("col", "row", None),
            P("row", None),
            P("row", "col"),
            P("row"),
            P("col", "row"),
            P("row"),
            P("row", "col"),
            P("row"),
        ),
        check_vma=False,
    )
```
